32 devices in a mesh: rows: 2 (over core), imgs: 16 (over z, y, x).
Axes of the slice: x: 2, y: 2, z: 4, core: 2. Of those that a mesh axis runs over, the one named last changes fastest.
Arguments:
- inputs: bfloat16 [256, 22, 18, 320], P('imgs', 'rows')
- cotangent: bfloat16 [256, 22, 18, 320], P('imgs', 'rows')
- scales: float32 [4, 320], replicated, may hold values from 0.25 to 1.75
- shifts: float32 [8, 320], replicated, may hold values from -3 to 3
- hidden_shift: float32 [2, 1280], replicated, may hold values from -3 to 3
- w_inward: bfloat16 [320, 320], replicated, may hold values from -0.3125 to 0.3125
- w_gating: bfloat16 [320, 320], replicated, may hold values from -0.3125 to 0.3125
- w_outward: bfloat16 [320, 320], replicated, may hold values from -0.3125 to 0.3125
- w_expand: bfloat16 [320, 1280], replicated, may hold values from -0.3125 to 0.3125
- w_reduce: bfloat16 [1280, 320], replicated, may hold values from -0.15625 to 0.15625
- kernel_local: float32 [25, 320], replicated, may hold values from -1.25 to 1.25
- kernel_dilated: float32 [49, 320], replicated, may hold values from -0.875 to 0.875
- kernel_hidden: float32 [9, 1280], replicated, may hold values from -2 to 2
- image_size: int32 [256], replicated, may hold values from 14 to 18, as said below
- band_split: int32 [256], replicated, may hold values from 5 to 11, as said below
- slot_image: int32 [256], P('imgs'), may hold values from 0 to 255, each once
Outputs:
- result: float32 [256, 22, 18, 320], P('imgs', 'rows')
- input_grad: float32 [256, 22, 18, 320], P('imgs', 'rows')
- scales_grad: float32 [4, 320], replicated
- shifts_grad: float32 [8, 320], replicated
- hidden_shift_grad: float32 [2, 1280], replicated
- w_inward_grad: float32 [320, 320], replicated
- w_gating_grad: float32 [320, 320], replicated
- w_outward_grad: float32 [320, 320], replicated
- w_expand_grad: float32 [320, 1280], replicated
- w_reduce_grad: float32 [1280, 320], replicated
- kernel_local_grad: float32 [25, 320], replicated
- kernel_dilated_grad: float32 [49, 320], replicated
- kernel_hidden_grad: float32 [9, 1280], replicated
The draws below stay inside these ranges and needn't reach their ends.
Inputs may be any that keep to these rules, and one draw needn't show every extreme that they name: `image_size`: side of each square image in pixels: 14, 16 or 18. `band_split`: an image of side n has from n / 2 - 2 to n / 2 + 2 of its rows in the first band. `slot_image`: each image stands in exactly one slot.
All inputs are finite; a program needn't handle non-finite values.
Results may differ from the reference program's by a relative error of at most 0.003.
Values may be sent and summed in bfloat16 or wider, within the bound.
A program may use at most 320 MiB of HBM per device.

```python
import jax
import jax.numpy as jnp
from jax import lax

C = 320
F = 1280
IMG_DEV = 16
BAND = 11
WMAX = 18
IMAGES = 256
HEIGHT = 22
N_ROWS = 2


def image_plan(key):
    first_key, second_key = jax.random.split(key)
    extent = 14 + 2 * jax.random.randint(first_key, (IMAGES,), 0, 3)
    split_rows = extent // 2 + jax.random.randint(second_key, (IMAGES,), -2, 3)
    extent = extent.at[0].set(18).at[1].set(14)
    split_rows = split_rows.at[0].set(11).at[1].set(5)
    return (extent.astype(jnp.int32), split_rows.astype(jnp.int32))


def ramp_scale():
    image_frac = jnp.arange(IMAGES, dtype=jnp.float32) / (IMAGES - 1)
    row_frac = jnp.arange(HEIGHT, dtype=jnp.float32) / (HEIGHT - 1)
    return 1.0 + (image_frac[:, None, None, None] + row_frac[None, :, None, None])


def draw_image_size(key, part):
    extent, split_rows = image_plan(key)
    return extent


def draw_band_split(key, part):
    extent, split_rows = image_plan(key)
    return split_rows


def draw_inputs(key, part):
    key = jax.random.fold_in(key, 3)
    noise_key, shift_key = jax.random.split(key)
    noise = jnp.clip(jax.random.normal(noise_key, (IMAGES, HEIGHT, WMAX, C), jnp.float32), -6.0, 6.0)
    offset = 0.5 * jax.random.normal(shift_key, (C,), jnp.float32)
    return (ramp_scale() * (noise + offset)).astype(jnp.bfloat16)


def draw_cotangent(key, part):
    key = jax.random.fold_in(key, 5)
    noise_key, shift_key = jax.random.split(key)
    noise = jnp.clip(jax.random.normal(noise_key, (IMAGES, HEIGHT, WMAX, C), jnp.float32), -6.0, 6.0)
    offset = 0.3 * jax.random.normal(shift_key, (C,), jnp.float32)
    return (ramp_scale() * (noise + offset)).astype(jnp.bfloat16)


def bell_draw(rng, dims, scale, most, kind=jnp.bfloat16):
    array = scale * jax.random.normal(rng, dims, jnp.float32)
    return jnp.clip(array, min=-most, max=most).astype(kind)


def setup_inputs(seed: int = 0) -> dict:
    keys = jax.random.split(jax.random.key(seed), 17)
    return {
        "inputs": draw_inputs(jax.random.fold_in(keys[16], 71), 0),
        "cotangent": draw_cotangent(jax.random.fold_in(keys[16], 71), 0),
        "scales": jnp.clip(1.0 + 0.15 * jax.random.normal(keys[2], (4, C), jnp.float32), 0.25, 1.75),
        "shifts": bell_draw(keys[3], (8, C), 0.5, 3.0, jnp.float32),
        "hidden_shift": bell_draw(keys[4], (2, F), 0.5, 3.0, jnp.float32),
        "w_inward": bell_draw(keys[5], (C, C), C ** -0.5, 0.3125),
        "w_gating": bell_draw(keys[6], (C, C), C ** -0.5, 0.3125),
        "w_outward": bell_draw(keys[7], (C, C), C ** -0.5, 0.3125),
        "w_expand": bell_draw(keys[8], (C, F), C ** -0.5, 0.3125),
        "w_reduce": bell_draw(keys[9], (F, C), F ** -0.5, 0.15625),
        "kernel_local": bell_draw(keys[10], (25, C), 25 ** -0.5, 1.25, jnp.float32),
        "kernel_dilated": bell_draw(keys[11], (49, C), 49 ** -0.5, 0.875, jnp.float32),
        "kernel_hidden": bell_draw(keys[12], (9, F), 9 ** -0.5, 2.0, jnp.float32),
        "image_size": draw_image_size(jax.random.fold_in(keys[16], 71), 0),
        "band_split": draw_band_split(jax.random.fold_in(keys[16], 71), 0),
        "slot_image": jax.random.permutation(keys[15], IMAGES).astype(jnp.int32),
    }


@jax.custom_vjp
def low(v):
    return lax.optimization_barrier(v.astype(jnp.bfloat16)).astype(jnp.float32)

@jax.custom_vjp
def low_back(v):
    return v

def low_keep(v):
    return (low(v), None)

def low_pass(kept, grad):
    return (grad,)

def back_keep(v):
    return (v, None)

def back_low(kept, grad):
    return (low(grad),)
low.defvjp(low_keep, low_pass)
low_back.defvjp(back_keep, back_low)
epsilon = 1e-05

def smooth(values):
    return jax.nn.gelu(values, approximate=False)

def project(values, weight):
    return jnp.einsum('irwk,kn->irwn', values, weight, precision=lax.Precision.HIGHEST)

def depthwise(field, kernel, extent, dilation):
    margin = extent // 2 * dilation
    height = field.shape[1]
    columns = field.shape[2]
    padded = jnp.pad(field, ((0, 0), (margin, margin), (margin, margin), (0, 0)))
    summed = jnp.zeros(field.shape, jnp.float32)
    for row_tap in range(extent):
        for col_tap in range(extent):
            window = padded[:, row_tap * dilation:row_tap * dilation + height, col_tap * dilation:col_tap * dilation + columns, :]
            summed = summed + kernel[row_tap * extent + col_tap] * window
    return summed

def image_mask(image_size, band_split, slot_image):
    extent = image_size[slot_image]
    top_row = BAND - band_split[slot_image]
    row_index = jnp.arange(BAND * N_ROWS, dtype=jnp.int32)
    col_index = jnp.arange(WMAX, dtype=jnp.int32)
    row_inside = (row_index[None, :] >= top_row[:, None]) & (row_index[None, :] < (top_row + extent)[:, None])
    col_inside = col_index[None, :] < extent[:, None]
    return (row_inside[:, :, None] & col_inside[:, None, :]).astype(jnp.float32)[:, :, :, None]

def statistics(masked, counted, gain):
    mean_value = lax.optimization_barrier(jnp.sum(masked, axis=(0, 1, 2))) / counted
    variance = lax.optimization_barrier(jnp.sum(masked * masked, axis=(0, 1, 2))) / counted - mean_value * mean_value
    return (mean_value, lax.rsqrt(variance + epsilon) * gain)

def mixer_block(masked_in, inside, mean_one, scale_one, scales, shifts, w_inward, w_gating, w_outward, kernel_local, kernel_dilated):
    normed_one = low((masked_in - mean_one) * scale_one + shifts[0])
    pre_gelu = low_back(project(normed_one, w_inward) + shifts[1])
    gelu_out = low(smooth(pre_gelu))
    conv_one = low(low_back(depthwise(inside * gelu_out, kernel_local, 5, 1) + shifts[2]))
    conv_two = low(low_back(depthwise(inside * conv_one, kernel_dilated, 7, 3) + shifts[3]))
    gate_pre = low_back(project(conv_two, w_gating) + shifts[4])
    gated = low(gelu_out * gate_pre)
    branch = low_back(project(gated, w_outward) + shifts[5])
    return masked_in + scales[1] * (branch + normed_one)

def hidden_block(middle, inside, mean_two, scale_two, scales, shifts, hidden_shift, w_expand, w_reduce, kernel_hidden):
    normed_two = low((middle - mean_two) * scale_two + shifts[6])
    expanded = low(low_back(project(normed_two, w_expand) + hidden_shift[0]))
    hidden_conv = low_back(depthwise(inside * expanded, kernel_hidden, 3, 1) + hidden_shift[1])
    hidden_act = low(smooth(hidden_conv))
    reduced = low_back(project(hidden_act, w_reduce) + shifts[7])
    return inside * (middle + scales[3] * reduced)

def reference(inputs, cotangent, scales, shifts, hidden_shift, w_inward, w_gating, w_outward, w_expand, w_reduce, kernel_local, kernel_dilated, kernel_hidden, image_size, band_split, slot_image):
    inside = image_mask(image_size, band_split, slot_image)
    counted = jnp.sum(image_size * image_size).astype(jnp.float32)
    blocks = inside.shape[0] // IMG_DEV

    def grouped(values):
        return values.reshape((blocks, IMG_DEV) + values.shape[1:])

    def forward(pixels, scales, shifts, hidden_shift, w_inward, w_gating, w_outward, w_expand, w_reduce, kernel_local, kernel_dilated, kernel_hidden):
        masked_in = inside * pixels
        mean_one, scale_one = statistics(masked_in, counted, scales[0])
        mixer_step = jax.checkpoint(mixer_block)
        middle = lax.map(lambda block_pair: mixer_step(block_pair[0], block_pair[1], mean_one, scale_one, scales, shifts, w_inward, w_gating, w_outward, kernel_local, kernel_dilated), (grouped(masked_in), grouped(inside)))
        middle = middle.reshape(pixels.shape)
        mean_two, scale_two = statistics(inside * middle, counted, scales[2])
        hidden_step = jax.checkpoint(hidden_block)
        result = lax.map(lambda block_pair: hidden_step(block_pair[0], block_pair[1], mean_two, scale_two, scales, shifts, hidden_shift, w_expand, w_reduce, kernel_hidden), (grouped(middle), grouped(inside)))
        return result.reshape(pixels.shape)
    result, pullback = jax.vjp(forward, inputs.astype(jnp.float32), scales, shifts, hidden_shift, w_inward.astype(jnp.float32), w_gating.astype(jnp.float32), w_outward.astype(jnp.float32), w_expand.astype(jnp.float32), w_reduce.astype(jnp.float32), kernel_local, kernel_dilated, kernel_hidden)
    grads = pullback(cotangent.astype(jnp.float32))
    return (result, grads[0], grads[1], grads[2], grads[3], grads[4], grads[5], grads[6], grads[7], grads[8], grads[9], grads[10], grads[11])
```

```python
import functools

import jax
import jax.numpy as jnp
from jax import lax
from jax.experimental import pallas as pl
from jax.experimental.pallas import tpu as pltpu
from jax.sharding import PartitionSpec as P

MESH = pl.DeviceIdType.MESH
epsilon = 1e-05
bf16 = jnp.bfloat16
f32 = jnp.float32
SUB = 8
LANE = 128
MIB = 1 << 20
ANY = pl.BlockSpec(memory_space=pl.ANY)
VMEM = pl.BlockSpec(memory_space=pltpu.VMEM)


def low(values):
    return values.astype(bf16).astype(f32)


def normal_parts(v):
    bell = jnp.exp(-0.5 * (v * v))
    base = 1.0 + (0.3275911 * 0.7071067811865476) * jnp.abs(v)
    t = pl.reciprocal(base, approx=True)
    t = t * (2.0 - base * t)
    poly = 0.5 * 1.061405429
    for coef in (-1.453152027, 1.421413741, -0.284496736, 0.254829592):
        poly = poly * t + 0.5 * coef
    tail = poly * t * bell
    return jnp.where(v >= 0, 1.0 - tail, tail), bell * 0.3989422804014327


def dot(a, b):
    return jnp.dot(a, b, preferred_element_type=f32)


def dot_nt(a, b):
    return lax.dot_general(a, b, (((1,), (1,)), ((), ())), preferred_element_type=f32)


def dot_tn(a, b):
    return lax.dot_general(a, b, (((0,), (0,)), ((), ())), preferred_element_type=f32)


def groups_of(channels):
    return [(g, min(LANE, channels - g * LANE)) for g in range(pl.cdiv(channels, LANE))]


def spread_taps(k_ref, kb, flip=False):
    count, channels = k_ref.shape
    for tap in range(count):
        from_tap = count - 1 - tap if flip else tap
        row = jnp.broadcast_to(k_ref[from_tap : from_tap + 1, :], (SUB, channels))
        for g, width in groups_of(channels):
            kb[tap, g, :, :width] = row[:, g * LANE : g * LANE + width]


def add_row(acc, load, taps, dilation):
    columns, half = len(acc), len(taps) // 2
    for c in range(columns):
        value = load(c)
        for j, tap in enumerate(taps):
            at = c - (j - half) * dilation
            if 0 <= at < columns:
                acc[at] = acc[at] + tap * value
    return acc


def tap_sums(acc, load_fixed, load_moved, dilation):
    columns, half = load_fixed[1], len(acc) // 2
    fixed = [load_fixed[0](c) for c in range(columns)]
    for c in range(columns):
        value = load_moved(c)
        for j in range(len(acc)):
            at = c - (j - half) * dilation
            if 0 <= at < columns:
                acc[j] = acc[j] + fixed[at] * value
    return acc


def row_range(r, rows, half, dilation):
    low_i = jnp.maximum(half - r // dilation, 0)
    high_i = jnp.minimum(half + (rows - 1 - r) // dilation, 2 * half)
    return low_i, high_i + 1


def zeros_list(count):
    return [jnp.zeros((SUB, LANE), f32) for _ in range(count)]


def b8(ref, i):
    return jnp.broadcast_to(ref[i : i + 1, :], (SUB, ref.shape[1]))


def make_col_mask(meta, cm):
    size = meta[2]
    for c in range(cm.shape[0]):
        cm[c] = (size > c).astype(f32)


def row_mask(meta, cm, r):
    at = (r * 1).astype(f32)
    inside = (at >= meta[1]) & (at < meta[1] + meta[2])
    return cm[...] * inside.astype(f32)[None]


def pixels3(values):
    return values.reshape(values.shape[0] // SUB, SUB, values.shape[1])


def pixels2(values):
    return values.reshape(values.shape[0] * SUB, values.shape[2])


def fold(values):
    return jnp.sum(values, axis=0)


def statistics(sums, count, i):
    mean = b8(sums, i) / count
    return mean, lax.rsqrt(b8(sums, i + 1) / count - mean * mean + epsilon)


def mixer_kernel(
    xw, cw, meta, count, sums1, scales, shifts, w_in, w_gate, w_out, kl, kd,
    xa_o, ca_o, gl_o, sl_o, c1_o, c2_o, gp_o, bn_o, sums_o,
    cm, klb, kdb, xa, ca, gl, sl, c1, c2, gp, bn, gf, c1f, sem,
):
    rows, px, channels = xa.shape
    columns = px // SUB
    groups = groups_of(channels)
    offsets = xw.shape[0] - rows + 1
    make_col_mask(meta, cm)
    spread_taps(kl, klb)
    spread_taps(kd, kdb)
    for edge in (0, 1, rows + 2, rows + 3):
        gf[:, edge] = jnp.zeros(gf.shape[:1] + gf.shape[2:], f32)
    total = count[0:1, 0:1]
    mean, rstd = statistics(sums1, total, 0)
    scale = rstd * b8(scales, 0)
    starts = [meta[0] == float(t) for t in range(offsets)]

    def aligned(ref, r):
        value = pixels3(ref[r].astype(f32))
        for t in range(1, offsets):
            value = jnp.where(starts[t][None], pixels3(ref[r + t].astype(f32)), value)
        return value

    def first(r, _):
        mask = row_mask(meta, cm, r)
        x = mask * aligned(xw, r)
        xa[r] = pixels2(x).astype(bf16)
        ca[r] = pixels2(mask * aligned(cw, r)).astype(bf16)
        normed = pixels2((x - mean) * scale + b8(shifts, 0)).astype(bf16)
        pre = pixels3(dot(normed, w_in[...])) + b8(shifts, 1)
        phi_sum, bell = normal_parts(pre)
        gelu = mask * low(pre * phi_sum)
        sl[r] = pixels2(phi_sum + pre * bell)
        gl[r] = pixels2(gelu).astype(bf16)
        for g, width in groups:
            gf[g, r + 2, :, :, :width] = gelu[:, :, g * LANE : g * LANE + width]
        return 0

    lax.fori_loop(0, rows, first, 0)
    early = [(xa, xa_o), (ca, ca_o), (gl, gl_o), (sl, sl_o)]
    copies = [pltpu.make_async_copy(a, b, sem.at[k]) for k, (a, b) in enumerate(early)]
    for copy in copies:
        copy.start()

    def local(r, _):
        mask = row_mask(meta, cm, r)
        for g, width in groups:
            acc = zeros_list(columns)
            for i in range(5):
                taps = [klb[5 * i + j, g] for j in range(5)]
                acc = add_row(acc, lambda c: gf[g, r + i, c], taps, 1)
            bias = b8(shifts, 2)[:, g * LANE : g * LANE + width]
            value = jnp.stack(acc)[:, :, :width] + bias
            value = mask[:, :, :width] * low(value)
            c1f[g, r, :, :, :width] = value
            c1[r, :, g * LANE : g * LANE + width] = pixels2(value).astype(bf16)
        return 0

    lax.fori_loop(0, rows, local, 0)
    copies.append(pltpu.make_async_copy(c1, c1_o, sem.at[4]))
    copies[-1].start()

    def dilated(r, _):
        low_i, high_i = row_range(r, rows, 3, 3)
        for g, width in groups:

            def tap_row(i, acc):
                taps = [kdb[7 * i + j, g] for j in range(7)]
                at = r + (i - 3) * 3
                return add_row(list(acc), lambda c: c1f[g, at, c], taps, 3)

            acc = lax.fori_loop(low_i, high_i, tap_row, zeros_list(columns))
            bias = b8(shifts, 3)[:, g * LANE : g * LANE + width]
            value = jnp.stack(acc)[:, :, :width] + bias
            c2[r, :, g * LANE : g * LANE + width] = pixels2(value).astype(bf16)
        return 0

    lax.fori_loop(0, rows, dilated, 0)
    copies.append(pltpu.make_async_copy(c2, c2_o, sem.at[5]))
    copies[-1].start()

    def last(r, sums):
        mask = row_mask(meta, cm, r)
        gate = dot(c2[r], w_gate[...]) + jnp.broadcast_to(shifts[4:5, :], (px, channels))
        gp[r] = gate
        gated = (gl[r].astype(f32) * gate).astype(bf16)
        branch = dot(gated, w_out[...])
        x = pixels3(xa[r].astype(f32))
        normed = low((x - mean) * scale + b8(shifts, 0))
        both = pixels3(branch) + b8(shifts, 5) + normed
        bn[r] = pixels2(both)
        middle = mask * (x + b8(scales, 1) * both)
        return sums[0] + fold(middle), sums[1] + fold(middle * middle)

    zero = jnp.zeros((SUB, channels), f32)
    sums = lax.fori_loop(0, rows, last, (zero, zero))
    copies.append(pltpu.make_async_copy(gp, gp_o, sem.at[6]))
    copies[-1].start()
    copies.append(pltpu.make_async_copy(bn, bn_o, sem.at[7]))
    copies[-1].start()
    sums_o[0] = sums[0]
    sums_o[1] = sums[1]
    for copy in copies:
        copy.wait()


def mixer_forward(xw, cw, meta, count, sums1, scales, shifts, w_in, w_gate, w_out, kl, kd):
    band, px, channels = xw.shape
    columns = px // SUB
    rows = columns
    n = len(groups_of(channels))
    small = (rows, px, channels)
    kinds = (bf16, bf16, bf16, f32, bf16, bf16, f32, f32)
    return pl.pallas_call(
        mixer_kernel,
        name="mixer_forward",
        out_shape=[jax.ShapeDtypeStruct(small, k) for k in kinds]
        + [jax.ShapeDtypeStruct((2, SUB, channels), f32)],
        in_specs=[VMEM] * 12,
        out_specs=[ANY] * 8 + [VMEM],
        scratch_shapes=[
            pltpu.VMEM((columns, SUB, channels), f32),
            pltpu.VMEM((25, n, SUB, LANE), f32),
            pltpu.VMEM((49, n, SUB, LANE), f32),
        ]
        + [pltpu.VMEM(small, k) for k in kinds]
        + [
            pltpu.VMEM((n, rows + 4, columns, SUB, LANE), f32),
            pltpu.VMEM((n, rows, columns, SUB, LANE), f32),
            pltpu.SemaphoreType.DMA((8,)),
        ],
        compiler_params=pltpu.CompilerParams(vmem_limit_bytes=56 * MIB),
    )(xw, cw, meta, count, sums1, scales, shifts, w_in, w_gate, w_out, kl, kd)


def hidden_kernel(
    xa, ca, bn, meta, count, sums2, scales, shifts, hshift, w_e, w_rt, kh,
    res_o, gn_o, gwe_o, gwr_o, gk_o, gh_o, sums_o,
    cm, khb, kfb, n2, gr, ha, ge, em, gc, kacc, wet, wr, sem,
):
    rows, px, channels = xa.shape
    columns = px // SUB
    hidden = w_e.shape[1]
    wide = em.shape[0] * LANE
    parts = em.shape[0]
    make_col_mask(meta, cm)
    spread_taps(kh, khb)
    spread_taps(kh, kfb, flip=True)
    for edge in (0, rows + 1):
        em[:, edge] = jnp.zeros(em.shape[:1] + em.shape[2:], f32)
        gc[:, edge] = jnp.zeros(gc.shape[:1] + gc.shape[2:], f32)
    wet[...] = w_e[...].astype(f32).T.astype(bf16)
    wr[...] = w_rt[...].astype(f32).T.astype(bf16)
    total = count[0:1, 0:1]
    mean, rstd = statistics(sums2, total, 0)
    scale = rstd * b8(scales, 2)

    def middle_of(r):
        return pixels3(xa[r].astype(f32)) + b8(scales, 1) * pixels3(bn[r])

    def prepare(r, acc):
        normed = (middle_of(r) - mean) * scale + b8(shifts, 6)
        n2[r] = pixels2(normed).astype(bf16)
        grad = (b8(scales, 3) * pixels3(ca[r].astype(f32))).astype(bf16)
        gr[r] = pixels2(grad)
        return acc + fold(grad.astype(f32))

    zero = jnp.zeros((SUB, channels), f32)
    sums_o[2] = lax.fori_loop(0, rows, prepare, zero)

    def chunk(f, _):
        base = pl.multiple_of(f * wide, wide)
        lanes = pl.ds(base, wide)
        group = f * parts

        def expand(r, _):
            mask = row_mask(meta, cm, r)[:, :, :LANE]
            value = dot(n2[r], w_e[:, lanes])
            value = low(value + jnp.broadcast_to(hshift[0:1, lanes], value.shape))
            for g in range(parts):
                em[g, r + 1] = mask * pixels3(value[:, g * LANE : (g + 1) * LANE])
            return 0

        lax.fori_loop(0, rows, expand, 0)

        def forward(r, acc):
            grad = dot(gr[r], w_rt[:, lanes])
            out = []
            for g in range(parts):
                conv = zeros_list(columns)
                for i in range(3):
                    taps = [khb[3 * i + j, group + g] for j in range(3)]
                    conv = add_row(conv, lambda c: em[g, r + i, c], taps, 1)
                here = pl.ds(pl.multiple_of(base + g * LANE, LANE), LANE)
                v = jnp.stack(conv) + jnp.broadcast_to(hshift[1:2, here], (SUB, LANE))
                phi_sum, bell = normal_parts(v)
                ha[r, :, here] = pixels2(v * phi_sum).astype(bf16)
                part = pixels3(grad[:, g * LANE : (g + 1) * LANE])
                back = low(part * (phi_sum + v * bell))
                gc[g, r + 1] = back
                out.append(acc[g] + fold(back))
            return tuple(out)

        bias = lax.fori_loop(0, rows, forward, tuple(zeros_list(parts)))
        for g in range(parts):
            here = pl.ds(pl.multiple_of(base + g * LANE, LANE), LANE)
            gh_o[1:2, here] = jnp.sum(bias[g], axis=0, keepdims=True)
            for tap in range(9):
                kacc[g, tap] = jnp.zeros((SUB, LANE), f32)

        def backward(r, acc):
            mask = row_mask(meta, cm, r)[:, :, :LANE]
            out = []
            for g in range(parts):
                conv = zeros_list(columns)
                for i in range(3):
                    taps = [kfb[3 * i + j, group + g] for j in range(3)]
                    sums = [kacc[g, 3 * i + j] for j in range(3)]
                    fixed = [em[g, r + 1, c] for c in range(columns)]
                    for c in range(columns):
                        value = gc[g, r + i, c]
                        for j in range(3):
                            at = c - (j - 1)
                            if 0 <= at < columns:
                                conv[at] = conv[at] + taps[j] * value
                                sums[j] = sums[j] + fixed[at] * value
                    for j in range(3):
                        kacc[g, 3 * i + j] = sums[j]
                here = pl.ds(pl.multiple_of(base + g * LANE, LANE), LANE)
                value = low(mask * jnp.stack(conv))
                ge[r, :, here] = pixels2(value).astype(bf16)
                out.append(acc[g] + fold(value))
            return tuple(out)

        bias = lax.fori_loop(0, rows, backward, tuple(zeros_list(parts)))
        for g in range(parts):
            here = pl.ds(pl.multiple_of(base + g * LANE, LANE), LANE)
            gh_o[0:1, here] = jnp.sum(bias[g], axis=0, keepdims=True)
            for tap in range(9):
                gk_o[8 - tap : 9 - tap, here] = jnp.sum(kacc[g, tap], axis=0, keepdims=True)
        return 0

    lax.fori_loop(0, hidden // wide, chunk, 0)

    whole = rows * px
    gwe_o[...] = dot_tn(n2[...].reshape(whole, channels), ge[...].reshape(whole, hidden))
    gwr_o[...] = dot_tn(gr[...].reshape(whole, channels), ha[...].reshape(whole, hidden))

    def finish(r, sums):
        mask = row_mask(meta, cm, r)
        reduced = pixels3(dot(ha[r], wr[...])) + b8(shifts, 7)
        middle = middle_of(r)
        res_o[r] = pixels2(mask * (middle + b8(scales, 3) * reduced))
        gn = pixels3(dot(ge[r], wet[...]))
        gn_o[r] = pixels2(gn)
        hat = (middle - mean) * rstd
        out = pixels3(ca[r].astype(f32))
        return sums[0] + fold(gn), sums[1] + fold(gn * hat), sums[2] + fold(out * reduced)

    sums = lax.fori_loop(0, rows, finish, (zero, zero, zero))
    sums_o[0] = sums[0]
    sums_o[1] = sums[1]
    sums_o[3] = sums[2]


def hidden_block(xa, ca, bn, meta, count, sums2, scales, shifts, hshift, w_e, w_rt, kh):
    rows, px, channels = xa.shape
    columns = px // SUB
    hidden = w_e.shape[1]
    groups = hidden // LANE
    parts = 2
    shape = jax.ShapeDtypeStruct
    return pl.pallas_call(
        hidden_kernel,
        name="hidden_block",
        out_shape=[
            shape((rows, px, channels), f32),
            shape((rows, px, channels), f32),
            shape((channels, hidden), f32),
            shape((channels, hidden), f32),
            shape((9, hidden), f32),
            shape((2, hidden), f32),
            shape((4, SUB, channels), f32),
        ],
        in_specs=[VMEM] * 12,
        out_specs=[VMEM] * 7,
        scratch_shapes=[
            pltpu.VMEM((columns, SUB, channels), f32),
            pltpu.VMEM((9, groups, SUB, LANE), f32),
            pltpu.VMEM((9, groups, SUB, LANE), f32),
            pltpu.VMEM((rows, px, channels), bf16),
            pltpu.VMEM((rows, px, channels), bf16),
            pltpu.VMEM((rows, px, hidden), bf16),
            pltpu.VMEM((rows, px, hidden), bf16),
            pltpu.VMEM((parts, rows + 2, columns, SUB, LANE), f32),
            pltpu.VMEM((parts, rows + 2, columns, SUB, LANE), f32),
            pltpu.VMEM((parts, 9, SUB, LANE), f32),
            pltpu.VMEM((hidden, channels), bf16),
            pltpu.VMEM((hidden, channels), bf16),
            pltpu.SemaphoreType.DMA((1,)),
        ],
        compiler_params=pltpu.CompilerParams(vmem_limit_bytes=60 * MIB),
    )(xa, ca, bn, meta, count, sums2, scales, shifts, hshift, w_e, w_rt, kh)


def back_kernel(
    gn, bn, xa, ca, gl, sl, c1, c2, gp, meta, count, sums1, sums2, sums3, scales, shifts,
    w_in, w_gate, w_out, kl, kd,
    mix_o, gwi_o, gwg_o, gwo_o, gkl_o, gkd_o, sums_o,
    cm, klb, kdb, gb, gg, gt, gm, tt, g2, g1, src, sem,
):
    rows, px, channels = xa.shape
    columns = px // SUB
    groups = groups_of(channels)
    make_col_mask(meta, cm)
    spread_taps(kl, klb, flip=True)
    spread_taps(kd, kdb, flip=True)
    for edge in (0, 1, rows + 2, rows + 3):
        g1[:, edge] = jnp.zeros(g1.shape[:1] + g1.shape[2:], f32)
    total = count[0:1, 0:1]
    mean1, rstd1 = statistics(sums1, total, 0)
    scale1 = rstd1 * b8(scales, 0)
    mean2, rstd2 = statistics(sums2, total, 0)
    scale2 = rstd2 * b8(scales, 2)
    back0 = b8(sums3, 0) / total
    back1 = b8(sums3, 1) / total
    zero = jnp.zeros((SUB, channels), f32)

    def first(r, sums):
        mask = row_mask(meta, cm, r)
        both = pixels3(bn[r])
        middle = pixels3(xa[r].astype(f32)) + b8(scales, 1) * both
        hat = (middle - mean2) * rstd2
        grad = pixels3(ca[r].astype(f32)) + scale2 * (
            pixels3(gn[r]) - mask * (back0 + hat * back1)
        )
        gm[r] = pixels2(grad)
        branch = (b8(scales, 1) * grad).astype(bf16)
        gb[r] = pixels2(branch)
        gated_grad = dot_nt(pixels2(branch), w_out[...])
        gelu = gl[r].astype(f32)
        gate_grad = (gated_grad * gelu).astype(bf16)
        gg[r] = gate_grad
        gt[r] = (gelu * gp[r]).astype(bf16)
        tt[r] = gated_grad * gp[r]
        conv = low(dot_nt(gate_grad, w_gate[...]))
        for g, width in groups:
            g2[g, r, :, :, :width] = pixels3(conv[:, g * LANE : g * LANE + width])
            src[g, r, :, :, :width] = pixels3(c1[r, :, g * LANE : g * LANE + width].astype(f32))
        return (
            sums[0] + fold(grad * both),
            sums[1] + fold(branch.astype(f32)),
            sums[2] + fold(pixels3(gate_grad.astype(f32))),
            sums[3] + fold(pixels3(conv)),
        )

    sums = lax.fori_loop(0, rows, first, (zero,) * 4)
    for k in range(4):
        sums_o[2 + k] = sums[k]
    whole = rows * px
    flat = lambda ref: ref[...].reshape(whole, channels)
    gwo_o[...] = dot_tn(flat(gt), flat(gb))
    gwg_o[...] = dot_tn(flat(c2), flat(gg))

    for g, width in groups:
        for i in range(7):
            first_row = max(0, 3 * (3 - i))
            last_row = min(rows, rows - 3 * (i - 3))

            def taps_row(r, acc, g=g, i=i):
                at = r + (i - 3) * 3
                return tap_sums(
                    list(acc), (lambda c: g2[g, r, c], columns), lambda c: src[g, at, c], 3
                )

            acc = lax.fori_loop(first_row, last_row, taps_row, zeros_list(7))
            for j in range(7):
                row = jnp.sum(acc[j], axis=0, keepdims=True)
                gkd_o[7 * i + j : 7 * i + j + 1, g * LANE : g * LANE + width] = row[:, :width]

    def dilated(r, sums):
        mask = row_mask(meta, cm, r)
        low_i, high_i = row_range(r, rows, 3, 3)
        out = []
        for g, width in groups:

            def tap_row(i, acc):
                taps = [kdb[7 * i + j, g] for j in range(7)]
                at = r + (i - 3) * 3
                return add_row(list(acc), lambda c: g2[g, at, c], taps, 3)

            acc = lax.fori_loop(low_i, high_i, tap_row, zeros_list(columns))
            value = low(mask[:, :, :width] * jnp.stack(acc)[:, :, :width])
            g1[g, r + 2, :, :, :width] = value
            out.append(sums[g] + fold(value))
        return tuple(out)

    start = tuple(jnp.zeros((SUB, width), f32) for g, width in groups)
    sums = lax.fori_loop(0, rows, dilated, start)
    for g, width in groups:
        sums_o[6, :, g * LANE : g * LANE + width] = sums[g]

    def refill(r, _):
        for g, width in groups:
            src[g, r, :, :, :width] = pixels3(gl[r, :, g * LANE : g * LANE + width].astype(f32))
        return 0

    lax.fori_loop(0, rows, refill, 0)

    for g, width in groups:
        for i in range(5):

            def taps_row(r, acc, g=g, i=i):
                return tap_sums(
                    list(acc), (lambda c: src[g, r, c], columns), lambda c: g1[g, r + i, c], 1
                )

            acc = lax.fori_loop(0, rows, taps_row, zeros_list(5))
            for j in range(5):
                tap = 24 - (5 * i + j)
                row = jnp.sum(acc[j], axis=0, keepdims=True)
                gkl_o[tap : tap + 1, g * LANE : g * LANE + width] = row[:, :width]

    def local(r, sums):
        mask = row_mask(meta, cm, r)
        parts = []
        for g, width in groups:
            acc = zeros_list(columns)
            for i in range(5):
                taps = [klb[5 * i + j, g] for j in range(5)]
                acc = add_row(acc, lambda c: g1[g, r + i, c], taps, 1)
            value = mask[:, :, :width] * jnp.stack(acc)[:, :, :width]
            at = slice(g * LANE, g * LANE + width)
            grad = (tt[r, :, at] + pixels2(value)) * sl[r, :, at]
            gg[r, :, at] = grad.astype(bf16)
            parts.append(sums[g] + fold(pixels3(low(grad))))
        return tuple(parts)

    sums = lax.fori_loop(0, rows, local, start)
    for g, width in groups:
        sums_o[7, :, g * LANE : g * LANE + width] = sums[g]

    def last(r, sums):
        x = pixels3(xa[r].astype(f32))
        grad = pixels3(gm[r])
        gn1 = pixels3(dot_nt(gg[r], w_in[...])) + b8(scales, 1) * grad
        mix_o[r] = pixels2(grad + scale1 * gn1)
        hat = (x - mean1) * rstd1
        normed = (x - mean1) * scale1 + b8(shifts, 0)
        gb[r] = pixels2(normed).astype(bf16)
        return sums[0] + fold(gn1), sums[1] + fold(gn1 * hat)

    sums = lax.fori_loop(0, rows, last, (zero, zero))
    sums_o[0] = sums[0]
    sums_o[1] = sums[1]
    gwi_o[...] = dot_tn(flat(gb), flat(gg))


def mixer_back(gn, bn, xa, ca, gl, sl, c1, c2, gp, meta, count, sums1, sums2, sums3, scales,
               shifts, w_in, w_gate, w_out, kl, kd):
    rows, px, channels = xa.shape
    columns = px // SUB
    n = len(groups_of(channels))
    small = (rows, px, channels)
    shape = jax.ShapeDtypeStruct
    square = shape((channels, channels), f32)
    return pl.pallas_call(
        back_kernel,
        name="mixer_back",
        out_shape=[
            shape(small, f32), square, square, square,
            shape((25, channels), f32), shape((49, channels), f32), shape((8, SUB, channels), f32),
        ],
        in_specs=[VMEM] * 21,
        out_specs=[VMEM] * 7,
        scratch_shapes=[
            pltpu.VMEM((columns, SUB, channels), f32),
            pltpu.VMEM((25, n, SUB, LANE), f32),
            pltpu.VMEM((49, n, SUB, LANE), f32),
            pltpu.VMEM(small, bf16),
            pltpu.VMEM(small, bf16),
            pltpu.VMEM(small, bf16),
            pltpu.VMEM(small, f32),
            pltpu.VMEM(small, f32),
            pltpu.VMEM((n, rows, columns, SUB, LANE), f32),
            pltpu.VMEM((n, rows + 4, columns, SUB, LANE), f32),
            pltpu.VMEM((n, rows, columns, SUB, LANE), f32),
            pltpu.SemaphoreType.DMA((1,)),
        ],
        compiler_params=pltpu.CompilerParams(vmem_limit_bytes=62 * MIB),
    )(gn, bn, xa, ca, gl, sl, c1, c2, gp, meta, count, sums1, sums2, sums3, scales, shifts,
      w_in, w_gate, w_out, kl, kd)


def input_kernel(mix, xa, meta, count, sums1, sums4, scales, out, cm, al):
    rows, px, channels = xa.shape
    make_col_mask(meta, cm)
    total = count[0:1, 0:1]
    mean1, rstd1 = statistics(sums1, total, 0)
    scale1 = rstd1 * b8(scales, 0)
    back0 = b8(sums4, 0) / total
    back1 = b8(sums4, 1) / total

    def one(r, _):
        mask = row_mask(meta, cm, r)
        hat = (pixels3(xa[r].astype(f32)) - mean1) * rstd1
        grad = mask * (pixels3(mix[r]) - scale1 * (back0 + hat * back1))
        al[r] = pixels2(grad)
        return 0

    lax.fori_loop(0, rows, one, 0)
    unalign(al, meta, out)


def unalign(al, meta, out):
    rows, px, channels = al.shape
    offsets = out.shape[0] - rows + 1
    for at in range(out.shape[0]):
        value = jnp.zeros((px // SUB, SUB, channels), f32)
        for t in range(offsets):
            if 0 <= at - t < rows:
                chosen = (meta[0] == float(t))[None]
                value = jnp.where(chosen, pixels3(al[at - t]), value)
        out[at] = pixels2(value)


def input_grad_kernel(mix, xa, meta, count, sums1, sums4, scales, band):
    rows, px, channels = xa.shape
    return pl.pallas_call(
        input_kernel,
        name="input_grad",
        out_shape=jax.ShapeDtypeStruct((band, px, channels), f32),
        in_specs=[VMEM] * 7,
        out_specs=VMEM,
        scratch_shapes=[
            pltpu.VMEM((px // SUB, SUB, channels), f32),
            pltpu.VMEM((rows, px, channels), f32),
        ],
        compiler_params=pltpu.CompilerParams(vmem_limit_bytes=56 * MIB),
    )(mix, xa, meta, count, sums1, sums4, scales)


def unalign_kernel(res, meta, out):
    unalign(res, meta, out)


def unaligned(res, meta, band):
    rows, px, channels = res.shape
    return pl.pallas_call(
        unalign_kernel,
        name="unalign",
        out_shape=jax.ShapeDtypeStruct((band, px, channels), f32),
        in_specs=[VMEM] * 2,
        out_specs=VMEM,
        compiler_params=pltpu.CompilerParams(vmem_limit_bytes=56 * MIB),
    )(res, meta)


def reduce_kernel(stages, v_ref, out_ref, mine, *rest):
    slots, sems = rest[: len(stages)], rest[len(stages) :]
    core = lax.axis_index("rows")
    chip = lax.axis_index("imgs")
    barrier = pltpu.get_barrier_semaphore()
    peers = []
    for axis, stride, size in stages:
        place = lax.rem((core if axis == "rows" else chip) // stride, size)
        stage = []
        for step in range(1, size):
            other = lax.rem(place + step, size)
            index = (core if axis == "rows" else chip) + (other - place) * stride
            stage.append((step, (index, chip) if axis == "rows" else (core, index)))
        peers.append(stage)
    for stage in peers:
        for step, device in stage:
            pl.semaphore_signal(barrier, inc=1, device_id=device, device_id_type=MESH)
    pl.semaphore_wait(barrier, sum(len(stage) for stage in peers))
    mine[...] = jnp.sum(v_ref[...], axis=1)
    for k, stage in enumerate(peers):
        slot, (send, recv) = slots[k], sems[2 * k : 2 * k + 2]
        copies = []
        for step, device in stage:
            copies.append(
                pltpu.make_async_remote_copy(
                    src_ref=mine,
                    dst_ref=slot.at[step - 1],
                    send_sem=send.at[step - 1],
                    recv_sem=recv.at[step - 1],
                    device_id=device,
                    device_id_type=MESH,
                )
            )
            copies[-1].start()
        for copy in copies:
            copy.wait()
        total = mine[...]
        for step, device in stage:
            total = total + slot[step - 1]
        mine[...] = total
    out_ref[...] = mine[...]


def reduce_all(v, sizes, collective_id):
    k, _, channels = v.shape
    stages = [("rows", 1, sizes["rows"])]
    left, stride = sizes["imgs"], 1
    while left > 1:
        size = 4 if left % 4 == 0 else (2 if left % 2 == 0 else left)
        stages.append(("imgs", stride, size))
        left, stride = left // size, stride * size
    stages = [s for s in stages if s[2] > 1]
    table = (k, channels)
    sems = []
    for _, _, size in stages:
        sems += [pltpu.SemaphoreType.DMA((size - 1,))] * 2
    return pl.pallas_call(
        functools.partial(reduce_kernel, stages),
        name="reduce_all",
        out_shape=jax.ShapeDtypeStruct(table, f32),
        in_specs=[VMEM],
        out_specs=VMEM,
        scratch_shapes=[pltpu.VMEM(table, f32)]
        + [pltpu.VMEM((size - 1,) + table, f32) for _, _, size in stages]
        + sems,
        compiler_params=pltpu.CompilerParams(collective_id=collective_id, has_side_effects=True),
    )(v)


def halves(values, core, half, axis):
    mine = lax.dynamic_slice_in_dim(values, core * half, half, axis=axis)
    other = lax.dynamic_slice_in_dim(values, (1 - core) * half, half, axis=axis)
    return mine, lax.ppermute(other, "rows", [(0, 1), (1, 0)])


def first_sums_kernel(x, meta, out, cm):
    rows, columns, images, channels = x.shape
    size, top = meta[2], meta[0]
    for c in range(columns):
        cm[c] = (size > c).astype(f32)

    def one(r, sums):
        at = (r * 1).astype(f32)
        inside = ((at >= top) & (at < top + size)).astype(f32)
        value = cm[...] * inside[None] * x[r].astype(f32)
        return sums[0] + fold(value), sums[1] + fold(value * value)

    zero = jnp.zeros((images, channels), f32)
    sums = lax.fori_loop(0, rows, one, (zero, zero))
    for k in range(2):
        out[k] = sums[k][:SUB] + sums[k][SUB:]


def first_sums(x, meta):
    rows, columns, images, channels = x.shape
    return pl.pallas_call(
        first_sums_kernel,
        name="first_sums",
        out_shape=jax.ShapeDtypeStruct((2, SUB, channels), f32),
        in_specs=[VMEM] * 2,
        out_specs=VMEM,
        scratch_shapes=[pltpu.VMEM((columns, images, channels), f32)],
        compiler_params=pltpu.CompilerParams(vmem_limit_bytes=32 * MIB),
    )(x, meta)


def on_device(sizes, inputs, cotangent, scales, shifts, hidden_shift, w_inward, w_gating,
              w_outward, w_expand, w_reduce, kernel_local, kernel_dilated, kernel_hidden,
              image_size, band_split, slot_image):
    images, band, columns, channels = inputs.shape
    half = images // 2
    px = columns * half
    core = lax.axis_index("rows")
    counted = jnp.sum(image_size * image_size).astype(f32)
    count = jnp.full((SUB, LANE), counted)
    everyone = jnp.arange(image_size.shape[0], dtype=jnp.int32)
    chosen = (slot_image[:, None] == everyone[None, :]).astype(jnp.int32)
    extent = jnp.sum(chosen * image_size[None, :], axis=1)
    top = band - jnp.sum(chosen * band_split[None, :], axis=1)
    start = jnp.clip(top, 0, 2 * band - columns)
    own_meta = jnp.stack([top - core * band, top, extent]).astype(f32)
    own_meta = jnp.broadcast_to(own_meta[:, :, None], (3, images, channels))
    meta = jnp.stack([start, top - start, extent]).astype(f32)
    meta = lax.dynamic_slice_in_dim(meta, core * half, half, axis=1)
    meta = jnp.broadcast_to(meta[:, :, None], (3, half, channels))

    x = jnp.transpose(inputs, (1, 2, 0, 3))
    y = jnp.transpose(cotangent, (1, 2, 0, 3))
    sums1 = reduce_all(first_sums(x, own_meta), sizes, 1)

    def gather_rows(v):
        mine, theirs = halves(v, core, half, 2)
        upper = jnp.where(core == 0, mine, theirs)
        lower = jnp.where(core == 0, theirs, mine)
        return jnp.concatenate([upper, lower], axis=0).reshape(2 * band, px, channels)

    xw, cw = gather_rows(x), gather_rows(y)
    xa, ca, gl, sl, c1, c2, gp, bn, part2 = mixer_forward(
        xw, cw, meta, count, sums1, scales, shifts, w_inward, w_gating, w_outward,
        kernel_local, kernel_dilated,
    )
    sums2 = reduce_all(part2, sizes, 2)
    res, gn, gwe, gwr, gk, gh, part3 = hidden_block(
        xa, ca, bn, meta, count, sums2, scales, shifts, hidden_shift, w_expand, w_reduce.T,
        kernel_hidden,
    )
    sums3 = reduce_all(part3, sizes, 3)
    mix, gwi, gwg, gwo, gkl, gkd, part4 = mixer_back(
        gn, bn, xa, ca, gl, sl, c1, c2, gp, meta, count, sums1, sums2, sums3, scales, shifts,
        w_inward, w_gating, w_outward, kernel_local, kernel_dilated,
    )
    sums4 = reduce_all(part4, sizes, 4)

    def scatter_rows(v):
        v = v.reshape(2 * band, columns, half, channels)
        mine = lax.dynamic_slice_in_dim(v, core * band, band, axis=0)
        other = lax.dynamic_slice_in_dim(v, (1 - core) * band, band, axis=0)
        theirs = lax.ppermute(other, "rows", [(0, 1), (1, 0)])
        lower = jnp.where(core == 0, mine, theirs)
        upper = jnp.where(core == 0, theirs, mine)
        both = jnp.concatenate([lower, upper], axis=2)
        return jnp.transpose(both, (2, 0, 1, 3))

    result = scatter_rows(unaligned(res, meta, 2 * band))
    input_grad = scatter_rows(
        input_grad_kernel(mix, xa, meta, count, sums1, sums4, scales, 2 * band)
    )
    gwe, gwr, gk, gh, gwi, gwg, gwo, gkl, gkd = lax.psum(
        (gwe, gwr, gk, gh, gwi, gwg, gwo, gkl, gkd), ("rows", "imgs")
    )
    scales_grad = jnp.stack([sums4[1], sums4[2], sums3[1], sums3[3]])
    shifts_grad = jnp.stack(
        [sums4[0], sums4[7], sums4[6], sums4[5], sums4[4], sums4[3], sums3[0], sums3[2]]
    )
    return (
        result, input_grad, scales_grad, shifts_grad, gh, gwi, gwg, gwo, gwe, gwr.T,
        gkl, gkd, gk,
    )


def solution(mesh):
    wide = P("imgs", "rows", None, None)
    sizes = dict(mesh.shape)
    return jax.shard_map(
        functools.partial(on_device, sizes),
        mesh=mesh,
        in_specs=(wide, wide) + (P(),) * 13 + (P("imgs"),),
        out_specs=(wide, wide) + (P(),) * 11,
        check_vma=False,
    )
```

```python
import functools
import math

import jax
import jax.numpy as jnp
from jax import lax
from jax.experimental import pallas as pl
from jax.experimental.pallas import tpu as pltpu
from jax.sharding import PartitionSpec as P

MESH = pl.DeviceIdType.MESH
epsilon = 1e-05
bf16 = jnp.bfloat16
f32 = jnp.float32
SUB = 8
LANE = 128
MIB = 1 << 20
ANY = pl.BlockSpec(memory_space=pl.ANY)
VMEM = pl.BlockSpec(memory_space=pltpu.VMEM)


def low(values):
    return values.astype(bf16).astype(f32)


def normal_parts(v):
    bell = jnp.exp(-0.5 * (v * v))
    base = 1.0 + (0.3275911 * 0.7071067811865476) * jnp.abs(v)
    t = pl.reciprocal(base, approx=True)
    t = t * (2.0 - base * t)
    poly = 0.5 * 1.061405429
    for coef in (-1.453152027, 1.421413741, -0.284496736, 0.254829592):
        poly = poly * t + 0.5 * coef
    tail = poly * t * bell
    return jnp.where(v >= 0, 1.0 - tail, tail), bell * 0.3989422804014327


def dot(a, b):
    return jnp.dot(a, b, preferred_element_type=f32)


def dot_nt(a, b):
    return lax.dot_general(a, b, (((1,), (1,)), ((), ())), preferred_element_type=f32)


def dot_tn(a, b):
    return lax.dot_general(a, b, (((0,), (0,)), ((), ())), preferred_element_type=f32)


def groups_of(channels):
    return [(g, min(LANE, channels - g * LANE)) for g in range(pl.cdiv(channels, LANE))]


def spread_taps(k_ref, kb, flip=False):
    count, channels = k_ref.shape
    for tap in range(count):
        from_tap = count - 1 - tap if flip else tap
        row = jnp.broadcast_to(k_ref[from_tap : from_tap + 1, :], (SUB, channels))
        for g, width in groups_of(channels):
            kb[tap, g, :, :width] = row[:, g * LANE : g * LANE + width]


def add_row(acc, load, taps, dilation):
    columns, half = len(acc), len(taps) // 2
    for c in range(columns):
        value = load(c)
        for j, tap in enumerate(taps):
            at = c - (j - half) * dilation
            if 0 <= at < columns:
                acc[at] = acc[at] + tap * value
    return acc


def tap_sums(acc, load_fixed, load_moved, dilation):
    columns, half = load_fixed[1], len(acc) // 2
    fixed = [load_fixed[0](c) for c in range(columns)]
    for c in range(columns):
        value = load_moved(c)
        for j in range(len(acc)):
            at = c - (j - half) * dilation
            if 0 <= at < columns:
                acc[j] = acc[j] + fixed[at] * value
    return acc


def row_range(r, rows, half, dilation):
    low_i = jnp.maximum(half - r // dilation, 0)
    high_i = jnp.minimum(half + (rows - 1 - r) // dilation, 2 * half)
    return low_i, high_i + 1


def zeros_list(count):
    return [jnp.zeros((SUB, LANE), f32) for _ in range(count)]


def b8(ref, i):
    return jnp.broadcast_to(ref[i : i + 1, :], (SUB, ref.shape[1]))


def make_col_mask(meta, cm):
    size = meta[2]
    for c in range(cm.shape[0]):
        cm[c] = (size > c).astype(f32)


def row_mask(meta, cm, r):
    at = (r * 1).astype(f32)
    inside = (at >= meta[1]) & (at < meta[1] + meta[2])
    return cm[...] * inside.astype(f32)[None]


def pixels3(values):
    return values.reshape(values.shape[0] // SUB, SUB, values.shape[1])


def pixels2(values):
    return values.reshape(values.shape[0] * SUB, values.shape[2])


def fold(values):
    return jnp.sum(values, axis=0)


def statistics(sums, count, i):
    mean = b8(sums, i) / count
    return mean, lax.rsqrt(b8(sums, i + 1) / count - mean * mean + epsilon)


def stage_list(sizes):
    stages = [("rows", 1, sizes["rows"])]
    left, stride = sizes["imgs"], 1
    while left > 1:
        size = 4 if left % 4 == 0 else (2 if left % 2 == 0 else left)
        stages.append(("imgs", stride, size))
        left, stride = left // size, stride * size
    return [s for s in stages if s[2] > 1]


def stage_peers(stages):
    core = lax.axis_index("rows")
    chip = lax.axis_index("imgs")
    found = []
    for axis, stride, size in stages:
        index = core if axis == "rows" else chip
        place = lax.rem(index // stride, size)
        peers = []
        for step in range(1, size):
            other = lax.rem(place + step, size)
            at = index + (other - place) * stride
            peers.append((step, other, (at, chip) if axis == "rows" else (core, at)))
        found.append((place, peers))
    return found


def say_here(found):
    barrier = pltpu.get_barrier_semaphore()
    for _, peers in found:
        for _, _, device in peers:
            pl.semaphore_signal(barrier, inc=1, device_id=device, device_id_type=MESH)


def wait_all_here(found):
    pl.semaphore_wait(pltpu.get_barrier_semaphore(), sum(len(peers) for _, peers in found))


def greet(found):
    say_here(found)
    wait_all_here(found)


def remote(src, dst, send, recv, device):
    return pltpu.make_async_remote_copy(
        src_ref=src, dst_ref=dst, send_sem=send, recv_sem=recv,
        device_id=device, device_id_type=MESH,
    )


def all_sum(mine, slots, sems, found):
    for k, (_, peers) in enumerate(found):
        slot, (send, recv) = slots[k], sems[2 * k : 2 * k + 2]
        copies = []
        for step, _, device in peers:
            copies.append(
                remote(mine, slot.at[step - 1], send.at[step - 1], recv.at[step - 1], device)
            )
            copies[-1].start()
        for copy in copies:
            copy.wait()
        total = mine[...]
        for step, _, _ in peers:
            total = total + slot[step - 1]
        mine[...] = total


def sum_scratch(stages, table):
    sems = []
    for _, _, size in stages:
        sems += [pltpu.SemaphoreType.DMA((size - 1,))] * 2
    slots = [pltpu.VMEM((size - 1,) + table, f32) for _, _, size in stages]
    return [pltpu.VMEM(table, f32)] + slots + sems


def reduce_kernel(stages, v_ref, out_ref, mine, *rest):
    found = stage_peers(stages)
    greet(found)
    mine[...] = jnp.sum(v_ref[...], axis=1)
    all_sum(mine, rest[: len(stages)], rest[len(stages) :], found)
    out_ref[...] = mine[...]


def reduce_all(v, stages, collective_id):
    k, _, channels = v.shape
    table = (k, channels)
    return pl.pallas_call(
        functools.partial(reduce_kernel, stages),
        name="reduce_all",
        out_shape=jax.ShapeDtypeStruct(table, f32),
        in_specs=[VMEM],
        out_specs=VMEM,
        scratch_shapes=sum_scratch(stages, table),
        compiler_params=pltpu.CompilerParams(collective_id=collective_id, has_side_effects=True),
    )(v)


def mixer_kernel(
    stages, xw, cw, meta, count, sums1, scales, shifts, w_in, w_gate, w_out, kl, kd,
    xa_o, ca_o, gl_o, sl_o, c1_o, c2_o, gp_o, bn_o, sums_o,
    cm, klb, kdb, xa, ca, gl, sl, c1, c2, gp, bn, gf, c1f, sem, mine, *rest,
):
    found = stage_peers(stages)
    say_here(found)
    rows, px, channels = xa.shape
    columns = px // SUB
    groups = groups_of(channels)
    offsets = xw.shape[0] - rows + 1
    make_col_mask(meta, cm)
    spread_taps(kl, klb)
    spread_taps(kd, kdb)
    for edge in (0, 1, rows + 2, rows + 3):
        gf[:, edge] = jnp.zeros(gf.shape[:1] + gf.shape[2:], f32)
    total = count[0:1, 0:1]
    mean, rstd = statistics(sums1, total, 0)
    scale = rstd * b8(scales, 0)
    starts = [meta[0] == float(t) for t in range(offsets)]

    def aligned(ref, r):
        value = pixels3(ref[r].astype(f32))
        for t in range(1, offsets):
            value = jnp.where(starts[t][None], pixels3(ref[r + t].astype(f32)), value)
        return value

    def first(r, _):
        mask = row_mask(meta, cm, r)
        x = mask * aligned(xw, r)
        xa[r] = pixels2(x).astype(bf16)
        ca[r] = pixels2(mask * aligned(cw, r)).astype(bf16)
        normed = pixels2((x - mean) * scale + b8(shifts, 0)).astype(bf16)
        pre = pixels3(dot(normed, w_in[...])) + b8(shifts, 1)
        phi_sum, bell = normal_parts(pre)
        gelu = mask * low(pre * phi_sum)
        sl[r] = pixels2(phi_sum + pre * bell)
        gl[r] = pixels2(gelu).astype(bf16)
        for g, width in groups:
            gf[g, r + 2, :, :, :width] = gelu[:, :, g * LANE : g * LANE + width]
        return 0

    lax.fori_loop(0, rows, first, 0)
    early = [(xa, xa_o), (ca, ca_o), (gl, gl_o), (sl, sl_o)]
    copies = [pltpu.make_async_copy(a, b, sem.at[k]) for k, (a, b) in enumerate(early)]
    for copy in copies:
        copy.start()

    def local(r, _):
        mask = row_mask(meta, cm, r)
        for g, width in groups:
            acc = zeros_list(columns)
            for i in range(5):
                taps = [klb[5 * i + j, g] for j in range(5)]
                acc = add_row(acc, lambda c: gf[g, r + i, c], taps, 1)
            bias = b8(shifts, 2)[:, g * LANE : g * LANE + width]
            value = jnp.stack(acc)[:, :, :width] + bias
            value = mask[:, :, :width] * low(value)
            c1f[g, r, :, :, :width] = value
            c1[r, :, g * LANE : g * LANE + width] = pixels2(value).astype(bf16)
        return 0

    lax.fori_loop(0, rows, local, 0)
    copies.append(pltpu.make_async_copy(c1, c1_o, sem.at[4]))
    copies[-1].start()

    def dilated(r, _):
        low_i, high_i = row_range(r, rows, 3, 3)
        for g, width in groups:

            def tap_row(i, acc):
                taps = [kdb[7 * i + j, g] for j in range(7)]
                at = r + (i - 3) * 3
                return add_row(list(acc), lambda c: c1f[g, at, c], taps, 3)

            acc = lax.fori_loop(low_i, high_i, tap_row, zeros_list(columns))
            bias = b8(shifts, 3)[:, g * LANE : g * LANE + width]
            value = jnp.stack(acc)[:, :, :width] + bias
            c2[r, :, g * LANE : g * LANE + width] = pixels2(value).astype(bf16)
        return 0

    lax.fori_loop(0, rows, dilated, 0)
    copies.append(pltpu.make_async_copy(c2, c2_o, sem.at[5]))
    copies[-1].start()

    def last(r, sums):
        mask = row_mask(meta, cm, r)
        gate = dot(c2[r], w_gate[...]) + jnp.broadcast_to(shifts[4:5, :], (px, channels))
        gp[r] = gate
        gated = (gl[r].astype(f32) * gate).astype(bf16)
        branch = dot(gated, w_out[...])
        x = pixels3(xa[r].astype(f32))
        normed = low((x - mean) * scale + b8(shifts, 0))
        both = pixels3(branch) + b8(shifts, 5) + normed
        bn[r] = pixels2(both)
        middle = mask * (x + b8(scales, 1) * both)
        return sums[0] + fold(middle), sums[1] + fold(middle * middle)

    zero = jnp.zeros((SUB, channels), f32)
    sums = lax.fori_loop(0, rows, last, (zero, zero))
    copies.append(pltpu.make_async_copy(gp, gp_o, sem.at[6]))
    copies[-1].start()
    copies.append(pltpu.make_async_copy(bn, bn_o, sem.at[7]))
    copies[-1].start()
    for k in range(2):
        mine[k : k + 1, :] = jnp.sum(sums[k], axis=0, keepdims=True)
    wait_all_here(found)
    all_sum(mine, rest[: len(stages)], rest[len(stages) :], found)
    sums_o[...] = mine[...]
    for copy in copies:
        copy.wait()


def mixer_forward(stages, xw, cw, meta, count, sums1, scales, shifts, w_in, w_gate, w_out, kl, kd):
    band, px, channels = xw.shape
    columns = px // SUB
    rows = columns
    n = len(groups_of(channels))
    small = (rows, px, channels)
    kinds = (bf16, bf16, bf16, f32, bf16, bf16, f32, f32)
    return pl.pallas_call(
        functools.partial(mixer_kernel, stages),
        name="mixer_forward",
        out_shape=[jax.ShapeDtypeStruct(small, k) for k in kinds]
        + [jax.ShapeDtypeStruct((2, channels), f32)],
        in_specs=[VMEM] * 12,
        out_specs=[ANY] * 8 + [VMEM],
        scratch_shapes=[
            pltpu.VMEM((columns, SUB, channels), f32),
            pltpu.VMEM((25, n, SUB, LANE), f32),
            pltpu.VMEM((49, n, SUB, LANE), f32),
        ]
        + [pltpu.VMEM(small, k) for k in kinds]
        + [
            pltpu.VMEM((n, rows + 4, columns, SUB, LANE), f32),
            pltpu.VMEM((n, rows, columns, SUB, LANE), f32),
            pltpu.SemaphoreType.DMA((8,)),
        ]
        + sum_scratch(stages, (2, channels)),
        compiler_params=pltpu.CompilerParams(
            collective_id=2, has_side_effects=True, vmem_limit_bytes=56 * MIB
        ),
    )(xw, cw, meta, count, sums1, scales, shifts, w_in, w_gate, w_out, kl, kd)


def hidden_kernel(
    stages, xa, ca, bn, meta, count, sums2, scales, shifts, hshift, w_e, w_rt, kh,
    res_o, gn_o, gwe_o, gwr_o, gk_o, gh_o, sums_o,
    cm, khb, kfb, n2, gr, ha, ge, em, gc, kacc, wet, wr, mine, *rest,
):
    found = stage_peers(stages)
    say_here(found)
    rows, px, channels = xa.shape
    columns = px // SUB
    hidden = w_e.shape[1]
    wide = em.shape[0] * LANE
    parts = em.shape[0]
    wide_step = 6
    make_col_mask(meta, cm)
    spread_taps(kh, khb)
    spread_taps(kh, kfb, flip=True)
    for edge in (0, rows + 1):
        em[:, edge] = jnp.zeros(em.shape[:1] + em.shape[2:], f32)
        gc[:, edge] = jnp.zeros(gc.shape[:1] + gc.shape[2:], f32)
    wet[...] = w_e[...].astype(f32).T.astype(bf16)
    wr[...] = w_rt[...].astype(f32).T.astype(bf16)
    total = count[0:1, 0:1]
    mean, rstd = statistics(sums2, total, 0)
    scale = rstd * b8(scales, 2)

    def middle_of(r):
        return pixels3(xa[r].astype(f32)) + b8(scales, 1) * pixels3(bn[r])

    def prepare(r, acc):
        normed = (middle_of(r) - mean) * scale + b8(shifts, 6)
        n2[r] = pixels2(normed).astype(bf16)
        grad = (b8(scales, 3) * pixels3(ca[r].astype(f32))).astype(bf16)
        gr[r] = pixels2(grad)
        return acc + fold(grad.astype(f32))

    zero = jnp.zeros((SUB, channels), f32)
    grad_sum = lax.fori_loop(0, rows, prepare, zero)

    def chunk(f, _):
        base = pl.multiple_of(f * wide, wide)
        lanes = pl.ds(base, wide)
        group = f * parts

        def expand(b, _):
            tall = n2[pl.ds(b * wide_step, wide_step)].reshape(wide_step * px, channels)
            product = dot(tall, w_e[:, lanes])
            for k in range(wide_step):
                r = b * wide_step + k
                mask = row_mask(meta, cm, r)[:, :, :LANE]
                value = product[k * px : (k + 1) * px]
                value = low(value + jnp.broadcast_to(hshift[0:1, lanes], value.shape))
                for g in range(parts):
                    em[g, r + 1] = mask * pixels3(value[:, g * LANE : (g + 1) * LANE])
            return 0

        lax.fori_loop(0, rows // wide_step, expand, 0)

        def forward(r, acc):
            grad = dot(gr[r], w_rt[:, lanes])
            out = []
            for g in range(parts):
                conv = zeros_list(columns)
                for i in range(3):
                    taps = [khb[3 * i + j, group + g] for j in range(3)]
                    conv = add_row(conv, lambda c: em[g, r + i, c], taps, 1)
                here = pl.ds(pl.multiple_of(base + g * LANE, LANE), LANE)
                v = jnp.stack(conv) + jnp.broadcast_to(hshift[1:2, here], (SUB, LANE))
                phi_sum, bell = normal_parts(v)
                ha[r, :, here] = pixels2(v * phi_sum).astype(bf16)
                part = pixels3(grad[:, g * LANE : (g + 1) * LANE])
                back = low(part * (phi_sum + v * bell))
                gc[g, r + 1] = back
                out.append(acc[g] + fold(back))
            return tuple(out)

        bias = lax.fori_loop(0, rows, forward, tuple(zeros_list(parts)))
        for g in range(parts):
            here = pl.ds(pl.multiple_of(base + g * LANE, LANE), LANE)
            gh_o[1:2, here] = jnp.sum(bias[g], axis=0, keepdims=True)
            for tap in range(9):
                kacc[g, tap] = jnp.zeros((SUB, LANE), f32)

        def backward(r, acc):
            mask = row_mask(meta, cm, r)[:, :, :LANE]
            out = []
            for g in range(parts):
                conv = zeros_list(columns)
                for i in range(3):
                    taps = [kfb[3 * i + j, group + g] for j in range(3)]
                    sums = [kacc[g, 3 * i + j] for j in range(3)]
                    fixed = [em[g, r + 1, c] for c in range(columns)]
                    for c in range(columns):
                        value = gc[g, r + i, c]
                        for j in range(3):
                            at = c - (j - 1)
                            if 0 <= at < columns:
                                conv[at] = conv[at] + taps[j] * value
                                sums[j] = sums[j] + fixed[at] * value
                    for j in range(3):
                        kacc[g, 3 * i + j] = sums[j]
                here = pl.ds(pl.multiple_of(base + g * LANE, LANE), LANE)
                value = low(mask * jnp.stack(conv))
                ge[r, :, here] = pixels2(value).astype(bf16)
                out.append(acc[g] + fold(value))
            return tuple(out)

        bias = lax.fori_loop(0, rows, backward, tuple(zeros_list(parts)))
        for g in range(parts):
            here = pl.ds(pl.multiple_of(base + g * LANE, LANE), LANE)
            gh_o[0:1, here] = jnp.sum(bias[g], axis=0, keepdims=True)
            for tap in range(9):
                gk_o[8 - tap : 9 - tap, here] = jnp.sum(kacc[g, tap], axis=0, keepdims=True)
        return 0

    lax.fori_loop(0, hidden // wide, chunk, 0)

    whole = rows * px
    gwe_o[...] = dot_tn(n2[...].reshape(whole, channels), ge[...].reshape(whole, hidden))
    gwr_o[...] = dot_tn(gr[...].reshape(whole, channels), ha[...].reshape(whole, hidden))

    step = 3

    def finish(b, sums):
        sums = list(sums)
        at = pl.ds(b * step, step)
        tall = step * px
        reduced_all = dot(ha[at].reshape(tall, hidden), wr[...])
        gn_all = dot(ge[at].reshape(tall, hidden), wet[...])
        for k in range(step):
            r = b * step + k
            mask = row_mask(meta, cm, r)
            reduced = pixels3(reduced_all[k * px : (k + 1) * px]) + b8(shifts, 7)
            middle = middle_of(r)
            res_o[r] = pixels2(mask * (middle + b8(scales, 3) * reduced))
            gn = pixels3(gn_all[k * px : (k + 1) * px])
            gn_o[r] = pixels2(gn)
            hat = (middle - mean) * rstd
            out = pixels3(ca[r].astype(f32))
            sums[0] = sums[0] + fold(gn)
            sums[1] = sums[1] + fold(gn * hat)
            sums[2] = sums[2] + fold(out * reduced)
        return tuple(sums)

    sums = lax.fori_loop(0, rows // step, finish, (zero, zero, zero))
    for k, value in enumerate((sums[0], sums[1], grad_sum, sums[2])):
        mine[k : k + 1, :] = jnp.sum(value, axis=0, keepdims=True)
    wait_all_here(found)
    all_sum(mine, rest[: len(stages)], rest[len(stages) :], found)
    sums_o[...] = mine[...]


def hidden_block(stages, xa, ca, bn, meta, count, sums2, scales, shifts, hshift, w_e, w_rt, kh):
    rows, px, channels = xa.shape
    columns = px // SUB
    hidden = w_e.shape[1]
    groups = hidden // LANE
    parts = 2
    shape = jax.ShapeDtypeStruct
    return pl.pallas_call(
        functools.partial(hidden_kernel, stages),
        name="hidden_block",
        out_shape=[
            shape((rows, px, channels), f32),
            shape((rows, px, channels), f32),
            shape((channels, hidden), f32),
            shape((channels, hidden), f32),
            shape((9, hidden), f32),
            shape((2, hidden), f32),
            shape((4, channels), f32),
        ],
        in_specs=[VMEM] * 12,
        out_specs=[VMEM] * 7,
        scratch_shapes=[
            pltpu.VMEM((columns, SUB, channels), f32),
            pltpu.VMEM((9, groups, SUB, LANE), f32),
            pltpu.VMEM((9, groups, SUB, LANE), f32),
            pltpu.VMEM((rows, px, channels), bf16),
            pltpu.VMEM((rows, px, channels), bf16),
            pltpu.VMEM((rows, px, hidden), bf16),
            pltpu.VMEM((rows, px, hidden), bf16),
            pltpu.VMEM((parts, rows + 2, columns, SUB, LANE), f32),
            pltpu.VMEM((parts, rows + 2, columns, SUB, LANE), f32),
            pltpu.VMEM((parts, 9, SUB, LANE), f32),
            pltpu.VMEM((hidden, channels), bf16),
            pltpu.VMEM((hidden, channels), bf16),
        ]
        + sum_scratch(stages, (4, channels)),
        compiler_params=pltpu.CompilerParams(
            collective_id=3, has_side_effects=True, vmem_limit_bytes=60 * MIB
        ),
    )(xa, ca, bn, meta, count, sums2, scales, shifts, hshift, w_e, w_rt, kh)


def back_kernel(
    stages, gn, bn, xa, ca, gl, sl, c1, c2, gp, meta, count, sums1, sums2, sums3, scales, shifts,
    w_in, w_gate, w_out, kl, kd,
    mix_o, gwi_o, gwg_o, gwo_o, gkl_o, gkd_o, sums_o,
    cm, klb, kdb, gb, gg, gt, gm, tt, g2, g1, src, mine, *rest,
):
    found = stage_peers(stages)
    say_here(found)
    rows, px, channels = xa.shape
    columns = px // SUB
    groups = groups_of(channels)
    make_col_mask(meta, cm)
    spread_taps(kl, klb, flip=True)
    spread_taps(kd, kdb, flip=True)
    for edge in (0, 1, rows + 2, rows + 3):
        g1[:, edge] = jnp.zeros(g1.shape[:1] + g1.shape[2:], f32)
    total = count[0:1, 0:1]
    mean1, rstd1 = statistics(sums1, total, 0)
    scale1 = rstd1 * b8(scales, 0)
    mean2, rstd2 = statistics(sums2, total, 0)
    scale2 = rstd2 * b8(scales, 2)
    back0 = b8(sums3, 0) / total
    back1 = b8(sums3, 1) / total
    zero = jnp.zeros((SUB, channels), f32)

    def first(r, sums):
        mask = row_mask(meta, cm, r)
        both = pixels3(bn[r])
        middle = pixels3(xa[r].astype(f32)) + b8(scales, 1) * both
        hat = (middle - mean2) * rstd2
        grad = pixels3(ca[r].astype(f32)) + scale2 * (
            pixels3(gn[r]) - mask * (back0 + hat * back1)
        )
        gm[r] = pixels2(grad)
        branch = (b8(scales, 1) * grad).astype(bf16)
        gb[r] = pixels2(branch)
        gated_grad = dot_nt(pixels2(branch), w_out[...])
        gelu = gl[r].astype(f32)
        gate_grad = (gated_grad * gelu).astype(bf16)
        gg[r] = gate_grad
        gt[r] = (gelu * gp[r]).astype(bf16)
        tt[r] = gated_grad * gp[r]
        conv = low(dot_nt(gate_grad, w_gate[...]))
        for g, width in groups:
            g2[g, r, :, :, :width] = pixels3(conv[:, g * LANE : g * LANE + width])
            src[g, r, :, :, :width] = pixels3(c1[r, :, g * LANE : g * LANE + width].astype(f32))
        return (
            sums[0] + fold(grad * both),
            sums[1] + fold(branch.astype(f32)),
            sums[2] + fold(pixels3(gate_grad.astype(f32))),
            sums[3] + fold(pixels3(conv)),
        )

    sums = lax.fori_loop(0, rows, first, (zero,) * 4)
    for k in range(4):
        mine[2 + k : 3 + k, :] = jnp.sum(sums[k], axis=0, keepdims=True)
    whole = rows * px
    flat = lambda ref: ref[...].reshape(whole, channels)
    gwo_o[...] = dot_tn(flat(gt), flat(gb))
    gwg_o[...] = dot_tn(flat(c2), flat(gg))

    for g, width in groups:
        for i in range(7):
            first_row = max(0, 3 * (3 - i))
            last_row = min(rows, rows - 3 * (i - 3))

            def taps_row(r, acc, g=g, i=i):
                at = r + (i - 3) * 3
                return tap_sums(
                    list(acc), (lambda c: g2[g, r, c], columns), lambda c: src[g, at, c], 3
                )

            acc = lax.fori_loop(first_row, last_row, taps_row, zeros_list(7))
            for j in range(7):
                row = jnp.sum(acc[j], axis=0, keepdims=True)
                gkd_o[7 * i + j : 7 * i + j + 1, g * LANE : g * LANE + width] = row[:, :width]

    def dilated(r, sums):
        mask = row_mask(meta, cm, r)
        low_i, high_i = row_range(r, rows, 3, 3)
        out = []
        for g, width in groups:

            def tap_row(i, acc):
                taps = [kdb[7 * i + j, g] for j in range(7)]
                at = r + (i - 3) * 3
                return add_row(list(acc), lambda c: g2[g, at, c], taps, 3)

            acc = lax.fori_loop(low_i, high_i, tap_row, zeros_list(columns))
            value = low(mask[:, :, :width] * jnp.stack(acc)[:, :, :width])
            g1[g, r + 2, :, :, :width] = value
            out.append(sums[g] + fold(value))
        return tuple(out)

    start = tuple(jnp.zeros((SUB, width), f32) for g, width in groups)
    sums = lax.fori_loop(0, rows, dilated, start)
    for g, width in groups:
        mine[6:7, g * LANE : g * LANE + width] = jnp.sum(sums[g], axis=0, keepdims=True)

    def refill(r, _):
        for g, width in groups:
            src[g, r, :, :, :width] = pixels3(gl[r, :, g * LANE : g * LANE + width].astype(f32))
        return 0

    lax.fori_loop(0, rows, refill, 0)

    for g, width in groups:
        for i in range(5):

            def taps_row(r, acc, g=g, i=i):
                return tap_sums(
                    list(acc), (lambda c: src[g, r, c], columns), lambda c: g1[g, r + i, c], 1
                )

            acc = lax.fori_loop(0, rows, taps_row, zeros_list(5))
            for j in range(5):
                tap = 24 - (5 * i + j)
                row = jnp.sum(acc[j], axis=0, keepdims=True)
                gkl_o[tap : tap + 1, g * LANE : g * LANE + width] = row[:, :width]

    def local(r, sums):
        mask = row_mask(meta, cm, r)
        parts = []
        for g, width in groups:
            acc = zeros_list(columns)
            for i in range(5):
                taps = [klb[5 * i + j, g] for j in range(5)]
                acc = add_row(acc, lambda c: g1[g, r + i, c], taps, 1)
            value = mask[:, :, :width] * jnp.stack(acc)[:, :, :width]
            at = slice(g * LANE, g * LANE + width)
            grad = (tt[r, :, at] + pixels2(value)) * sl[r, :, at]
            gg[r, :, at] = grad.astype(bf16)
            parts.append(sums[g] + fold(pixels3(low(grad))))
        return tuple(parts)

    sums = lax.fori_loop(0, rows, local, start)
    for g, width in groups:
        mine[7:8, g * LANE : g * LANE + width] = jnp.sum(sums[g], axis=0, keepdims=True)

    def last(r, sums):
        x = pixels3(xa[r].astype(f32))
        grad = pixels3(gm[r])
        gn1 = pixels3(dot_nt(gg[r], w_in[...])) + b8(scales, 1) * grad
        mix_o[r] = pixels2(grad + scale1 * gn1)
        hat = (x - mean1) * rstd1
        normed = (x - mean1) * scale1 + b8(shifts, 0)
        gb[r] = pixels2(normed).astype(bf16)
        return sums[0] + fold(gn1), sums[1] + fold(gn1 * hat)

    sums = lax.fori_loop(0, rows, last, (zero, zero))
    for k in range(2):
        mine[k : k + 1, :] = jnp.sum(sums[k], axis=0, keepdims=True)
    wait_all_here(found)
    all_sum(mine, rest[: len(stages)], rest[len(stages) :], found)
    sums_o[...] = mine[...]
    gwi_o[...] = dot_tn(flat(gb), flat(gg))


def mixer_back(stages, gn, bn, xa, ca, gl, sl, c1, c2, gp, meta, count, sums1, sums2, sums3, scales,
               shifts, w_in, w_gate, w_out, kl, kd):
    rows, px, channels = xa.shape
    columns = px // SUB
    n = len(groups_of(channels))
    small = (rows, px, channels)
    shape = jax.ShapeDtypeStruct
    square = shape((channels, channels), f32)
    return pl.pallas_call(
        functools.partial(back_kernel, stages),
        name="mixer_back",
        out_shape=[
            shape(small, f32), square, square, square,
            shape((25, channels), f32), shape((49, channels), f32), shape((8, channels), f32),
        ],
        in_specs=[VMEM] * 21,
        out_specs=[VMEM] * 7,
        scratch_shapes=[
            pltpu.VMEM((columns, SUB, channels), f32),
            pltpu.VMEM((25, n, SUB, LANE), f32),
            pltpu.VMEM((49, n, SUB, LANE), f32),
            pltpu.VMEM(small, bf16),
            pltpu.VMEM(small, bf16),
            pltpu.VMEM(small, bf16),
            pltpu.VMEM(small, f32),
            pltpu.VMEM(small, f32),
            pltpu.VMEM((n, rows, columns, SUB, LANE), f32),
            pltpu.VMEM((n, rows + 4, columns, SUB, LANE), f32),
            pltpu.VMEM((n, rows, columns, SUB, LANE), f32),
        ]
        + sum_scratch(stages, (8, channels)),
        compiler_params=pltpu.CompilerParams(
            collective_id=4, has_side_effects=True, vmem_limit_bytes=62 * MIB
        ),
    )(gn, bn, xa, ca, gl, sl, c1, c2, gp, meta, count, sums1, sums2, sums3, scales, shifts,
      w_in, w_gate, w_out, kl, kd)


def input_kernel(mix, xa, meta, count, sums1, sums4, scales, out, cm, al):
    rows, px, channels = xa.shape
    make_col_mask(meta, cm)
    total = count[0:1, 0:1]
    mean1, rstd1 = statistics(sums1, total, 0)
    scale1 = rstd1 * b8(scales, 0)
    back0 = b8(sums4, 0) / total
    back1 = b8(sums4, 1) / total

    def one(r, _):
        mask = row_mask(meta, cm, r)
        hat = (pixels3(xa[r].astype(f32)) - mean1) * rstd1
        grad = mask * (pixels3(mix[r]) - scale1 * (back0 + hat * back1))
        al[r] = pixels2(grad)
        return 0

    lax.fori_loop(0, rows, one, 0)
    unalign(al, meta, out)


def unalign(al, meta, out):
    rows, px, channels = al.shape
    offsets = out.shape[0] - rows + 1
    for at in range(out.shape[0]):
        value = jnp.zeros((px // SUB, SUB, channels), f32)
        for t in range(offsets):
            if 0 <= at - t < rows:
                chosen = (meta[0] == float(t))[None]
                value = jnp.where(chosen, pixels3(al[at - t]), value)
        out[at] = pixels2(value)


def input_grad_kernel(mix, xa, meta, count, sums1, sums4, scales, band):
    rows, px, channels = xa.shape
    return pl.pallas_call(
        input_kernel,
        name="input_grad",
        out_shape=jax.ShapeDtypeStruct((band, px, channels), f32),
        in_specs=[VMEM] * 7,
        out_specs=VMEM,
        scratch_shapes=[
            pltpu.VMEM((px // SUB, SUB, channels), f32),
            pltpu.VMEM((rows, px, channels), f32),
        ],
        compiler_params=pltpu.CompilerParams(vmem_limit_bytes=56 * MIB),
    )(mix, xa, meta, count, sums1, sums4, scales)


def unalign_kernel(res, meta, out):
    unalign(res, meta, out)


def unaligned(res, meta, band):
    rows, px, channels = res.shape
    return pl.pallas_call(
        unalign_kernel,
        name="unalign",
        out_shape=jax.ShapeDtypeStruct((band, px, channels), f32),
        in_specs=[VMEM] * 2,
        out_specs=VMEM,
        compiler_params=pltpu.CompilerParams(vmem_limit_bytes=56 * MIB),
    )(res, meta)


def tile_plan(shapes):
    plan, base = [], 0
    for rows, width in shapes:
        blocks = pl.cdiv(rows, SUB)
        plan.append((base, rows, groups_of(width)))
        base += blocks * pl.cdiv(width, LANE)
    return plan, base


def tiles_in(refs, plan, buf):
    for ref, (base, rows, groups) in zip(refs, plan):
        n, full = len(groups), rows // SUB

        def block(b, _, ref=ref, base=base, groups=groups, n=n):
            at = pl.ds(pl.multiple_of(b * SUB, SUB), SUB)
            for g, width in groups:
                buf[base + b * n + g, :, :width] = ref[at, g * LANE : g * LANE + width]
            return 0

        lax.fori_loop(0, full, block, 0)
        if rows % SUB:
            for g, width in groups:
                buf[base + full * n + g, : rows % SUB, :width] = ref[
                    full * SUB :, g * LANE : g * LANE + width
                ]


def tiles_out(refs, plan, buf):
    for ref, (base, rows, groups) in zip(refs, plan):
        n, full = len(groups), rows // SUB

        def block(b, _, ref=ref, base=base, groups=groups, n=n):
            at = pl.ds(pl.multiple_of(b * SUB, SUB), SUB)
            for g, width in groups:
                ref[at, g * LANE : g * LANE + width] = buf[base + b * n + g, :, :width]
            return 0

        lax.fori_loop(0, full, block, 0)
        if rows % SUB:
            for g, width in groups:
                ref[full * SUB :, g * LANE : g * LANE + width] = buf[
                    base + full * n + g, : rows % SUB, :width
                ]


def grads_kernel(stages, plan, *refs):
    count = len(plan)
    ins, outs, (buf, full, *rest) = refs[:count], refs[count : 2 * count], refs[2 * count :]
    slots, sems = rest[: len(stages)], rest[len(stages) :]
    found = stage_peers(stages)

    def clear(t, _):
        buf[t] = jnp.zeros((SUB, LANE), f32)
        return 0

    lax.fori_loop(0, buf.shape[0], clear, 0)
    tiles_in(ins, plan, buf)
    greet(found)
    start, length, steps = 0, buf.shape[0], []
    for k, (place, peers) in enumerate(found):
        share = length // stages[k][2]
        send, recv = sems[4 * k : 4 * k + 2]
        copies = []
        for step, other, device in peers:
            src = buf.at[pl.ds(start + other * share, share)]
            copies.append(
                remote(src, slots[k].at[step - 1], send.at[step - 1], recv.at[step - 1], device)
            )
            copies[-1].start()
        for copy in copies:
            copy.wait()
        start, length = start + place * share, share

        def add(t, _, start=start, k=k, n=len(peers)):
            total = buf[start + t]
            for i in range(n):
                total = total + slots[k][i, t]
            buf[start + t] = total
            return 0

        lax.fori_loop(0, length, add, 0)
        steps.append((start, length))

    def settle(t, _):
        full[start + t] = buf[start + t]
        return 0

    lax.fori_loop(0, length, settle, 0)
    for k in reversed(range(len(stages))):
        start, length = steps[k]
        send, recv = sems[4 * k + 2 : 4 * k + 4]
        copies = []
        for step, other, device in found[k][1]:
            here = full.at[pl.ds(start, length)]
            copies.append(remote(here, here, send.at[step - 1], recv.at[step - 1], device))
            copies[-1].start()
        for copy in copies:
            copy.wait()
    tiles_out(outs, plan, full)


def sum_grads(arrays, stages, collective_id):
    devices = math.prod(size for _, _, size in stages)
    plan, tiles = tile_plan([a.shape for a in arrays])
    tiles = pl.cdiv(tiles, devices) * devices
    slots, sems, length = [], [], tiles
    for _, _, size in stages:
        length //= size
        slots.append(pltpu.VMEM((size - 1, length, SUB, LANE), f32))
        sems += [pltpu.SemaphoreType.DMA((size - 1,))] * 4
    return pl.pallas_call(
        functools.partial(grads_kernel, stages, plan),
        name="sum_grads",
        out_shape=[jax.ShapeDtypeStruct(a.shape, f32) for a in arrays],
        in_specs=[VMEM] * len(arrays),
        out_specs=[VMEM] * len(arrays),
        scratch_shapes=[pltpu.VMEM((tiles, SUB, LANE), f32)] * 2 + slots + sems,
        compiler_params=pltpu.CompilerParams(
            collective_id=collective_id, has_side_effects=True, vmem_limit_bytes=48 * MIB
        ),
    )(*arrays)


def halves(values, core, half, axis):
    mine = lax.dynamic_slice_in_dim(values, core * half, half, axis=axis)
    other = lax.dynamic_slice_in_dim(values, (1 - core) * half, half, axis=axis)
    return mine, lax.ppermute(other, "rows", [(0, 1), (1, 0)])


def first_sums_kernel(x, meta, out, cm):
    rows, columns, images, channels = x.shape
    size, top = meta[2], meta[0]
    for c in range(columns):
        cm[c] = (size > c).astype(f32)

    def one(r, sums):
        at = (r * 1).astype(f32)
        inside = ((at >= top) & (at < top + size)).astype(f32)
        value = cm[...] * inside[None] * x[r].astype(f32)
        return sums[0] + fold(value), sums[1] + fold(value * value)

    zero = jnp.zeros((images, channels), f32)
    sums = lax.fori_loop(0, rows, one, (zero, zero))
    for k in range(2):
        out[k] = sums[k][:SUB] + sums[k][SUB:]


def first_sums(x, meta):
    rows, columns, images, channels = x.shape
    return pl.pallas_call(
        first_sums_kernel,
        name="first_sums",
        out_shape=jax.ShapeDtypeStruct((2, SUB, channels), f32),
        in_specs=[VMEM] * 2,
        out_specs=VMEM,
        scratch_shapes=[pltpu.VMEM((columns, images, channels), f32)],
        compiler_params=pltpu.CompilerParams(vmem_limit_bytes=32 * MIB),
    )(x, meta)


def on_device(sizes, inputs, cotangent, scales, shifts, hidden_shift, w_inward, w_gating,
              w_outward, w_expand, w_reduce, kernel_local, kernel_dilated, kernel_hidden,
              image_size, band_split, slot_image):
    images, band, columns, channels = inputs.shape
    half = images // 2
    px = columns * half
    core = lax.axis_index("rows")
    counted = jnp.sum(image_size * image_size).astype(f32)
    count = jnp.full((SUB, LANE), counted)
    everyone = jnp.arange(image_size.shape[0], dtype=jnp.int32)
    chosen = (slot_image[:, None] == everyone[None, :]).astype(jnp.int32)
    extent = jnp.sum(chosen * image_size[None, :], axis=1)
    top = band - jnp.sum(chosen * band_split[None, :], axis=1)
    start = jnp.clip(top, 0, 2 * band - columns)
    own_meta = jnp.stack([top - core * band, top, extent]).astype(f32)
    own_meta = jnp.broadcast_to(own_meta[:, :, None], (3, images, channels))
    meta = jnp.stack([start, top - start, extent]).astype(f32)
    meta = lax.dynamic_slice_in_dim(meta, core * half, half, axis=1)
    meta = jnp.broadcast_to(meta[:, :, None], (3, half, channels))

    x = jnp.transpose(inputs, (1, 2, 0, 3))
    y = jnp.transpose(cotangent, (1, 2, 0, 3))
    stages = stage_list(sizes)
    sums1 = reduce_all(first_sums(x, own_meta), stages, 1)

    def gather_rows(v):
        mine, theirs = halves(v, core, half, 2)
        upper = jnp.where(core == 0, mine, theirs)
        lower = jnp.where(core == 0, theirs, mine)
        return jnp.concatenate([upper, lower], axis=0).reshape(2 * band, px, channels)

    xw, cw = gather_rows(x), gather_rows(y)
    xa, ca, gl, sl, c1, c2, gp, bn, sums2 = mixer_forward(
        stages, xw, cw, meta, count, sums1, scales, shifts, w_inward, w_gating, w_outward,
        kernel_local, kernel_dilated,
    )
    res, gn, gwe, gwr, gk, gh, sums3 = hidden_block(
        stages, xa, ca, bn, meta, count, sums2, scales, shifts, hidden_shift, w_expand, w_reduce.T,
        kernel_hidden,
    )
    mix, gwi, gwg, gwo, gkl, gkd, sums4 = mixer_back(
        stages, gn, bn, xa, ca, gl, sl, c1, c2, gp, meta, count, sums1, sums2, sums3, scales, shifts,
        w_inward, w_gating, w_outward, kernel_local, kernel_dilated,
    )

    def scatter_rows(v):
        v = v.reshape(2 * band, columns, half, channels)
        mine = lax.dynamic_slice_in_dim(v, core * band, band, axis=0)
        other = lax.dynamic_slice_in_dim(v, (1 - core) * band, band, axis=0)
        theirs = lax.ppermute(other, "rows", [(0, 1), (1, 0)])
        lower = jnp.where(core == 0, mine, theirs)
        upper = jnp.where(core == 0, theirs, mine)
        both = jnp.concatenate([lower, upper], axis=2)
        return jnp.transpose(both, (2, 0, 1, 3))

    result = scatter_rows(unaligned(res, meta, 2 * band))
    input_grad = scatter_rows(
        input_grad_kernel(mix, xa, meta, count, sums1, sums4, scales, 2 * band)
    )
    gwe, gwr, gk, gh, gwi, gwg, gwo, gkl, gkd = sum_grads(
        (gwe, gwr, gk, gh, gwi, gwg, gwo, gkl, gkd), stages, 5
    )
    scales_grad = jnp.stack([sums4[1], sums4[2], sums3[1], sums3[3]])
    shifts_grad = jnp.stack(
        [sums4[0], sums4[7], sums4[6], sums4[5], sums4[4], sums4[3], sums3[0], sums3[2]]
    )
    return (
        result, input_grad, scales_grad, shifts_grad, gh, gwi, gwg, gwo, gwe, gwr.T,
        gkl, gkd, gk,
    )


def solution(mesh):
    wide = P("imgs", "rows", None, None)
    sizes = dict(mesh.shape)
    return jax.shard_map(
        functools.partial(on_device, sizes),
        mesh=mesh,
        in_specs=(wide, wide) + (P(),) * 13 + (P("imgs"),),
        out_specs=(wide, wide) + (P(),) * 11,
        check_vma=False,
    )
```

```python
import functools
import math

import jax
import jax.numpy as jnp
from jax import lax
from jax.experimental import pallas as pl
from jax.experimental.pallas import tpu as pltpu
from jax.sharding import PartitionSpec as P

MESH = pl.DeviceIdType.MESH
epsilon = 1e-05
bf16 = jnp.bfloat16
f32 = jnp.float32
SUB = 8
LANE = 128
MIB = 1 << 20
ANY = pl.BlockSpec(memory_space=pl.ANY)
VMEM = pl.BlockSpec(memory_space=pltpu.VMEM)


def low(values):
    return values.astype(bf16).astype(f32)


def normal_parts(v):
    bell = jnp.exp(-0.5 * (v * v))
    base = 1.0 + (0.3275911 * 0.7071067811865476) * jnp.abs(v)
    t = pl.reciprocal(base, approx=True)
    t = t * (2.0 - base * t)
    poly = 0.5 * 1.061405429
    for coef in (-1.453152027, 1.421413741, -0.284496736, 0.254829592):
        poly = poly * t + 0.5 * coef
    tail = poly * t * bell
    return jnp.where(v >= 0, 1.0 - tail, tail), bell * 0.3989422804014327


def dot(a, b):
    return jnp.dot(a, b, preferred_element_type=f32)


def dot_nt(a, b):
    return lax.dot_general(a, b, (((1,), (1,)), ((), ())), preferred_element_type=f32)


def dot_tn(a, b):
    return lax.dot_general(a, b, (((0,), (0,)), ((), ())), preferred_element_type=f32)


def groups_of(channels):
    return [(g, min(LANE, channels - g * LANE)) for g in range(pl.cdiv(channels, LANE))]


def spread_taps(k_ref, kb, flip=False):
    count, channels = k_ref.shape
    for tap in range(count):
        from_tap = count - 1 - tap if flip else tap
        row = jnp.broadcast_to(k_ref[from_tap : from_tap + 1, :], (SUB, channels))
        for g, width in groups_of(channels):
            kb[tap, g, :, :width] = row[:, g * LANE : g * LANE + width]


def add_row(acc, load, taps, dilation):
    columns, half = len(acc), len(taps) // 2
    for c in range(columns):
        value = load(c)
        for j, tap in enumerate(taps):
            at = c - (j - half) * dilation
            if 0 <= at < columns:
                acc[at] = acc[at] + tap * value
    return acc


def tap_sums(acc, load_fixed, load_moved, dilation):
    columns, half = load_fixed[1], len(acc) // 2
    fixed = [load_fixed[0](c) for c in range(columns)]
    for c in range(columns):
        value = load_moved(c)
        for j in range(len(acc)):
            at = c - (j - half) * dilation
            if 0 <= at < columns:
                acc[j] = acc[j] + fixed[at] * value
    return acc


def row_range(r, rows, half, dilation):
    low_i = jnp.maximum(half - r // dilation, 0)
    high_i = jnp.minimum(half + (rows - 1 - r) // dilation, 2 * half)
    return low_i, high_i + 1


def zeros_list(count):
    return [jnp.zeros((SUB, LANE), f32) for _ in range(count)]


def b8(ref, i):
    return jnp.broadcast_to(ref[i : i + 1, :], (SUB, ref.shape[1]))


def make_col_mask(meta, cm):
    size = meta[2]
    for c in range(cm.shape[0]):
        cm[c] = (size > c).astype(f32)


def row_mask(meta, cm, r):
    at = (r * 1).astype(f32)
    inside = (at >= meta[1]) & (at < meta[1] + meta[2])
    return cm[...] * inside.astype(f32)[None]


def pixels3(values):
    return values.reshape(values.shape[0] // SUB, SUB, values.shape[1])


def pixels2(values):
    return values.reshape(values.shape[0] * SUB, values.shape[2])


def fold(values):
    return jnp.sum(values, axis=0)


def statistics(sums, count, i):
    mean = b8(sums, i) / count
    return mean, lax.rsqrt(b8(sums, i + 1) / count - mean * mean + epsilon)


def stage_list(sizes):
    stages = [("rows", 1, sizes["rows"])]
    left, stride = sizes["imgs"], 1
    while left > 1:
        size = 4 if left % 4 == 0 else (2 if left % 2 == 0 else left)
        stages.append(("imgs", stride, size))
        left, stride = left // size, stride * size
    return [s for s in stages if s[2] > 1]


def stage_peers(stages):
    core = lax.axis_index("rows")
    chip = lax.axis_index("imgs")
    found = []
    for axis, stride, size in stages:
        index = core if axis == "rows" else chip
        place = lax.rem(index // stride, size)
        peers = []
        for step in range(1, size):
            other = lax.rem(place + step, size)
            at = index + (other - place) * stride
            peers.append((step, other, (at, chip) if axis == "rows" else (core, at)))
        found.append((place, peers))
    return found


def say_here(found):
    barrier = pltpu.get_barrier_semaphore()
    for _, peers in found:
        for _, _, device in peers:
            pl.semaphore_signal(barrier, inc=1, device_id=device, device_id_type=MESH)


def wait_all_here(found):
    pl.semaphore_wait(pltpu.get_barrier_semaphore(), sum(len(peers) for _, peers in found))


def greet(found):
    say_here(found)
    wait_all_here(found)


def remote(src, dst, send, recv, device):
    return pltpu.make_async_remote_copy(
        src_ref=src, dst_ref=dst, send_sem=send, recv_sem=recv,
        device_id=device, device_id_type=MESH,
    )


def all_sum(mine, slots, sems, found):
    for k, (_, peers) in enumerate(found):
        slot, (send, recv) = slots[k], sems[2 * k : 2 * k + 2]
        copies = []
        for step, _, device in peers:
            copies.append(
                remote(mine, slot.at[step - 1], send.at[step - 1], recv.at[step - 1], device)
            )
            copies[-1].start()
        for copy in copies:
            copy.wait()
        total = mine[...]
        for step, _, _ in peers:
            total = total + slot[step - 1]
        mine[...] = total


def sum_scratch(stages, table):
    sems = []
    for _, _, size in stages:
        sems += [pltpu.SemaphoreType.DMA((size - 1,))] * 2
    slots = [pltpu.VMEM((size - 1,) + table, f32) for _, _, size in stages]
    return [pltpu.VMEM(table, f32)] + slots + sems


def reduce_kernel(stages, v_ref, out_ref, mine, *rest):
    found = stage_peers(stages)
    greet(found)
    mine[...] = jnp.sum(v_ref[...], axis=1)
    all_sum(mine, rest[: len(stages)], rest[len(stages) :], found)
    out_ref[...] = mine[...]


def reduce_all(v, stages, collective_id):
    k, _, channels = v.shape
    table = (k, channels)
    return pl.pallas_call(
        functools.partial(reduce_kernel, stages),
        name="reduce_all",
        out_shape=jax.ShapeDtypeStruct(table, f32),
        in_specs=[VMEM],
        out_specs=VMEM,
        scratch_shapes=sum_scratch(stages, table),
        compiler_params=pltpu.CompilerParams(collective_id=collective_id, has_side_effects=True),
    )(v)


def mixer_kernel(
    stages, xw, cw, meta, count, sums1, scales, shifts, w_in, w_gate, w_out, kl, kd,
    xa_o, ca_o, gl_o, sl_o, c1_o, c2_o, gp_o, bn_o, sums_o,
    cm, klb, kdb, xa, ca, gl, sl, c1, c2, gp, bn, gf, c1f, sem, mine, *rest,
):
    found = stage_peers(stages)
    say_here(found)
    rows, px, channels = xa.shape
    columns = px // SUB
    groups = groups_of(channels)
    offsets = xw.shape[0] - rows + 1
    make_col_mask(meta, cm)
    spread_taps(kl, klb)
    spread_taps(kd, kdb)
    for edge in (0, 1, rows + 2, rows + 3):
        gf[:, edge] = jnp.zeros(gf.shape[:1] + gf.shape[2:], f32)
    total = count[0:1, 0:1]
    mean, rstd = statistics(sums1, total, 0)
    scale = rstd * b8(scales, 0)
    starts = [meta[0] == float(t) for t in range(offsets)]

    def aligned(ref, r):
        value = pixels3(ref[r].astype(f32))
        for t in range(1, offsets):
            value = jnp.where(starts[t][None], pixels3(ref[r + t].astype(f32)), value)
        return value

    def first(r, _):
        mask = row_mask(meta, cm, r)
        x = mask * aligned(xw, r)
        xa[r] = pixels2(x).astype(bf16)
        ca[r] = pixels2(mask * aligned(cw, r)).astype(bf16)
        normed = pixels2((x - mean) * scale + b8(shifts, 0)).astype(bf16)
        pre = pixels3(dot(normed, w_in[...])) + b8(shifts, 1)
        phi_sum, bell = normal_parts(pre)
        gelu = mask * low(pre * phi_sum)
        sl[r] = pixels2(phi_sum + pre * bell)
        gl[r] = pixels2(gelu).astype(bf16)
        for g, width in groups:
            gf[g, r + 2, :, :, :width] = gelu[:, :, g * LANE : g * LANE + width]
        return 0

    lax.fori_loop(0, rows, first, 0)
    early = [(xa, xa_o), (ca, ca_o), (gl, gl_o), (sl, sl_o)]
    copies = [pltpu.make_async_copy(a, b, sem.at[k]) for k, (a, b) in enumerate(early)]
    for copy in copies:
        copy.start()

    def local(r, _):
        mask = row_mask(meta, cm, r)
        for g, width in groups:
            acc = zeros_list(columns)
            for i in range(5):
                taps = [klb[5 * i + j, g] for j in range(5)]
                acc = add_row(acc, lambda c: gf[g, r + i, c], taps, 1)
            bias = b8(shifts, 2)[:, g * LANE : g * LANE + width]
            value = jnp.stack(acc)[:, :, :width] + bias
            value = mask[:, :, :width] * low(value)
            c1f[g, r, :, :, :width] = value
            c1[r, :, g * LANE : g * LANE + width] = pixels2(value).astype(bf16)
        return 0

    lax.fori_loop(0, rows, local, 0)
    copies.append(pltpu.make_async_copy(c1, c1_o, sem.at[4]))
    copies[-1].start()

    def dilated(r, _):
        low_i, high_i = row_range(r, rows, 3, 3)
        for g, width in groups:

            def tap_row(i, acc):
                taps = [kdb[7 * i + j, g] for j in range(7)]
                at = r + (i - 3) * 3
                return add_row(list(acc), lambda c: c1f[g, at, c], taps, 3)

            acc = lax.fori_loop(low_i, high_i, tap_row, zeros_list(columns))
            bias = b8(shifts, 3)[:, g * LANE : g * LANE + width]
            value = jnp.stack(acc)[:, :, :width] + bias
            c2[r, :, g * LANE : g * LANE + width] = pixels2(value).astype(bf16)
        return 0

    lax.fori_loop(0, rows, dilated, 0)
    copies.append(pltpu.make_async_copy(c2, c2_o, sem.at[5]))
    copies[-1].start()

    def last(r, sums):
        mask = row_mask(meta, cm, r)
        gate = dot(c2[r], w_gate[...]) + jnp.broadcast_to(shifts[4:5, :], (px, channels))
        gp[r] = gate
        gated = (gl[r].astype(f32) * gate).astype(bf16)
        branch = dot(gated, w_out[...])
        x = pixels3(xa[r].astype(f32))
        normed = low((x - mean) * scale + b8(shifts, 0))
        both = pixels3(branch) + b8(shifts, 5) + normed
        bn[r] = pixels2(both)
        middle = mask * (x + b8(scales, 1) * both)
        return sums[0] + fold(middle), sums[1] + fold(middle * middle)

    zero = jnp.zeros((SUB, channels), f32)
    sums = lax.fori_loop(0, rows, last, (zero, zero))
    copies.append(pltpu.make_async_copy(gp, gp_o, sem.at[6]))
    copies[-1].start()
    copies.append(pltpu.make_async_copy(bn, bn_o, sem.at[7]))
    copies[-1].start()
    for k in range(2):
        mine[k : k + 1, :] = jnp.sum(sums[k], axis=0, keepdims=True)
    wait_all_here(found)
    all_sum(mine, rest[: len(stages)], rest[len(stages) :], found)
    sums_o[...] = mine[...]
    for copy in copies:
        copy.wait()


def mixer_forward(stages, xw, cw, meta, count, sums1, scales, shifts, w_in, w_gate, w_out, kl, kd):
    band, px, channels = xw.shape
    columns = px // SUB
    rows = columns
    n = len(groups_of(channels))
    small = (rows, px, channels)
    kinds = (bf16, bf16, bf16, f32, bf16, bf16, f32, f32)
    return pl.pallas_call(
        functools.partial(mixer_kernel, stages),
        name="mixer_forward",
        out_shape=[jax.ShapeDtypeStruct(small, k) for k in kinds]
        + [jax.ShapeDtypeStruct((2, channels), f32)],
        in_specs=[VMEM] * 12,
        out_specs=[ANY] * 8 + [VMEM],
        scratch_shapes=[
            pltpu.VMEM((columns, SUB, channels), f32),
            pltpu.VMEM((25, n, SUB, LANE), f32),
            pltpu.VMEM((49, n, SUB, LANE), f32),
        ]
        + [pltpu.VMEM(small, k) for k in kinds]
        + [
            pltpu.VMEM((n, rows + 4, columns, SUB, LANE), f32),
            pltpu.VMEM((n, rows, columns, SUB, LANE), f32),
            pltpu.SemaphoreType.DMA((8,)),
        ]
        + sum_scratch(stages, (2, channels)),
        compiler_params=pltpu.CompilerParams(
            collective_id=2, has_side_effects=True, vmem_limit_bytes=56 * MIB
        ),
    )(xw, cw, meta, count, sums1, scales, shifts, w_in, w_gate, w_out, kl, kd)


def hidden_kernel(
    stages, xa, ca, bn, meta, count, sums2, scales, shifts, hshift, w_e, w_rt, kh,
    nat_o, gn_o, tiles_o, sums_o,
    cm, khb, kfb, n2, gr, ha, ge, em, gc, kacc, wet, wr, res, nat, gn_s, tiles, sem, mine, *rest,
):
    found = stage_peers(stages)
    say_here(found)
    rows, px, channels = xa.shape
    columns = px // SUB
    hidden = w_e.shape[1]
    wide = em.shape[0] * LANE
    parts = em.shape[0]
    wide_step = 6
    groups = hidden // LANE
    tap_tile, bias_tile, last_tile = hidden_tiles(channels, hidden)
    for t in range(tap_tile, last_tile):
        tiles[t] = jnp.zeros((SUB, LANE), f32)
    make_col_mask(meta, cm)
    spread_taps(kh, khb)
    spread_taps(kh, kfb, flip=True)
    for edge in (0, rows + 1):
        em[:, edge] = jnp.zeros(em.shape[:1] + em.shape[2:], f32)
        gc[:, edge] = jnp.zeros(gc.shape[:1] + gc.shape[2:], f32)
    wet[...] = w_e[...].astype(f32).T.astype(bf16)
    wr[...] = w_rt[...].astype(f32).T.astype(bf16)
    total = count[0:1, 0:1]
    mean, rstd = statistics(sums2, total, 0)
    scale = rstd * b8(scales, 2)

    def middle_of(r):
        return pixels3(xa[r].astype(f32)) + b8(scales, 1) * pixels3(bn[r])

    def prepare(r, acc):
        normed = (middle_of(r) - mean) * scale + b8(shifts, 6)
        n2[r] = pixels2(normed).astype(bf16)
        grad = (b8(scales, 3) * pixels3(ca[r].astype(f32))).astype(bf16)
        gr[r] = pixels2(grad)
        return acc + fold(grad.astype(f32))

    zero = jnp.zeros((SUB, channels), f32)
    grad_sum = lax.fori_loop(0, rows, prepare, zero)

    def chunk(f, _):
        base = pl.multiple_of(f * wide, wide)
        lanes = pl.ds(base, wide)
        group = f * parts

        def expand(b, _):
            tall = n2[pl.ds(b * wide_step, wide_step)].reshape(wide_step * px, channels)
            product = dot(tall, w_e[:, lanes])
            for k in range(wide_step):
                r = b * wide_step + k
                mask = row_mask(meta, cm, r)[:, :, :LANE]
                value = product[k * px : (k + 1) * px]
                value = low(value + jnp.broadcast_to(hshift[0:1, lanes], value.shape))
                for g in range(parts):
                    em[g, r + 1] = mask * pixels3(value[:, g * LANE : (g + 1) * LANE])
            return 0

        lax.fori_loop(0, rows // wide_step, expand, 0)

        def forward(r, acc):
            grad = dot(gr[r], w_rt[:, lanes])
            out = []
            for g in range(parts):
                conv = zeros_list(columns)
                for i in range(3):
                    taps = [khb[3 * i + j, group + g] for j in range(3)]
                    conv = add_row(conv, lambda c: em[g, r + i, c], taps, 1)
                here = pl.ds(pl.multiple_of(base + g * LANE, LANE), LANE)
                v = jnp.stack(conv) + jnp.broadcast_to(hshift[1:2, here], (SUB, LANE))
                phi_sum, bell = normal_parts(v)
                ha[r, :, here] = pixels2(v * phi_sum).astype(bf16)
                part = pixels3(grad[:, g * LANE : (g + 1) * LANE])
                back = low(part * (phi_sum + v * bell))
                gc[g, r + 1] = back
                out.append(acc[g] + fold(back))
            return tuple(out)

        bias = lax.fori_loop(0, rows, forward, tuple(zeros_list(parts)))
        for g in range(parts):
            tiles[bias_tile + group + g, 1:2, :] = jnp.sum(bias[g], axis=0, keepdims=True)
            for tap in range(9):
                kacc[g, tap] = jnp.zeros((SUB, LANE), f32)

        def backward(r, acc):
            mask = row_mask(meta, cm, r)[:, :, :LANE]
            out = []
            for g in range(parts):
                conv = zeros_list(columns)
                for i in range(3):
                    taps = [kfb[3 * i + j, group + g] for j in range(3)]
                    sums = [kacc[g, 3 * i + j] for j in range(3)]
                    fixed = [em[g, r + 1, c] for c in range(columns)]
                    for c in range(columns):
                        value = gc[g, r + i, c]
                        for j in range(3):
                            at = c - (j - 1)
                            if 0 <= at < columns:
                                conv[at] = conv[at] + taps[j] * value
                                sums[j] = sums[j] + fixed[at] * value
                    for j in range(3):
                        kacc[g, 3 * i + j] = sums[j]
                here = pl.ds(pl.multiple_of(base + g * LANE, LANE), LANE)
                value = low(mask * jnp.stack(conv))
                ge[r, :, here] = pixels2(value).astype(bf16)
                out.append(acc[g] + fold(value))
            return tuple(out)

        bias = lax.fori_loop(0, rows, backward, tuple(zeros_list(parts)))
        for g in range(parts):
            tiles[bias_tile + group + g, 0:1, :] = jnp.sum(bias[g], axis=0, keepdims=True)
            for tap in range(9):
                at = tap_tile + (8 - tap) // SUB * groups + group + g
                row = (8 - tap) % SUB
                tiles[at, row : row + 1, :] = jnp.sum(kacc[g, tap], axis=0, keepdims=True)
        return 0

    lax.fori_loop(0, hidden // wide, chunk, 0)

    whole = rows * px
    blocks = channels // SUB
    for k, (left, right) in enumerate(((n2, ge), (gr, ha))):
        grad = dot_tn(left[...].reshape(whole, channels), right[...].reshape(whole, hidden))
        for g in range(groups):
            part = grad[:, g * LANE : (g + 1) * LANE].reshape(blocks, SUB, LANE)
            tiles[pl.ds(k * blocks * groups + g, blocks, stride=groups)] = part
    copies = [pltpu.make_async_copy(tiles, tiles_o, sem.at[0])]
    copies[0].start()

    step = 3

    def finish(b, sums):
        sums = list(sums)
        at = pl.ds(b * step, step)
        tall = step * px
        reduced_all = dot(ha[at].reshape(tall, hidden), wr[...])
        gn_all = dot(ge[at].reshape(tall, hidden), wet[...])
        for k in range(step):
            r = b * step + k
            mask = row_mask(meta, cm, r)
            reduced = pixels3(reduced_all[k * px : (k + 1) * px]) + b8(shifts, 7)
            middle = middle_of(r)
            res[r] = pixels2(mask * (middle + b8(scales, 3) * reduced))
            gn = pixels3(gn_all[k * px : (k + 1) * px])
            gn_s[r] = pixels2(gn)
            hat = (middle - mean) * rstd
            out = pixels3(ca[r].astype(f32))
            sums[0] = sums[0] + fold(gn)
            sums[1] = sums[1] + fold(gn * hat)
            sums[2] = sums[2] + fold(out * reduced)
        return tuple(sums)

    sums = lax.fori_loop(0, rows // step, finish, (zero, zero, zero))
    copies.append(pltpu.make_async_copy(gn_s, gn_o, sem.at[1]))
    copies[-1].start()
    for k, value in enumerate((sums[0], sums[1], grad_sum, sums[2])):
        mine[k : k + 1, :] = jnp.sum(value, axis=0, keepdims=True)
    wait_all_here(found)
    unalign(res, meta, nat)
    copies.append(pltpu.make_async_copy(nat, nat_o, sem.at[2]))
    copies[-1].start()
    all_sum(mine, rest[: len(stages)], rest[len(stages) :], found)
    sums_o[...] = mine[...]
    for copy in copies:
        copy.wait()


def hidden_tiles(channels, hidden):
    groups = hidden // LANE
    tap_tile = 2 * (channels // SUB) * groups
    return tap_tile, tap_tile + 2 * groups, tap_tile + 3 * groups


def hidden_block(stages, tiles, band, xa, ca, bn, meta, count, sums2, scales, shifts, hshift, w_e, w_rt, kh):
    rows, px, channels = xa.shape
    columns = px // SUB
    hidden = w_e.shape[1]
    groups = hidden // LANE
    parts = 2
    shape = jax.ShapeDtypeStruct
    return pl.pallas_call(
        functools.partial(hidden_kernel, stages),
        name="hidden_block",
        out_shape=[
            shape((2 * band, columns, SUB, channels), f32),
            shape((rows, px, channels), f32),
            shape((tiles, SUB, LANE), f32),
            shape((4, channels), f32),
        ],
        in_specs=[VMEM] * 12,
        out_specs=[ANY] * 3 + [VMEM],
        scratch_shapes=[
            pltpu.VMEM((columns, SUB, channels), f32),
            pltpu.VMEM((9, groups, SUB, LANE), f32),
            pltpu.VMEM((9, groups, SUB, LANE), f32),
            pltpu.VMEM((rows, px, channels), bf16),
            pltpu.VMEM((rows, px, channels), bf16),
            pltpu.VMEM((rows, px, hidden), bf16),
            pltpu.VMEM((rows, px, hidden), bf16),
            pltpu.VMEM((parts, rows + 2, columns, SUB, LANE), f32),
            pltpu.VMEM((parts, rows + 2, columns, SUB, LANE), f32),
            pltpu.VMEM((parts, 9, SUB, LANE), f32),
            pltpu.VMEM((hidden, channels), bf16),
            pltpu.VMEM((hidden, channels), bf16),
            pltpu.VMEM((rows, px, channels), f32),
            pltpu.VMEM((2 * band, columns, SUB, channels), f32),
            pltpu.VMEM((rows, px, channels), f32),
            pltpu.VMEM((tiles, SUB, LANE), f32),
            pltpu.SemaphoreType.DMA((3,)),
        ]
        + sum_scratch(stages, (4, channels)),
        compiler_params=pltpu.CompilerParams(
            collective_id=3, has_side_effects=True, vmem_limit_bytes=60 * MIB
        ),
    )(xa, ca, bn, meta, count, sums2, scales, shifts, hshift, w_e, w_rt, kh)


class Wave:
    def __init__(self, order, buf, full, pair_base, slots, sems, staging, sem):
        self.order, self.found = order, stage_peers(order)
        self.buf, self.full, self.pair_base = buf, full, pair_base
        self.slots, self.sems, self.staging, self.sem = slots, sems, staging, sem
        self.start, self.length = 0, buf.shape[0]
        self.shares, self.copies = [], []

    @property
    def steps(self):
        return 2 * len(self.order) + 1

    def wait(self):
        for copy in self.copies:
            copy.wait()
        self.copies = []

    def add(self, k):
        place, peers = self.found[k]
        share = self.length // self.order[k][2]
        self.start, self.length = self.start + place * share, share
        self.shares.append((self.start, self.length))
        size = math.gcd(share, 16)
        start, buf, slot, count = self.start, self.buf, self.slots[k], len(peers)

        def some(t, _):
            at = pl.ds(start + t * size, size)
            total = buf[at]
            for i in range(count):
                total = total + slot[i, pl.ds(t * size, size)]
            buf[at] = total
            return 0

        lax.fori_loop(0, share // size, some, 0)

    def scatter(self, k):
        share = self.length // self.order[k][2]
        send, recv = self.sems[4 * k : 4 * k + 2]
        for step, other, device in self.found[k][1]:
            src = self.buf.at[pl.ds(self.start + other * share, share)]
            at = step - 1
            self.copies.append(remote(src, self.slots[k].at[at], send.at[at], recv.at[at], device))
            self.copies[-1].start()

    def round(self):
        start, buf, staging = self.start, self.buf, self.staging
        pairs = self.length // 2

        def one(p, _):
            both = jnp.concatenate([buf[start + 2 * p], buf[start + 2 * p + 1]], axis=0)
            staging[p] = both.astype(bf16)
            return 0

        lax.fori_loop(0, pairs, one, 0)
        copy = pltpu.make_async_copy(staging, self.part(len(self.order) - 1), self.sem.at[0])
        copy.start()
        copy.wait()

    def part(self, k):
        start, length = self.shares[k]
        return self.full.at[pl.ds(self.pair_base + start // 2, length // 2)]

    def gather(self, k):
        send, recv = self.sems[4 * k + 2 : 4 * k + 4]
        here = self.part(k)
        for step, _, device in self.found[k][1]:
            at = step - 1
            self.copies.append(remote(here, here, send.at[at], recv.at[at], device))
            self.copies[-1].start()

    def step(self, i):
        n = len(self.order)
        if i > 0:
            self.wait()
        if 1 <= i <= n:
            self.add(i - 1)
        if i < n:
            self.scatter(i)
        elif i < 2 * n:
            if i == n:
                self.round()
            self.gather(2 * n - 1 - i)


def wave_scratch(order, tiles):
    slots, sems, length = [], [], tiles
    for _, _, size in order:
        length //= size
        slots.append(pltpu.VMEM((size - 1, length, SUB, LANE), f32))
        sems += [pltpu.SemaphoreType.DMA((size - 1,))] * 4
    own = [
        pltpu.VMEM((tiles, SUB, LANE), f32),
        pltpu.VMEM((length // 2, 2 * SUB, LANE), bf16),
        pltpu.SemaphoreType.DMA((1,)),
    ]
    return own + slots + sems


def make_wave(order, full, pair_base, refs):
    buf, staging, sem, *rest = refs[: 3 + 5 * len(order)]
    slots, sems = rest[: len(order)], rest[len(order) :]
    return Wave(order, buf, full, pair_base, slots, sems, staging, sem), refs[3 + 5 * len(order) :]


def wave_plan(sizes, channels, hidden):
    chips = sizes["imgs"]
    side = 2 if chips == 16 else 4
    one, two = ("imgs", 1, side), ("imgs", side, side)
    rest = ("imgs", side * side, chips // (side * side))
    first = ("rows", 1, sizes["rows"])
    first_order, second_order = [first, one, two, rest], [first, two, one, rest]
    short_order = [first, ("imgs", 1, side * side), rest]
    step = 2 * sizes["rows"] * chips
    square = channels // SUB * pl.cdiv(channels, LANE)
    small = pl.cdiv(25, SUB) + pl.cdiv(49, SUB)
    half = pl.cdiv(hidden_tiles(channels, hidden)[2], 2 * step) * step
    return [
        (first_order, half),
        (second_order, half),
        (first_order, pl.cdiv(2 * square, step) * step),
        (short_order, pl.cdiv(square + small * pl.cdiv(channels, LANE), step) * step),
    ]


def back_kernel(
    stages, plan, gn, bn_i, xa_i, ca_i, gl_i, sl_i, c1_i, c2_i, gp, tiles_i, nat_i,
    meta, count, sums1, sums2, sums3, scales, shifts, w_in, w_gate, w_out, kl, kd,
    mixq_o, resq_o, full_o, sums_o,
    cm, klb, kdb, gm, tt, sl, xa, ca, gl, c1, c2, gb, gg, gt, g2, g1, src, gw,
    in_sem, move_sem, mine, *rest,
):
    found = stage_peers(stages)
    say_here(found)
    rows, px, channels = xa.shape
    columns = px // SUB
    groups = groups_of(channels)
    core, chip = lax.axis_index("rows"), lax.axis_index("imgs")
    band = mixq_o.shape[0]
    parts = 3
    step = rows // parts
    pairs = [
        (gn, gm), (bn_i, gw), (xa_i, xa), (ca_i, ca), (gl_i, gl), (gp, tt), (c1_i, c1),
    ]
    loads = []
    for p in range(parts):
        at = pl.ds(p * step, step)
        loads.append([])
        for k, (a, b) in enumerate(pairs):
            loads[p].append(pltpu.make_async_copy(a.at[at], b.at[at], in_sem.at[p, k]))
            loads[p][-1].start()
    tail, waves, pair_base = list(rest[len(stages) * 3 :]), [], 0
    for order, tiles in plan:
        wave, tail = make_wave(order, full_o, pair_base, tail)
        waves.append(wave)
        pair_base += tiles // 2
    late = [
        pltpu.make_async_copy(c2_i, c2, in_sem.at[0, 7]),
        pltpu.make_async_copy(sl_i, sl, in_sem.at[1, 7]),
    ]
    half = plan[0][1]
    tile_loads = [
        pltpu.make_async_copy(tiles_i.at[pl.ds(k * half, half)], waves[k].buf, in_sem.at[k, 8])
        for k in range(2)
    ]
    for copy in tile_loads + late:
        copy.start()
    make_col_mask(meta, cm)
    spread_taps(kl, klb, flip=True)
    spread_taps(kd, kdb, flip=True)
    for edge in (0, 1, rows + 2, rows + 3):
        g1[:, edge] = jnp.zeros(g1.shape[:1] + g1.shape[2:], f32)
    total = count[0:1, 0:1]
    mean1, rstd1 = statistics(sums1, total, 0)
    scale1 = rstd1 * b8(scales, 0)
    mean2, rstd2 = statistics(sums2, total, 0)
    scale2 = rstd2 * b8(scales, 2)
    back0 = b8(sums3, 0) / total
    back1 = b8(sums3, 1) / total
    zero = jnp.zeros((SUB, channels), f32)

    def to_rows(v, out, first_sem):
        images = pl.ds(pl.multiple_of(core * SUB, SUB), SUB)
        there = remote(
            v.at[pl.ds((1 - core) * band, band)], out.at[:, :, images, :],
            move_sem.at[first_sem], move_sem.at[first_sem + 1], (1 - core, chip),
        )
        here = pltpu.make_async_copy(
            v.at[pl.ds(core * band, band)], out.at[:, :, images, :], move_sem.at[first_sem + 2]
        )
        return [there, here]

    wait_all_here(found)
    moves = to_rows(nat_i, resq_o, 0)
    for copy in moves:
        copy.start()
    for copy in tile_loads:
        copy.wait()
    done = [0, 0, 0, 0]

    def advance(*which):
        for w in which:
            if done[w] < waves[w].steps:
                waves[w].step(done[w])
                done[w] += 1

    advance(0, 1)

    def first(b, sums):
        sums = list(sums)
        gated_parts = []
        for k in range(step // 2):
            r = b * (step // 2) + k
            mask = row_mask(meta, cm, r)
            both = gw[r]
            middle = pixels3(xa[r].astype(f32)) + b8(scales, 1) * both
            hat = (middle - mean2) * rstd2
            grad = pixels3(ca[r].astype(f32)) + scale2 * (
                pixels3(gm[r]) - mask * (back0 + hat * back1)
            )
            gm[r] = pixels2(grad)
            branch = (b8(scales, 1) * grad).astype(bf16)
            gb[r] = pixels2(branch)
            sums[0] = sums[0] + fold(grad * both)
            sums[1] = sums[1] + fold(branch.astype(f32))
            gated_parts.append(pixels2(branch))
        gated_grad = dot_nt(jnp.concatenate(gated_parts, axis=0), w_out[...])
        gate_parts = []
        for k in range(step // 2):
            r = b * (step // 2) + k
            mine_grad = gated_grad[k * px : (k + 1) * px]
            gelu = gl[r].astype(f32)
            gate_grad = (mine_grad * gelu).astype(bf16)
            gg[r] = gate_grad
            gate = tt[r]
            gt[r] = (gelu * gate).astype(bf16)
            tt[r] = mine_grad * gate
            sums[2] = sums[2] + fold(pixels3(gate_grad.astype(f32)))
            gate_parts.append(gate_grad)
        conv_all = low(dot_nt(jnp.concatenate(gate_parts, axis=0), w_gate[...]))
        for k in range(step // 2):
            r = b * (step // 2) + k
            conv = conv_all[k * px : (k + 1) * px]
            for g, width in groups:
                at = slice(g * LANE, g * LANE + width)
                g2[g, r, :, :, :width] = pixels3(conv[:, at])
                src[g, r, :, :, :width] = pixels3(c1[r, :, at].astype(f32))
            sums[3] = sums[3] + fold(pixels3(conv))
        return tuple(sums)

    sums = (zero,) * 4
    for p in range(parts):
        for copy in loads[p]:
            copy.wait()
        sums = lax.fori_loop(2 * p, 2 * p + 2, first, sums)
        if p == 1:
            advance(0, 1)
    for k in range(4):
        mine[2 + k : 3 + k, :] = jnp.sum(sums[k], axis=0, keepdims=True)
    whole = rows * px
    flat = lambda ref: ref[...].reshape(whole, channels)
    blocks, n = channels // SUB, len(groups)

    def square(left, right, wave, base):
        grad = dot_tn(flat(left), flat(right))
        for g, width in groups:
            part = grad[:, g * LANE : g * LANE + width].reshape(blocks, SUB, width)
            wave.buf[pl.ds(base + g, blocks, stride=n), :, :width] = part

    def clear(buf):
        def one(t, _):
            buf[t] = jnp.zeros((SUB, LANE), f32)
            return 0

        lax.fori_loop(0, buf.shape[0], one, 0)

    clear(waves[2].buf)
    clear(waves[3].buf)
    square(gt, gb, waves[2], 0)
    for copy in late:
        copy.wait()
    square(c2, gg, waves[2], blocks * n)
    advance(2)

    def put_tap(tap, g, acc, base):
        row = jnp.sum(acc, axis=0, keepdims=True)
        at = base + tap // SUB * n + g
        waves[3].buf[at, tap % SUB : tap % SUB + 1, :] = row

    near_base = blocks * n
    far_base = near_base + pl.cdiv(kl.shape[0], SUB) * n
    for g, width in groups:
        for i in range(7):
            first_row = max(0, 3 * (3 - i))
            last_row = min(rows, rows - 3 * (i - 3))

            def taps_row(r, acc, g=g, i=i):
                at = r + (i - 3) * 3
                return tap_sums(
                    list(acc), (lambda c: g2[g, r, c], columns), lambda c: src[g, at, c], 3
                )

            acc = lax.fori_loop(first_row, last_row, taps_row, zeros_list(7))
            for j in range(7):
                put_tap(7 * i + j, g, acc[j], far_base)
        if g == 1:
            advance(0, 1, 2)

    advance(0, 1)

    def dilated(r, sums):
        mask = row_mask(meta, cm, r)
        low_i, high_i = row_range(r, rows, 3, 3)
        out = []
        for g, width in groups:

            def tap_row(i, acc):
                taps = [kdb[7 * i + j, g] for j in range(7)]
                at = r + (i - 3) * 3
                return add_row(list(acc), lambda c: g2[g, at, c], taps, 3)

            acc = lax.fori_loop(low_i, high_i, tap_row, zeros_list(columns))
            value = low(mask[:, :, :width] * jnp.stack(acc)[:, :, :width])
            g1[g, r + 2, :, :, :width] = value
            out.append(sums[g] + fold(value))
        return tuple(out)

    start = tuple(jnp.zeros((SUB, width), f32) for g, width in groups)
    sums = lax.fori_loop(0, rows // 2, dilated, start)
    advance(2)
    sums = lax.fori_loop(rows // 2, rows, dilated, sums)
    for g, width in groups:
        at = slice(g * LANE, g * LANE + width)
        mine[6:7, at] = jnp.sum(sums[g], axis=0, keepdims=True)
    advance(0, 1, 2)

    def refill(r, _):
        for g, width in groups:
            src[g, r, :, :, :width] = pixels3(gl[r, :, g * LANE : g * LANE + width].astype(f32))
        return 0

    lax.fori_loop(0, rows, refill, 0)

    for g, width in groups:
        for i in range(5):

            def taps_row(r, acc, g=g, i=i):
                return tap_sums(
                    list(acc), (lambda c: src[g, r, c], columns), lambda c: g1[g, r + i, c], 1
                )

            acc = lax.fori_loop(0, rows, taps_row, zeros_list(5))
            for j in range(5):
                put_tap(24 - (5 * i + j), g, acc[j], near_base)
        advance(0, 1, 2)

    def local(r, sums):
        mask = row_mask(meta, cm, r)
        out = []
        for g, width in groups:
            acc = zeros_list(columns)
            for i in range(5):
                taps = [klb[5 * i + j, g] for j in range(5)]
                acc = add_row(acc, lambda c: g1[g, r + i, c], taps, 1)
            value = mask[:, :, :width] * jnp.stack(acc)[:, :, :width]
            at = slice(g * LANE, g * LANE + width)
            grad = (tt[r, :, at] + pixels2(value)) * sl[r, :, at]
            gg[r, :, at] = grad.astype(bf16)
            out.append(sums[g] + fold(pixels3(low(grad))))
        x = pixels3(xa[r].astype(f32))
        gb[r] = pixels2((x - mean1) * scale1 + b8(shifts, 0)).astype(bf16)
        return tuple(out)

    sums = start
    for p in range(2):
        sums = lax.fori_loop(p * (rows // 2), (p + 1) * (rows // 2), local, sums)
        advance(0, 1, 2)
    for g, width in groups:
        at = slice(g * LANE, g * LANE + width)
        mine[7:8, at] = jnp.sum(sums[g], axis=0, keepdims=True)
    square(gb, gg, waves[3], 0)
    advance(3)

    def last(b, sums):
        sums = list(sums)
        tall = gg[pl.ds(b * (step // 2), step // 2)].reshape(step // 2 * px, channels)
        product = dot_nt(tall, w_in[...])
        for k in range(step // 2):
            r = b * (step // 2) + k
            x = pixels3(xa[r].astype(f32))
            grad = pixels3(gm[r])
            gn1 = pixels3(product[k * px : (k + 1) * px]) + b8(scales, 1) * grad
            gm[r] = pixels2(grad + scale1 * gn1)
            hat = (x - mean1) * rstd1
            sums[0] = sums[0] + fold(gn1)
            sums[1] = sums[1] + fold(gn1 * hat)
        return tuple(sums)

    sums = lax.fori_loop(0, 2 * parts, last, (zero, zero))
    for k in range(2):
        mine[k : k + 1, :] = jnp.sum(sums[k], axis=0, keepdims=True)
    advance(3)
    unalign(gm, meta, gw)
    moves += to_rows(gw, mixq_o, 3)
    for copy in moves[2:]:
        copy.start()
    all_sum(mine, rest[: len(stages)], rest[len(stages) : len(stages) * 3], found)
    sums_o[...] = mine[...]
    while any(d < w.steps for d, w in zip(done, waves)):
        advance(0, 1, 2, 3)
    for copy in moves:
        copy.wait()


def mixer_back(stages, plan, band, gn, bn, xa, ca, gl, sl, c1, c2, gp, tiles, nat, meta, count,
               sums1, sums2, sums3, scales, shifts, w_in, w_gate, w_out, kl, kd):
    rows, px, channels = xa.shape
    columns = px // SUB
    n = len(groups_of(channels))
    small = (rows, px, channels)
    shape = jax.ShapeDtypeStruct
    pairs = sum(tiles // 2 for _, tiles in plan)
    waves = []
    for order, tiles_there in plan:
        waves += wave_scratch(order, tiles_there)
    return pl.pallas_call(
        functools.partial(back_kernel, stages, plan),
        name="mixer_back",
        out_shape=[
            shape((band, columns, 2 * SUB, channels), f32),
            shape((band, columns, 2 * SUB, channels), f32),
            shape((pairs, 2 * SUB, LANE), bf16),
            shape((8, channels), f32),
        ],
        in_specs=[ANY] * 11 + [VMEM] * 12,
        out_specs=[ANY] * 3 + [VMEM],
        scratch_shapes=[
            pltpu.VMEM((columns, SUB, channels), f32),
            pltpu.VMEM((25, n, SUB, LANE), f32),
            pltpu.VMEM((49, n, SUB, LANE), f32),
        ]
        + [pltpu.VMEM(small, k) for k in (f32,) * 3 + (bf16,) * 8]
        + [
            pltpu.VMEM((n, rows, columns, SUB, LANE), f32),
            pltpu.VMEM((n, rows + 4, columns, SUB, LANE), f32),
            pltpu.VMEM((n, rows, columns, SUB, LANE), f32),
            pltpu.VMEM((2 * band, columns, SUB, channels), f32),
            pltpu.SemaphoreType.DMA((3, 9)),
            pltpu.SemaphoreType.DMA((6,)),
        ]
        + sum_scratch(stages, (8, channels))
        + waves,
        compiler_params=pltpu.CompilerParams(
            collective_id=4, has_side_effects=True, vmem_limit_bytes=63 * MIB
        ),
    )(gn, bn.reshape(rows, columns, SUB, channels), xa, ca, gl, sl, c1, c2, gp, tiles, nat, meta,
      count, sums1, sums2, sums3, scales,
      shifts, w_in, w_gate, w_out, kl, kd)


def unalign(al, meta, out):
    rows, px, channels = al.shape
    offsets = out.shape[0] - rows + 1
    for at in range(out.shape[0]):
        value = jnp.zeros((px // SUB, SUB, channels), f32)
        for t in range(offsets):
            if 0 <= at - t < rows:
                chosen = (meta[0] == float(t))[None]
                value = jnp.where(chosen, pixels3(al[at - t]), value)
        out[at] = value


def tiles_out(full, base, ref):
    rows, width = ref.shape
    groups = groups_of(width)
    n, blocks = len(groups), rows // SUB
    period = 1 if n % 2 == 0 else 2

    def block(b, _):
        for k in range(period):
            for g, wide in groups:
                tile = k * n + g
                pair = base // 2 + b * (period * n // 2) + tile // 2
                value = full[pair].astype(f32)[tile % 2 * SUB : (tile % 2 + 1) * SUB]
                at = pl.ds(pl.multiple_of((b * period + k) * SUB, SUB), SUB)
                ref[at, g * LANE : g * LANE + wide] = value[:, :wide]
        return 0

    lax.fori_loop(0, blocks // period, block, 0)
    for b in range(blocks // period * period, pl.cdiv(rows, SUB)):
        count = min(SUB, rows - b * SUB)
        for g, wide in groups:
            tile = base + b * n + g
            value = full[tile // 2].astype(f32)[tile % 2 * SUB : tile % 2 * SUB + count]
            ref[b * SUB : b * SUB + count, g * LANE : g * LANE + wide] = value[:, :wide]


def finish_kernel(
    bases, x, mixq, resq, meta, count, sums1, sums4, scales, full, in_o, res_o, *rest,
):
    grads, cm = rest[:-1], rest[-1]
    row = pl.program_id(0)
    size, top = meta[2], meta[0]

    @pl.when(row == 0)
    def _():
        for c in range(cm.shape[0]):
            cm[c] = (size > c).astype(f32)
        for ref, base in zip(grads, bases):
            tiles_out(full, base, ref)

    total = count[0:1, 0:1]
    mean = sums1[0:1, :] / total
    rstd = lax.rsqrt(sums1[1:2, :] / total - mean * mean + epsilon)
    scale = rstd * scales[0:1, :]
    back0, back1 = sums4[0:1, :] / total, sums4[1:2, :] / total
    spread = lambda v: jnp.broadcast_to(v, size.shape)
    mean, rstd, scale, back0, back1 = (spread(v) for v in (mean, rstd, scale, back0, back1))
    at = row.astype(f32)
    inside = ((at >= top) & (at < top + size)).astype(f32)
    mask = cm[...] * inside[None]
    hat = (mask * x[0].astype(f32) - mean) * rstd
    in_o[0] = mask * (mixq[0] - scale * (back0 + hat * back1))
    res_o[0] = resq[0]


def finish(x, mixq, resq, meta, count, sums1, sums4, scales, full, shapes, bases):
    band, columns, images, channels = x.shape
    block = pl.BlockSpec((1, columns, images, channels), lambda r: (r, 0, 0, 0))
    shape = jax.ShapeDtypeStruct
    return pl.pallas_call(
        functools.partial(finish_kernel, bases),
        name="finish",
        grid=(band,),
        out_shape=[shape(x.shape, f32)] * 2 + [shape(s, f32) for s in shapes],
        in_specs=[block] * 3 + [VMEM] * 6,
        out_specs=[block] * 2 + [VMEM] * len(shapes),
        scratch_shapes=[pltpu.VMEM((columns, images, channels), f32)],
        compiler_params=pltpu.CompilerParams(vmem_limit_bytes=48 * MIB),
    )(x, mixq, resq, meta, count, sums1, sums4, scales, full)


def halves(values, core, half, axis):
    mine = lax.dynamic_slice_in_dim(values, core * half, half, axis=axis)
    other = lax.dynamic_slice_in_dim(values, (1 - core) * half, half, axis=axis)
    return mine, lax.ppermute(other, "rows", [(0, 1), (1, 0)])


def first_sums_kernel(x, meta, out, cm):
    rows, columns, images, channels = x.shape
    size, top = meta[2], meta[0]
    for c in range(columns):
        cm[c] = (size > c).astype(f32)

    def one(r, sums):
        at = (r * 1).astype(f32)
        inside = ((at >= top) & (at < top + size)).astype(f32)
        value = cm[...] * inside[None] * x[r].astype(f32)
        return sums[0] + fold(value), sums[1] + fold(value * value)

    zero = jnp.zeros((images, channels), f32)
    sums = lax.fori_loop(0, rows, one, (zero, zero))
    for k in range(2):
        out[k] = sums[k][:SUB] + sums[k][SUB:]


def first_sums(x, meta):
    rows, columns, images, channels = x.shape
    return pl.pallas_call(
        first_sums_kernel,
        name="first_sums",
        out_shape=jax.ShapeDtypeStruct((2, SUB, channels), f32),
        in_specs=[VMEM] * 2,
        out_specs=VMEM,
        scratch_shapes=[pltpu.VMEM((columns, images, channels), f32)],
        compiler_params=pltpu.CompilerParams(vmem_limit_bytes=32 * MIB),
    )(x, meta)


def on_device(sizes, inputs, cotangent, scales, shifts, hidden_shift, w_inward, w_gating,
              w_outward, w_expand, w_reduce, kernel_local, kernel_dilated, kernel_hidden,
              image_size, band_split, slot_image):
    images, band, columns, channels = inputs.shape
    half = images // 2
    px = columns * half
    core = lax.axis_index("rows")
    counted = jnp.sum(image_size * image_size).astype(f32)
    count = jnp.full((SUB, LANE), counted)
    everyone = jnp.arange(image_size.shape[0], dtype=jnp.int32)
    chosen = (slot_image[:, None] == everyone[None, :]).astype(jnp.int32)
    extent = jnp.sum(chosen * image_size[None, :], axis=1)
    top = band - jnp.sum(chosen * band_split[None, :], axis=1)
    start = jnp.clip(top, 0, 2 * band - columns)
    own_meta = jnp.stack([top - core * band, top, extent]).astype(f32)
    own_meta = jnp.broadcast_to(own_meta[:, :, None], (3, images, channels))
    meta = jnp.stack([start, top - start, extent]).astype(f32)
    meta = lax.dynamic_slice_in_dim(meta, core * half, half, axis=1)
    meta = jnp.broadcast_to(meta[:, :, None], (3, half, channels))

    x = jnp.transpose(inputs, (1, 2, 0, 3))
    y = jnp.transpose(cotangent, (1, 2, 0, 3))
    stages = stage_list(sizes)
    sums1 = reduce_all(first_sums(x, own_meta), stages, 1)

    def gather_rows(v):
        mine, theirs = halves(v, core, half, 2)
        upper = jnp.where(core == 0, mine, theirs)
        lower = jnp.where(core == 0, theirs, mine)
        return jnp.concatenate([upper, lower], axis=0).reshape(2 * band, px, channels)

    xw, cw = gather_rows(x), gather_rows(y)
    xa, ca, gl, sl, c1, c2, gp, bn, sums2 = mixer_forward(
        stages, xw, cw, meta, count, sums1, scales, shifts, w_inward, w_gating, w_outward,
        kernel_local, kernel_dilated,
    )
    hidden = w_expand.shape[1]
    plan = wave_plan(sizes, channels, hidden)
    half_tiles = plan[0][1]
    nat, gn, tiles, sums3 = hidden_block(
        stages, 2 * half_tiles, band, xa, ca, bn, meta, count, sums2, scales, shifts,
        hidden_shift, w_expand, w_reduce.T, kernel_hidden,
    )
    mixq, resq, full, sums4 = mixer_back(
        stages, plan, band, gn, bn, xa, ca, gl, sl, c1, c2, gp, tiles, nat, meta, count,
        sums1, sums2, sums3, scales, shifts, w_inward, w_gating, w_outward, kernel_local,
        kernel_dilated,
    )
    square, wide = (channels, channels), (channels, hidden)
    blocks, n = channels // SUB, len(groups_of(channels))
    tap_tile, bias_tile, _ = hidden_tiles(channels, hidden)
    second = 2 * half_tiles
    third = second + plan[2][1]
    near = third + blocks * n
    far = near + pl.cdiv(kernel_local.shape[0], SUB) * n
    targets = [
        (wide, 0),
        (wide, tap_tile // 2),
        (kernel_hidden.shape, tap_tile),
        (hidden_shift.shape, bias_tile),
        (square, second),
        (square, second + blocks * n),
        (square, third),
        (kernel_local.shape, near),
        (kernel_dilated.shape, far),
    ]
    input_grad, result, gwe, gwr, gk, gh, gwo, gwg, gwi, gkl, gkd = finish(
        x, mixq, resq, own_meta, count, sums1, sums4, scales, full,
        [t[0] for t in targets], [t[1] for t in targets],
    )
    scales_grad = jnp.stack([sums4[1], sums4[2], sums3[1], sums3[3]])
    shifts_grad = jnp.stack(
        [sums4[0], sums4[7], sums4[6], sums4[5], sums4[4], sums4[3], sums3[0], sums3[2]]
    )
    back = lambda v: jnp.transpose(v, (2, 0, 1, 3))
    return (
        back(result), back(input_grad), scales_grad, shifts_grad, gh, gwi, gwg, gwo, gwe, gwr.T,
        gkl, gkd, gk,
    )


def solution(mesh):
    wide = P("imgs", "rows", None, None)
    sizes = dict(mesh.shape)
    return jax.shard_map(
        functools.partial(on_device, sizes),
        mesh=mesh,
        in_specs=(wide, wide) + (P(),) * 13 + (P("imgs"),),
        out_specs=(wide, wide) + (P(),) * 11,
        check_vma=False,
    )
```

```python
import functools
import math

import jax
import jax.numpy as jnp
from jax import lax
from jax.experimental import pallas as pl
from jax.experimental.pallas import tpu as pltpu
from jax.sharding import PartitionSpec as P

MESH = pl.DeviceIdType.MESH
epsilon = 1e-05
bf16 = jnp.bfloat16
f32 = jnp.float32
SUB = 8
LANE = 128
MIB = 1 << 20
ANY = pl.BlockSpec(memory_space=pl.ANY)
VMEM = pl.BlockSpec(memory_space=pltpu.VMEM)


def low(values):
    return values.astype(bf16).astype(f32)


def normal_parts(v):
    bell = jnp.exp2((-0.5 * 1.4426950408889634) * (v * v))
    return 0.5 + 0.5 * lax.erf(v * 0.7071067811865476), bell * 0.3989422804014327


def dot(a, b):
    return jnp.dot(a, b, preferred_element_type=f32)


def dot_nt(a, b):
    return lax.dot_general(a, b, (((1,), (1,)), ((), ())), preferred_element_type=f32)


def dot_tn(a, b):
    return lax.dot_general(a, b, (((0,), (0,)), ((), ())), preferred_element_type=f32)


def groups_of(channels):
    return [(g, min(LANE, channels - g * LANE)) for g in range(pl.cdiv(channels, LANE))]


def spread_taps(k_ref, kb, flip=False):
    count, channels = k_ref.shape
    for tap in range(count):
        from_tap = count - 1 - tap if flip else tap
        row = jnp.broadcast_to(k_ref[from_tap : from_tap + 1, :], (SUB, channels))
        for g, width in groups_of(channels):
            kb[tap, g, :, :width] = row[:, g * LANE : g * LANE + width]


def add_row(acc, load, taps, dilation):
    columns, half = len(acc), len(taps) // 2
    for c in range(columns):
        value = load(c)
        for j, tap in enumerate(taps):
            at = c - (j - half) * dilation
            if 0 <= at < columns:
                acc[at] = acc[at] + tap * value
    return acc


def tap_sums(acc, load_fixed, load_moved, dilation):
    columns, half = load_fixed[1], len(acc) // 2
    fixed = [load_fixed[0](c) for c in range(columns)]
    for c in range(columns):
        value = load_moved(c)
        for j in range(len(acc)):
            at = c - (j - half) * dilation
            if 0 <= at < columns:
                acc[j] = acc[j] + fixed[at] * value
    return acc


def row_range(r, rows, half, dilation):
    low_i = jnp.maximum(half - r // dilation, 0)
    high_i = jnp.minimum(half + (rows - 1 - r) // dilation, 2 * half)
    return low_i, high_i + 1


def zeros_list(count):
    return [jnp.zeros((SUB, LANE), f32) for _ in range(count)]


def b8(ref, i):
    return jnp.broadcast_to(ref[i : i + 1, :], (SUB, ref.shape[1]))


def make_col_mask(meta, cm):
    size = meta[2]
    for c in range(cm.shape[0]):
        cm[c] = (size > c).astype(f32)


def row_mask(meta, cm, r):
    at = (r * 1).astype(f32)
    inside = (at >= meta[1]) & (at < meta[1] + meta[2])
    return cm[...] * inside.astype(f32)[None]


def pixels3(values):
    return values.reshape(values.shape[0] // SUB, SUB, values.shape[1])


def pixels2(values):
    return values.reshape(values.shape[0] * SUB, values.shape[2])


def fold(values):
    return jnp.sum(values, axis=0)


def statistics(sums, count, i):
    mean = b8(sums, i) / count
    return mean, lax.rsqrt(b8(sums, i + 1) / count - mean * mean + epsilon)


def stage_list(sizes):
    stages = [("rows", 1, sizes["rows"])]
    left, stride = sizes["imgs"], 1
    while left > 1:
        size = 4 if left % 4 == 0 else (2 if left % 2 == 0 else left)
        stages.append(("imgs", stride, size))
        left, stride = left // size, stride * size
    return [s for s in stages if s[2] > 1]


def reach_list(sizes):
    return [("rows", 1, sizes["rows"]), ("imgs", 1, sizes["imgs"])]


def stage_peers(stages):
    core = lax.axis_index("rows")
    chip = lax.axis_index("imgs")
    found = []
    for axis, stride, size in stages:
        index = core if axis == "rows" else chip
        place = lax.rem(index // stride, size)
        peers = []
        for step in range(1, size):
            other = lax.rem(place + step, size)
            at = index + (other - place) * stride
            peers.append((step, other, (at, chip) if axis == "rows" else (core, at)))
        found.append((place, peers))
    return found


def say_here(found):
    barrier = pltpu.get_barrier_semaphore()
    for _, peers in found:
        for _, _, device in peers:
            pl.semaphore_signal(barrier, inc=1, device_id=device, device_id_type=MESH)


def wait_all_here(found):
    pl.semaphore_wait(pltpu.get_barrier_semaphore(), sum(len(peers) for _, peers in found))


def greet(found):
    say_here(found)
    wait_all_here(found)


def remote(src, dst, send, recv, device):
    return pltpu.make_async_remote_copy(
        src_ref=src, dst_ref=dst, send_sem=send, recv_sem=recv,
        device_id=device, device_id_type=MESH,
    )


class AllSum:
    def __init__(self, stages, mine, rest):
        self.found, self.mine = stage_peers(stages), mine
        n = len(stages)
        self.slots, self.sems = rest[:n], rest[n : 3 * n]

    def start(self, k):
        slot, (send, recv) = self.slots[k], self.sems[2 * k : 2 * k + 2]
        self.copies = []
        for step, _, device in self.found[k][1]:
            at = step - 1
            self.copies.append(remote(self.mine, slot.at[at], send.at[at], recv.at[at], device))
            self.copies[-1].start()

    def end(self, k):
        for copy in self.copies:
            copy.wait()
        total = self.mine[...]
        for step, _, _ in self.found[k][1]:
            total = total + self.slots[k][step - 1]
        self.mine[...] = total


def all_sum(stages, mine, rest):
    total = AllSum(stages, mine, rest)
    for k in range(len(stages)):
        total.start(k)
        total.end(k)


def sum_scratch(stages, table):
    sems = []
    for _, _, size in stages:
        sems += [pltpu.SemaphoreType.DMA((size - 1,))] * 2
    slots = [pltpu.VMEM((size - 1,) + table, f32) for _, _, size in stages]
    return [pltpu.VMEM(table, f32)] + slots + sems


def mixer_kernel(
    stages, x_i, y_i, own_meta, meta, count, scales, shifts, w_in, w_gate, w_out, kl, kd,
    xa_o, ca_o, gl_o, sl_o, c1_o, c2_o, gp_o, bn_o, sums1_o, sums_o,
    cm, klb, kdb, xa, ca, gl, sl, c1, c2, gp, bn, gf, c1f, sem,
    own_cm, xs, ys, xw, cw, move_sem, mine, *rest,
):
    found = stage_peers(stages)
    say_here(found)
    rows, px, channels = xa.shape
    columns = px // SUB
    groups = groups_of(channels)
    offsets = xw.shape[0] - rows + 1
    core, chip = lax.axis_index("rows"), lax.axis_index("imgs")
    band = x_i.shape[0]
    upper = core == 0
    size, top = own_meta[1], own_meta[0]
    for c in range(columns):
        own_cm[c] = (size > c).astype(f32)

    def split(value, full, out, r):
        a, b = value[:, :SUB], value[:, SUB:]
        full[core * band + r] = pixels2(jnp.where(upper, a, b)).astype(bf16)
        out[r] = pixels2(jnp.where(upper, b, a)).astype(bf16)

    def split_x(r, sums):
        at = (r * 1).astype(f32)
        inside = ((at >= top) & (at < top + size)).astype(f32)
        value = x_i[r].astype(f32)
        split(value, xw, xs, r)
        value = own_cm[...] * inside[None] * value
        return sums[0] + fold(value), sums[1] + fold(value * value)

    def split_y(r, _):
        split(y_i[r].astype(f32), cw, ys, r)
        return 0

    def to_other(out, full, k):
        at = pl.ds(core * band, band)
        return remote(out, full.at[at], move_sem.at[k], move_sem.at[k + 1], (1 - core, chip))

    zero = jnp.zeros((2 * SUB, channels), f32)
    sums = lax.fori_loop(0, band, split_x, (zero, zero))
    for k in range(2):
        mine[k : k + 1, :] = jnp.sum(sums[k], axis=0, keepdims=True)
    wait_all_here(found)
    moves = [to_other(xs, xw, 0), to_other(ys, cw, 2)]
    first_sum = AllSum(stages, mine, rest)
    first_sum.start(0)
    moves[0].start()
    lax.fori_loop(0, band, split_y, 0)
    moves[1].start()
    first_sum.end(0)
    first_sum.start(1)
    make_col_mask(meta, cm)
    spread_taps(kl, klb)
    spread_taps(kd, kdb)
    for edge in (0, 1, rows + 2, rows + 3):
        gf[:, edge] = jnp.zeros(gf.shape[:1] + gf.shape[2:], f32)
    first_sum.end(1)
    for k in range(2, len(stages)):
        first_sum.start(k)
        first_sum.end(k)
    sums1_o[...] = mine[...]
    for copy in moves:
        copy.wait()
    total = count[0:1, 0:1]
    mean, rstd = statistics(sums1_o, total, 0)
    scale = rstd * b8(scales, 0)
    starts = [meta[0] == float(t) for t in range(offsets)]

    def aligned(ref, r):
        value = pixels3(ref[r].astype(f32))
        for t in range(1, offsets):
            value = jnp.where(starts[t][None], pixels3(ref[r + t].astype(f32)), value)
        return value

    def first(r, _):
        mask = row_mask(meta, cm, r)
        x = mask * aligned(xw, r)
        xa[r] = pixels2(x).astype(bf16)
        ca[r] = pixels2(mask * aligned(cw, r)).astype(bf16)
        normed = pixels2((x - mean) * scale + b8(shifts, 0)).astype(bf16)
        pre = pixels3(dot(normed, w_in[...])) + b8(shifts, 1)
        phi_sum, bell = normal_parts(pre)
        gelu = mask * low(pre * phi_sum)
        sl[r] = pixels2(phi_sum + pre * bell)
        gl[r] = pixels2(gelu).astype(bf16)
        for g, width in groups:
            gf[g, r + 2, :, :, :width] = gelu[:, :, g * LANE : g * LANE + width]
        return 0

    lax.fori_loop(0, rows, first, 0)
    early = [(xa, xa_o), (ca, ca_o), (gl, gl_o), (sl, sl_o)]
    copies = [pltpu.make_async_copy(a, b, sem.at[k]) for k, (a, b) in enumerate(early)]
    for copy in copies:
        copy.start()

    def local(r, _):
        mask = row_mask(meta, cm, r)
        for g, width in groups:
            acc = zeros_list(columns)
            for i in range(5):
                taps = [klb[5 * i + j, g] for j in range(5)]
                acc = add_row(acc, lambda c: gf[g, r + i, c], taps, 1)
            bias = b8(shifts, 2)[:, g * LANE : g * LANE + width]
            value = jnp.stack(acc)[:, :, :width] + bias
            value = mask[:, :, :width] * low(value)
            c1f[g, r, :, :, :width] = value
            c1[r, :, g * LANE : g * LANE + width] = pixels2(value).astype(bf16)
        return 0

    lax.fori_loop(0, rows, local, 0)
    copies.append(pltpu.make_async_copy(c1, c1_o, sem.at[4]))
    copies[-1].start()

    def dilated(r, _):
        low_i, high_i = row_range(r, rows, 3, 3)
        for g, width in groups:

            def tap_row(i, acc):
                taps = [kdb[7 * i + j, g] for j in range(7)]
                at = r + (i - 3) * 3
                return add_row(list(acc), lambda c: c1f[g, at, c], taps, 3)

            acc = lax.fori_loop(low_i, high_i, tap_row, zeros_list(columns))
            bias = b8(shifts, 3)[:, g * LANE : g * LANE + width]
            value = jnp.stack(acc)[:, :, :width] + bias
            c2[r, :, g * LANE : g * LANE + width] = pixels2(value).astype(bf16)
        return 0

    lax.fori_loop(0, rows, dilated, 0)
    copies.append(pltpu.make_async_copy(c2, c2_o, sem.at[5]))
    copies[-1].start()

    def last(r, sums):
        mask = row_mask(meta, cm, r)
        gate = dot(c2[r], w_gate[...]) + jnp.broadcast_to(shifts[4:5, :], (px, channels))
        gp[r] = gate
        gated = (gl[r].astype(f32) * gate).astype(bf16)
        branch = dot(gated, w_out[...])
        x = pixels3(xa[r].astype(f32))
        normed = low((x - mean) * scale + b8(shifts, 0))
        both = pixels3(branch) + b8(shifts, 5) + normed
        bn[r] = pixels2(both)
        middle = mask * (x + b8(scales, 1) * both)
        return sums[0] + fold(middle), sums[1] + fold(middle * middle)

    zero = jnp.zeros((SUB, channels), f32)
    sums = lax.fori_loop(0, rows, last, (zero, zero))
    copies.append(pltpu.make_async_copy(gp, gp_o, sem.at[6]))
    copies[-1].start()
    copies.append(pltpu.make_async_copy(bn, bn_o, sem.at[7]))
    copies[-1].start()
    for k in range(2):
        mine[k : k + 1, :] = jnp.sum(sums[k], axis=0, keepdims=True)
    all_sum(stages, mine, rest[3 * len(stages) :])
    sums_o[...] = mine[...]
    for copy in copies:
        copy.wait()


def mixer_forward(
    stages, x, y, own_meta, meta, count, scales, shifts, w_in, w_gate, w_out, kl, kd
):
    band, columns, images, channels = x.shape
    px = columns * SUB
    rows = columns
    n = len(groups_of(channels))
    small = (rows, px, channels)
    kinds = (bf16, bf16, bf16, f32, bf16, bf16, f32, f32)
    return pl.pallas_call(
        functools.partial(mixer_kernel, stages),
        name="mixer_forward",
        out_shape=[jax.ShapeDtypeStruct(small, k) for k in kinds]
        + [jax.ShapeDtypeStruct((2, channels), f32)] * 2,
        in_specs=[VMEM] * 12,
        out_specs=[ANY] * 8 + [VMEM] * 2,
        scratch_shapes=[
            pltpu.VMEM((columns, SUB, channels), f32),
            pltpu.VMEM((25, n, SUB, LANE), f32),
            pltpu.VMEM((49, n, SUB, LANE), f32),
        ]
        + [pltpu.VMEM(small, k) for k in kinds]
        + [
            pltpu.VMEM((n, rows + 4, columns, SUB, LANE), f32),
            pltpu.VMEM((n, rows, columns, SUB, LANE), f32),
            pltpu.SemaphoreType.DMA((8,)),
            pltpu.VMEM((columns, images, channels), f32),
            pltpu.VMEM((band, px, channels), bf16),
            pltpu.VMEM((band, px, channels), bf16),
            pltpu.VMEM((2 * band, px, channels), bf16),
            pltpu.VMEM((2 * band, px, channels), bf16),
            pltpu.SemaphoreType.DMA((4,)),
        ]
        + sum_scratch(stages, (2, channels))
        + sum_scratch(stages, (2, channels))[1:],
        compiler_params=pltpu.CompilerParams(
            collective_id=2, has_side_effects=True, vmem_limit_bytes=62 * MIB
        ),
    )(x, y, own_meta, meta, count, scales, shifts, w_in, w_gate, w_out, kl, kd)


class Wave:
    def __init__(self, order, tiles, refs, buf, base=0, full=None, pair_base=0, done=0):
        self.order, self.found = order, stage_peers(order)
        self.buf, self.base, self.full, self.pair_base = buf, base, full, pair_base
        n = len(order)
        self.slots, self.sems = refs[:n], refs[n:]
        self.start, self.length, self.origin = 0, tiles, 0
        self.shares, self.copies, self.done = [], [], done
        for k in range(done):
            self.take(k)
        self.origin = self.start

    @property
    def steps(self):
        return 2 * len(self.order) + 1

    def take(self, k):
        self.length //= self.order[k][2]
        self.start = self.start + self.found[k][0] * self.length
        self.shares.append((self.start, self.length))

    def wait(self):
        for copy in self.copies:
            copy.wait()
        self.copies = []

    def at(self, tile):
        return self.base + tile - self.origin

    def add(self, k):
        self.wait()
        self.take(k)
        size = math.gcd(self.length, 16)
        start, buf, slot = self.at(self.start), self.buf, self.slots[k]
        count = len(self.found[k][1])

        def some(t, _):
            at = pl.ds(start + t * size, size)
            total = buf[at]
            for i in range(count):
                total = total + slot[i, pl.ds(t * size, size)]
            buf[at] = total
            return 0

        lax.fori_loop(0, self.length // size, some, 0)

    def scatter(self, k):
        share = self.length // self.order[k][2]
        send, recv = self.sems[4 * k : 4 * k + 2]
        for step, other, device in self.found[k][1]:
            src = self.buf.at[pl.ds(self.at(self.start + other * share), share)]
            at = step - 1
            self.copies.append(remote(src, self.slots[k].at[at], send.at[at], recv.at[at], device))
            self.copies[-1].start()

    def round(self):
        start, buf, full = self.at(self.start), self.buf, self.full
        first = self.pair_base + self.start // 2

        def one(p, _):
            both = jnp.concatenate([buf[start + 2 * p], buf[start + 2 * p + 1]], axis=0)
            full[first + p] = both.astype(bf16)
            return 0

        lax.fori_loop(0, self.length // 2, one, 0)

    def part(self, k):
        start, length = self.shares[k]
        return self.full.at[pl.ds(self.pair_base + start // 2, length // 2)]

    def gather(self, k):
        send, recv = self.sems[4 * k + 2 : 4 * k + 4]
        here = self.part(k)
        for step, _, device in self.found[k][1]:
            at = step - 1
            self.copies.append(remote(here, here, send.at[at], recv.at[at], device))
            self.copies[-1].start()

    def guess(self, i):
        n = len(self.order)
        if i >= 2 * n:
            return 0.0
        k = i if i < n else 2 * n - 1 - i
        axis, _, size = self.order[k]
        share = self.length // size if i < n else self.shares[k][1] / 2
        if axis == "rows":
            return 1.5 + share * 0.008
        links = {2: 2, 4: 8}.get(size, 16)
        return LATENCY + links * share * PER_TILE

    def step(self, i):
        n = len(self.order)
        self.wait()
        if self.done < i <= n:
            self.add(i - 1)
        if i < n:
            self.scatter(i)
        elif i < 2 * n:
            if i == n:
                self.round()
            self.gather(2 * n - 1 - i)


def wave_scratch(order, tiles, first=0, last=None):
    last = len(order) if last is None else last
    slots, sems, length = [], [], tiles
    for k, (_, _, size) in enumerate(order):
        length //= size
        used = first <= k < last
        slots.append(pltpu.VMEM((size - 1, length if used else 1, SUB, LANE), f32))
        sems += [pltpu.SemaphoreType.DMA((size - 1,))] * 4
    return slots + sems


def wave_refs(order):
    return 5 * len(order)


LATENCY, PER_TILE = 3.0, 0.065
EARLY = 2


def early_tiles(order, tiles):
    return tiles // math.prod(size for _, _, size in order[:EARLY])


def hidden_kernel(
    stages, plan, xa, ca, bn, meta, count, sums2, scales, shifts, hshift, w_e, w_rt, kh,
    nat_o, gn_o, tiles_o, sums_o,
    cm, khb, kfb, n2, gr, ha, ge, em, gc, kacc, wet, wr, res, nat, gn_s, tiles, sem, mine, *rest,
):
    found = stage_peers(stages)
    say_here(found)
    tail, waves = list(rest[3 * len(stages) :]), []
    for k, (order, count_tiles) in enumerate(plan[:2]):
        refs, tail = tail[: wave_refs(order)], tail[wave_refs(order) :]
        waves.append(Wave(order, count_tiles, refs, tiles, base=k * count_tiles))
    rows, px, channels = xa.shape
    columns = px // SUB
    hidden = w_e.shape[1]
    wide = em.shape[0] * LANE
    parts = em.shape[0]
    wide_step = 6
    groups = hidden // LANE
    tap_tile, bias_tile, last_tile = hidden_tiles(channels, hidden)
    for t in range(tap_tile, last_tile):
        tiles[t] = jnp.zeros((SUB, LANE), f32)
    make_col_mask(meta, cm)
    spread_taps(kh, khb)
    spread_taps(kh, kfb, flip=True)
    for edge in (0, rows + 1):
        em[:, edge] = jnp.zeros(em.shape[:1] + em.shape[2:], f32)
        gc[:, edge] = jnp.zeros(gc.shape[:1] + gc.shape[2:], f32)
    wet[...] = w_e[...].astype(f32).T.astype(bf16)
    wr[...] = w_rt[...].astype(f32).T.astype(bf16)
    total = count[0:1, 0:1]
    mean, rstd = statistics(sums2, total, 0)
    scale = rstd * b8(scales, 2)

    def middle_of(r):
        return pixels3(xa[r].astype(f32)) + b8(scales, 1) * pixels3(bn[r])

    def prepare(r, acc):
        normed = (middle_of(r) - mean) * scale + b8(shifts, 6)
        n2[r] = pixels2(normed).astype(bf16)
        grad = (b8(scales, 3) * pixels3(ca[r].astype(f32))).astype(bf16)
        gr[r] = pixels2(grad)
        return acc + fold(grad.astype(f32))

    zero = jnp.zeros((SUB, channels), f32)
    grad_sum = lax.fori_loop(0, rows, prepare, zero)

    def chunk(f, _):
        base = pl.multiple_of(f * wide, wide)
        lanes = pl.ds(base, wide)
        group = f * parts

        def expand(b, _):
            tall = n2[pl.ds(b * wide_step, wide_step)].reshape(wide_step * px, channels)
            product = dot(tall, w_e[:, lanes])
            for k in range(wide_step):
                r = b * wide_step + k
                mask = row_mask(meta, cm, r)[:, :, :LANE]
                value = product[k * px : (k + 1) * px]
                value = low(value + jnp.broadcast_to(hshift[0:1, lanes], value.shape))
                for g in range(parts):
                    em[g, r + 1] = mask * pixels3(value[:, g * LANE : (g + 1) * LANE])
            return 0

        lax.fori_loop(0, rows // wide_step, expand, 0)

        def forward(r, acc):
            grad = dot(gr[r], w_rt[:, lanes])
            out = []
            for g in range(parts):
                conv = zeros_list(columns)
                for i in range(3):
                    taps = [khb[3 * i + j, group + g] for j in range(3)]
                    conv = add_row(conv, lambda c: em[g, r + i, c], taps, 1)
                here = pl.ds(pl.multiple_of(base + g * LANE, LANE), LANE)
                v = jnp.stack(conv) + jnp.broadcast_to(hshift[1:2, here], (SUB, LANE))
                phi_sum, bell = normal_parts(v)
                ha[r, :, here] = pixels2(v * phi_sum).astype(bf16)
                part = pixels3(grad[:, g * LANE : (g + 1) * LANE])
                back = low(part * (phi_sum + v * bell))
                gc[g, r + 1] = back
                out.append(acc[g] + fold(back))
            return tuple(out)

        bias = lax.fori_loop(0, rows, forward, tuple(zeros_list(parts)))
        for g in range(parts):
            tiles[bias_tile + group + g, 1:2, :] = jnp.sum(bias[g], axis=0, keepdims=True)
            for tap in range(9):
                kacc[g, tap] = jnp.zeros((SUB, LANE), f32)

        def backward(r, acc):
            mask = row_mask(meta, cm, r)[:, :, :LANE]
            out = []
            for g in range(parts):
                conv = zeros_list(columns)
                for i in range(3):
                    taps = [kfb[3 * i + j, group + g] for j in range(3)]
                    sums = [kacc[g, 3 * i + j] for j in range(3)]
                    fixed = [em[g, r + 1, c] for c in range(columns)]
                    for c in range(columns):
                        value = gc[g, r + i, c]
                        for j in range(3):
                            at = c - (j - 1)
                            if 0 <= at < columns:
                                conv[at] = conv[at] + taps[j] * value
                                sums[j] = sums[j] + fixed[at] * value
                    for j in range(3):
                        kacc[g, 3 * i + j] = sums[j]
                here = pl.ds(pl.multiple_of(base + g * LANE, LANE), LANE)
                value = low(mask * jnp.stack(conv))
                ge[r, :, here] = pixels2(value).astype(bf16)
                out.append(acc[g] + fold(value))
            return tuple(out)

        bias = lax.fori_loop(0, rows, backward, tuple(zeros_list(parts)))
        for g in range(parts):
            tiles[bias_tile + group + g, 0:1, :] = jnp.sum(bias[g], axis=0, keepdims=True)
            for tap in range(9):
                at = tap_tile + (8 - tap) // SUB * groups + group + g
                row = (8 - tap) % SUB
                tiles[at, row : row + 1, :] = jnp.sum(kacc[g, tap], axis=0, keepdims=True)
        return 0

    lax.fori_loop(0, hidden // wide, chunk, 0)

    whole = rows * px
    blocks = channels // SUB
    for k, (left, right) in enumerate(((n2, ge), (gr, ha))):
        grad = dot_tn(left[...].reshape(whole, channels), right[...].reshape(whole, hidden))
        for g in range(groups):
            part = grad[:, g * LANE : (g + 1) * LANE].reshape(blocks, SUB, LANE)
            tiles[pl.ds(k * blocks * groups + g, blocks, stride=groups)] = part
    wait_all_here(found)
    for wave in waves:
        wave.step(0)

    step = 3

    def finish(b, sums):
        sums = list(sums)
        at = pl.ds(b * step, step)
        tall = step * px
        reduced_all = dot(ha[at].reshape(tall, hidden), wr[...])
        gn_all = dot(ge[at].reshape(tall, hidden), wet[...])
        for k in range(step):
            r = b * step + k
            mask = row_mask(meta, cm, r)
            reduced = pixels3(reduced_all[k * px : (k + 1) * px]) + b8(shifts, 7)
            middle = middle_of(r)
            res[r] = pixels2(mask * (middle + b8(scales, 3) * reduced))
            gn = pixels3(gn_all[k * px : (k + 1) * px])
            gn_s[r] = pixels2(gn)
            hat = (middle - mean) * rstd
            out = pixels3(ca[r].astype(f32))
            sums[0] = sums[0] + fold(gn)
            sums[1] = sums[1] + fold(gn * hat)
            sums[2] = sums[2] + fold(out * reduced)
        return tuple(sums)

    sums = lax.fori_loop(0, 2, finish, (zero, zero, zero))
    for wave in waves:
        wave.step(1)
    sums = lax.fori_loop(2, rows // step, finish, sums)
    copies = [pltpu.make_async_copy(gn_s, gn_o, sem.at[1])]
    copies[-1].start()
    for k, value in enumerate((sums[0], sums[1], grad_sum, sums[2])):
        mine[k : k + 1, :] = jnp.sum(value, axis=0, keepdims=True)
    unalign(res, meta, nat)
    copies.append(pltpu.make_async_copy(nat, nat_o, sem.at[2]))
    copies[-1].start()
    all_sum(stages, mine, rest)
    sums_o[...] = mine[...]
    for k, wave in enumerate(waves):
        wave.add(EARLY - 1)
        at = pl.ds(wave.at(wave.start), wave.length)
        here = pl.ds(k * wave.length, wave.length)
        copies.append(pltpu.make_async_copy(tiles.at[at], tiles_o.at[here], sem.at[k and 3]))
        copies[-1].start()
    for copy in copies:
        copy.wait()


def hidden_tiles(channels, hidden):
    groups = hidden // LANE
    tap_tile = 2 * (channels // SUB) * groups
    return tap_tile, tap_tile + 2 * groups, tap_tile + 3 * groups


def hidden_block(stages, plan, band, xa, ca, bn, meta, count, sums2, scales, shifts, hshift, w_e, w_rt, kh):
    rows, px, channels = xa.shape
    columns = px // SUB
    hidden = w_e.shape[1]
    groups = hidden // LANE
    parts = 2
    shape = jax.ShapeDtypeStruct
    tiles = sum(count_tiles for _, count_tiles in plan[:2])
    early = sum(early_tiles(*wave) for wave in plan[:2])
    waves = []
    for wave in plan[:2]:
        waves += wave_scratch(*wave, 0, EARLY)
    return pl.pallas_call(
        functools.partial(hidden_kernel, stages, plan),
        name="hidden_block",
        out_shape=[
            shape((2 * band, columns, SUB, channels), f32),
            shape((rows, px, channels), f32),
            shape((early, SUB, LANE), f32),
            shape((4, channels), f32),
        ],
        in_specs=[VMEM] * 12,
        out_specs=[ANY] * 3 + [VMEM],
        scratch_shapes=[
            pltpu.VMEM((columns, SUB, channels), f32),
            pltpu.VMEM((9, groups, SUB, LANE), f32),
            pltpu.VMEM((9, groups, SUB, LANE), f32),
            pltpu.VMEM((rows, px, channels), bf16),
            pltpu.VMEM((rows, px, channels), bf16),
            pltpu.VMEM((rows, px, hidden), bf16),
            pltpu.VMEM((rows, px, hidden), bf16),
            pltpu.VMEM((parts, rows + 2, columns, SUB, LANE), f32),
            pltpu.VMEM((parts, rows + 2, columns, SUB, LANE), f32),
            pltpu.VMEM((parts, 9, SUB, LANE), f32),
            pltpu.VMEM((hidden, channels), bf16),
            pltpu.VMEM((hidden, channels), bf16),
            pltpu.VMEM((rows, px, channels), f32),
            pltpu.VMEM((2 * band, columns, SUB, channels), f32),
            pltpu.VMEM((rows, px, channels), f32),
            pltpu.VMEM((tiles, SUB, LANE), f32),
            pltpu.SemaphoreType.DMA((4,)),
        ]
        + sum_scratch(stages, (4, channels))
        + waves,
        compiler_params=pltpu.CompilerParams(
            collective_id=3, has_side_effects=True, vmem_limit_bytes=63 * MIB
        ),
    )(xa, ca, bn, meta, count, sums2, scales, shifts, hshift, w_e, w_rt, kh)


def wave_plan(sizes, channels, hidden):
    chips = sizes["imgs"]
    side = 2 if chips == 16 else 4
    one, two = ("imgs", 1, side), ("imgs", side, side)
    rest = ("imgs", side * side, chips // (side * side))
    first = ("rows", 1, sizes["rows"])
    first_order, second_order = [first, one, two, rest], [first, two, one, rest]
    short_order = [first, ("imgs", 1, chips)]
    step = 2 * sizes["rows"] * chips
    square = channels // SUB * pl.cdiv(channels, LANE)
    small = pl.cdiv(25, SUB) + pl.cdiv(49, SUB)
    half = pl.cdiv(hidden_tiles(channels, hidden)[2], 2 * step) * step
    return [
        (first_order, half),
        (second_order, half),
        (first_order, pl.cdiv(2 * square, step) * step),
        (short_order, pl.cdiv(square + small * pl.cdiv(channels, LANE), step) * step),
    ]


def back_kernel(
    reach, stages, plan, gn, bn_i, xa_i, ca_i, gl_i, sl_i, c1_i, c2_i, gp, tiles_i, nat_i,
    meta, count, sums1, sums2, sums3, scales, shifts, w_in, w_gate, w_out, kl, kd,
    mixo_o, mixq_o, resq_o, full_o, sums_o,
    cm, klb, kdb, gm, tt, sl, xa, ca, gl, c1, c2, gb, gg, gt, g2, g1, src, gw, full,
    in_sem, move_sem, mine, *rest,
):
    found = stage_peers(stages)
    say_here(stage_peers(reach))
    rows, px, channels = xa.shape
    columns = px // SUB
    groups = groups_of(channels)
    core, chip = lax.axis_index("rows"), lax.axis_index("imgs")
    band = mixq_o.shape[0]
    parts = 3
    step = rows // parts
    pairs = [
        (gn, gm), (bn_i, gw), (xa_i, xa), (ca_i, ca), (gl_i, gl), (gp, tt), (c1_i, c1),
    ]
    loads = []
    for p in range(parts):
        at = pl.ds(p * step, step)
        loads.append([])
        for k, (a, b) in enumerate(pairs):
            loads[p].append(pltpu.make_async_copy(a.at[at], b.at[at], in_sem.at[p, k]))
            loads[p][-1].start()
    tail, waves, pair_base = list(rest[len(stages) * 3 :]), [], 0
    for k, (order, tiles) in enumerate(plan):
        (buf, *refs), tail = tail[: 1 + wave_refs(order)], tail[1 + wave_refs(order) :]
        early = EARLY if k < 2 else 0
        waves.append(Wave(order, tiles, refs, buf, 0, full, pair_base, early))
        pair_base += tiles // 2
    late = [
        pltpu.make_async_copy(c2_i, c2, in_sem.at[0, 7]),
        pltpu.make_async_copy(sl_i, sl, in_sem.at[1, 7]),
    ]
    half = early_tiles(*plan[0])
    tile_loads = [
        pltpu.make_async_copy(tiles_i.at[pl.ds(k * half, half)], waves[k].buf, in_sem.at[k, 8])
        for k in range(2)
    ]
    for copy in tile_loads + late:
        copy.start()
    make_col_mask(meta, cm)
    spread_taps(kl, klb, flip=True)
    spread_taps(kd, kdb, flip=True)
    for edge in (0, 1, rows + 2, rows + 3):
        g1[:, edge] = jnp.zeros(g1.shape[:1] + g1.shape[2:], f32)
    total = count[0:1, 0:1]
    mean1, rstd1 = statistics(sums1, total, 0)
    scale1 = rstd1 * b8(scales, 0)
    mean2, rstd2 = statistics(sums2, total, 0)
    scale2 = rstd2 * b8(scales, 2)
    back0 = b8(sums3, 0) / total
    back1 = b8(sums3, 1) / total
    zero = jnp.zeros((SUB, channels), f32)

    def to_other(v, out, first_sem):
        return remote(
            v.at[pl.ds((1 - core) * band, band)], out,
            move_sem.at[first_sem], move_sem.at[first_sem + 1], (1 - core, chip),
        )

    all_found = stage_peers(reach)
    wait_all_here(all_found)
    for copy in tile_loads:
        copy.wait()
    done, ready, clock = [EARLY, EARLY, 0, 0], [0.0, 0.0, None, None], [0.0]

    def take(w):
        wave = waves[w]
        wave.step(done[w])
        ready[w] = clock[0] + wave.guess(done[w])
        done[w] += 1

    def stop(spent):
        clock[0] += spent
        for w, wave in enumerate(waves):
            if ready[w] is not None and done[w] < wave.steps and ready[w] <= clock[0]:
                take(w)

    stop(0.0)
    moves = [to_other(nat_i, resq_o, 0)]
    moves[0].start()

    def first(b, sums):
        sums = list(sums)
        gated_parts = []
        for k in range(step // 2):
            r = b * (step // 2) + k
            mask = row_mask(meta, cm, r)
            both = gw[r]
            middle = pixels3(xa[r].astype(f32)) + b8(scales, 1) * both
            hat = (middle - mean2) * rstd2
            grad = pixels3(ca[r].astype(f32)) + scale2 * (
                pixels3(gm[r]) - mask * (back0 + hat * back1)
            )
            gm[r] = pixels2(grad)
            branch = (b8(scales, 1) * grad).astype(bf16)
            gb[r] = pixels2(branch)
            sums[0] = sums[0] + fold(grad * both)
            sums[1] = sums[1] + fold(branch.astype(f32))
            gated_parts.append(pixels2(branch))
        gated_grad = dot_nt(jnp.concatenate(gated_parts, axis=0), w_out[...])
        gate_parts = []
        for k in range(step // 2):
            r = b * (step // 2) + k
            mine_grad = gated_grad[k * px : (k + 1) * px]
            gelu = gl[r].astype(f32)
            gate_grad = (mine_grad * gelu).astype(bf16)
            gg[r] = gate_grad
            gate = tt[r]
            gt[r] = (gelu * gate).astype(bf16)
            tt[r] = mine_grad * gate
            sums[2] = sums[2] + fold(pixels3(gate_grad.astype(f32)))
            gate_parts.append(gate_grad)
        conv_all = low(dot_nt(jnp.concatenate(gate_parts, axis=0), w_gate[...]))
        for k in range(step // 2):
            r = b * (step // 2) + k
            conv = conv_all[k * px : (k + 1) * px]
            for g, width in groups:
                at = slice(g * LANE, g * LANE + width)
                g2[g, r, :, :, :width] = pixels3(conv[:, at])
                src[g, r, :, :, :width] = pixels3(c1[r, :, at].astype(f32))
            sums[3] = sums[3] + fold(pixels3(conv))
        return tuple(sums)

    sums = (zero,) * 4
    for p in range(parts):
        for copy in loads[p]:
            copy.wait()
        sums = lax.fori_loop(2 * p, 2 * p + 2, first, sums)
        stop(3.0)
    for k in range(4):
        mine[2 + k : 3 + k, :] = jnp.sum(sums[k], axis=0, keepdims=True)
    whole = rows * px
    flat = lambda ref: ref[...].reshape(whole, channels)
    blocks, n = channels // SUB, len(groups)

    def square(left, right, wave, base):
        grad = dot_tn(flat(left), flat(right))
        for g, width in groups:
            part = grad[:, g * LANE : g * LANE + width].reshape(blocks, SUB, width)
            wave.buf[pl.ds(base + g, blocks, stride=n), :, :width] = part

    def clear(buf):
        def one(t, _):
            buf[t] = jnp.zeros((SUB, LANE), f32)
            return 0

        lax.fori_loop(0, buf.shape[0], one, 0)

    clear(waves[2].buf)
    clear(waves[3].buf)
    square(gt, gb, waves[2], 0)
    for copy in late:
        copy.wait()
    square(c2, gg, waves[2], blocks * n)
    ready[2] = 0.0
    stop(1.7)

    def put_tap(tap, g, acc, base):
        row = jnp.sum(acc, axis=0, keepdims=True)
        at = base + tap // SUB * n + g
        waves[3].buf[at, tap % SUB : tap % SUB + 1, :] = row

    near_base = blocks * n
    far_base = near_base + pl.cdiv(kl.shape[0], SUB) * n
    for g, width in groups:
        for i in range(7):
            first_row = max(0, 3 * (3 - i))
            last_row = min(rows, rows - 3 * (i - 3))

            def taps_row(r, acc, g=g, i=i):
                at = r + (i - 3) * 3
                return tap_sums(
                    list(acc), (lambda c: g2[g, r, c], columns), lambda c: src[g, at, c], 3
                )

            acc = lax.fori_loop(first_row, last_row, taps_row, zeros_list(7))
            for j in range(7):
                put_tap(7 * i + j, g, acc[j], far_base)
            stop(0.39)


    def dilated(r, sums):
        mask = row_mask(meta, cm, r)
        low_i, high_i = row_range(r, rows, 3, 3)
        out = []
        for g, width in groups:

            def tap_row(i, acc):
                taps = [kdb[7 * i + j, g] for j in range(7)]
                at = r + (i - 3) * 3
                return add_row(list(acc), lambda c: g2[g, at, c], taps, 3)

            acc = lax.fori_loop(low_i, high_i, tap_row, zeros_list(columns))
            value = low(mask[:, :, :width] * jnp.stack(acc)[:, :, :width])
            g1[g, r + 2, :, :, :width] = value
            out.append(sums[g] + fold(value))
        return tuple(out)

    start = tuple(jnp.zeros((SUB, width), f32) for g, width in groups)
    sums = start
    for p in range(parts * 2):
        sums = lax.fori_loop(p * (step // 2), (p + 1) * (step // 2), dilated, sums)
        stop(1.5)
    for g, width in groups:
        at = slice(g * LANE, g * LANE + width)
        mine[6:7, at] = jnp.sum(sums[g], axis=0, keepdims=True)

    def refill(r, _):
        for g, width in groups:
            src[g, r, :, :, :width] = pixels3(gl[r, :, g * LANE : g * LANE + width].astype(f32))
        return 0

    lax.fori_loop(0, rows, refill, 0)

    for g, width in groups:
        for i in range(5):

            def taps_row(r, acc, g=g, i=i):
                return tap_sums(
                    list(acc), (lambda c: src[g, r, c], columns), lambda c: g1[g, r + i, c], 1
                )

            acc = lax.fori_loop(0, rows, taps_row, zeros_list(5))
            for j in range(5):
                put_tap(24 - (5 * i + j), g, acc[j], near_base)
            stop(0.48)

    def local(r, sums):
        mask = row_mask(meta, cm, r)
        out = []
        for g, width in groups:
            acc = zeros_list(columns)
            for i in range(5):
                taps = [klb[5 * i + j, g] for j in range(5)]
                acc = add_row(acc, lambda c: g1[g, r + i, c], taps, 1)
            value = mask[:, :, :width] * jnp.stack(acc)[:, :, :width]
            at = slice(g * LANE, g * LANE + width)
            grad = (tt[r, :, at] + pixels2(value)) * sl[r, :, at]
            gg[r, :, at] = grad.astype(bf16)
            out.append(sums[g] + fold(pixels3(low(grad))))
        x = pixels3(xa[r].astype(f32))
        gb[r] = pixels2((x - mean1) * scale1 + b8(shifts, 0)).astype(bf16)
        return tuple(out)

    sums = start
    for p in range(parts * 2):
        sums = lax.fori_loop(p * (step // 2), (p + 1) * (step // 2), local, sums)
        stop(1.25)
    for g, width in groups:
        at = slice(g * LANE, g * LANE + width)
        mine[7:8, at] = jnp.sum(sums[g], axis=0, keepdims=True)
    square(gb, gg, waves[3], 0)
    ready[3] = 0.0
    stop(1.0)

    def last(b, sums):
        sums = list(sums)
        tall = gg[pl.ds(b * (step // 2), step // 2)].reshape(step // 2 * px, channels)
        product = dot_nt(tall, w_in[...])
        for k in range(step // 2):
            r = b * (step // 2) + k
            x = pixels3(xa[r].astype(f32))
            grad = pixels3(gm[r])
            gn1 = pixels3(product[k * px : (k + 1) * px]) + b8(scales, 1) * grad
            gm[r] = pixels2(grad + scale1 * gn1)
            hat = (x - mean1) * rstd1
            sums[0] = sums[0] + fold(gn1)
            sums[1] = sums[1] + fold(gn1 * hat)
        return tuple(sums)

    sums = (zero, zero)
    for p in range(parts * 2):
        sums = lax.fori_loop(p, p + 1, last, sums)
        stop(0.8)
    for k in range(2):
        mine[k : k + 1, :] = jnp.sum(sums[k], axis=0, keepdims=True)
    total_sum = AllSum(stages, mine, rest)
    total_sum.start(0)
    total_sum.end(0)
    stop(1.3)
    for k in range(1, len(stages)):
        total_sum.start(k)
        if k == 1:
            unalign(gm, meta, gw)
            moves.append(to_other(gw, mixq_o, 2))
            own_rows = gw.at[pl.ds(core * band, band)]
            moves.append(pltpu.make_async_copy(own_rows, mixo_o, move_sem.at[4]))
            for copy in moves[1:]:
                copy.start()
        total_sum.end(k)
        stop(3.0)
    sums_o[...] = mine[...]
    pair_base = 0
    for w, (_, tiles) in enumerate(plan):
        while done[w] < waves[w].steps:
            take(w)
        at = pl.ds(pair_base, tiles // 2)
        moves.append(pltpu.make_async_copy(full.at[at], full_o.at[at], move_sem.at[5 + w]))
        moves[-1].start()
        pair_base += tiles // 2
    for copy in moves:
        copy.wait()


def mixer_back(reach, stages, plan, band, gn, bn, xa, ca, gl, sl, c1, c2, gp, tiles, nat, meta, count,
               sums1, sums2, sums3, scales, shifts, w_in, w_gate, w_out, kl, kd):
    rows, px, channels = xa.shape
    columns = px // SUB
    n = len(groups_of(channels))
    small = (rows, px, channels)
    shape = jax.ShapeDtypeStruct
    pairs = sum(tiles // 2 for _, tiles in plan)
    waves = []
    for k, (order, count_tiles) in enumerate(plan):
        early = early_tiles(order, count_tiles) if k < 2 else count_tiles
        waves.append(pltpu.VMEM((early, SUB, LANE), f32))
        waves += wave_scratch(order, count_tiles, EARLY if k < 2 else 0)
    half = shape((band, columns, SUB, channels), f32)
    return pl.pallas_call(
        functools.partial(back_kernel, reach, stages, plan),
        name="mixer_back",
        out_shape=[
            half,
            half,
            half,
            shape((pairs, 2 * SUB, LANE), bf16),
            shape((8, channels), f32),
        ],
        in_specs=[ANY] * 11 + [VMEM] * 12,
        out_specs=[ANY] * 4 + [VMEM],
        scratch_shapes=[
            pltpu.VMEM((columns, SUB, channels), f32),
            pltpu.VMEM((25, n, SUB, LANE), f32),
            pltpu.VMEM((49, n, SUB, LANE), f32),
        ]
        + [pltpu.VMEM(small, k) for k in (f32,) * 3 + (bf16,) * 8]
        + [
            pltpu.VMEM((n, rows, columns, SUB, LANE), f32),
            pltpu.VMEM((n, rows + 4, columns, SUB, LANE), f32),
            pltpu.VMEM((n, rows, columns, SUB, LANE), f32),
            pltpu.VMEM((2 * band, columns, SUB, channels), f32),
            pltpu.VMEM((pairs, 2 * SUB, LANE), bf16),
            pltpu.SemaphoreType.DMA((3, 9)),
            pltpu.SemaphoreType.DMA((5 + len(plan),)),
        ]
        + sum_scratch(stages, (8, channels))
        + waves,
        compiler_params=pltpu.CompilerParams(
            collective_id=4, has_side_effects=True, vmem_limit_bytes=63 * MIB
        ),
    )(gn, bn.reshape(rows, columns, SUB, channels), xa, ca, gl, sl, c1, c2, gp, tiles, nat, meta,
      count, sums1, sums2, sums3, scales,
      shifts, w_in, w_gate, w_out, kl, kd)


def unalign(al, meta, out):
    rows, px, channels = al.shape
    offsets = out.shape[0] - rows + 1
    for at in range(out.shape[0]):
        value = jnp.zeros((px // SUB, SUB, channels), f32)
        for t in range(offsets):
            if 0 <= at - t < rows:
                chosen = (meta[0] == float(t))[None]
                value = jnp.where(chosen, pixels3(al[at - t]), value)
        out[at] = value


def tiles_out(full, base, ref):
    rows, width = ref.shape
    groups = groups_of(width)
    n, blocks = len(groups), rows // SUB
    period = 1 if n % 2 == 0 else 2

    def block(b, _):
        for k in range(period):
            for g, wide in groups:
                tile = k * n + g
                pair = base // 2 + b * (period * n // 2) + tile // 2
                value = full[pair].astype(f32)[tile % 2 * SUB : (tile % 2 + 1) * SUB]
                at = pl.ds(pl.multiple_of((b * period + k) * SUB, SUB), SUB)
                ref[at, g * LANE : g * LANE + wide] = value[:, :wide]
        return 0

    lax.fori_loop(0, blocks // period, block, 0)
    for b in range(blocks // period * period, pl.cdiv(rows, SUB)):
        count = min(SUB, rows - b * SUB)
        for g, wide in groups:
            tile = base + b * n + g
            value = full[tile // 2].astype(f32)[tile % 2 * SUB : tile % 2 * SUB + count]
            ref[b * SUB : b * SUB + count, g * LANE : g * LANE + wide] = value[:, :wide]


def finish_kernel(
    bases, x_i, mixo, mixq, nat, resq, meta, count, sums1, sums4, scales, full,
    in_o, res_o, *rest,
):
    n = len(bases)
    grads, (x, mix, res, cm), grad_s = rest[:n], rest[n : n + 4], rest[n + 4 : -3]
    in_sem, out_sem, grad_sem = rest[-3:]
    band, columns = x.shape[:2]
    core = lax.axis_index("rows")
    mine = pl.ds(pl.multiple_of(core * SUB, SUB), SUB)
    other = pl.ds(pl.multiple_of((1 - core) * SUB, SUB), SUB)

    def loads(r):
        pairs = [
            (x_i.at[r], x.at[r]),
            (mixo.at[r], mix.at[r, :, mine]),
            (mixq.at[r], mix.at[r, :, other]),
            (nat.at[core * band + r], res.at[r, :, mine]),
            (resq.at[r], res.at[r, :, other]),
        ]
        return [pltpu.make_async_copy(a, b, in_sem.at[r, k]) for k, (a, b) in enumerate(pairs)]

    def stores(r):
        pairs = [(mix.at[r], in_o.at[r]), (res.at[r], res_o.at[r])]
        return [pltpu.make_async_copy(a, b, out_sem.at[r, k]) for k, (a, b) in enumerate(pairs)]

    def begin(r, _):
        for copy in loads(r):
            copy.start()
        return 0

    lax.fori_loop(0, band, begin, 0)
    size, top = meta[1], meta[0]
    for c in range(columns):
        cm[c] = (size > c).astype(f32)
    copies = []
    for k, (ref, base) in enumerate(zip(grad_s, bases)):
        tiles_out(full, base, ref)
        copies.append(pltpu.make_async_copy(ref, grads[k], grad_sem.at[k]))
        copies[-1].start()
    total = count[0:1, 0:1]
    mean = sums1[0:1, :] / total
    rstd = lax.rsqrt(sums1[1:2, :] / total - mean * mean + epsilon)
    scale = rstd * scales[0:1, :]
    back0, back1 = sums4[0:1, :] / total, sums4[1:2, :] / total
    spread = lambda v: jnp.broadcast_to(v, size.shape)
    mean, rstd, scale, back0, back1 = (spread(v) for v in (mean, rstd, scale, back0, back1))

    def row(r, _):
        for copy in loads(r):
            copy.wait()
        at = (r * 1).astype(f32)
        inside = ((at >= top) & (at < top + size)).astype(f32)
        mask = cm[...] * inside[None]
        hat = (mask * x[r].astype(f32) - mean) * rstd
        mix[r] = mask * (mix[r] - scale * (back0 + hat * back1))
        for copy in stores(r):
            copy.start()
        return 0

    lax.fori_loop(0, band, row, 0)

    def end(r, _):
        for copy in stores(r):
            copy.wait()
        return 0

    lax.fori_loop(0, band, end, 0)
    for copy in copies:
        copy.wait()


def finish(x, mixo, mixq, nat, resq, meta, count, sums1, sums4, scales, full, shapes, bases):
    band, columns, images, channels = x.shape
    shape = jax.ShapeDtypeStruct
    return pl.pallas_call(
        functools.partial(finish_kernel, bases),
        name="finish",
        in_specs=[ANY] * 5 + [VMEM] * 6,
        out_specs=[ANY] * (2 + len(shapes)),
        scratch_shapes=[
            pltpu.VMEM(x.shape, bf16),
            pltpu.VMEM(x.shape, f32),
            pltpu.VMEM(x.shape, f32),
            pltpu.VMEM((columns, images, channels), f32),
        ]
        + [pltpu.VMEM(s, f32) for s in shapes]
        + [
            pltpu.SemaphoreType.DMA((band, 5)),
            pltpu.SemaphoreType.DMA((band, 2)),
            pltpu.SemaphoreType.DMA((len(shapes),)),
        ],
        out_shape=[shape(x.shape, f32)] * 2 + [shape(s, f32) for s in shapes],
        compiler_params=pltpu.CompilerParams(vmem_limit_bytes=62 * MIB),
    )(x, mixo, mixq, nat, resq, meta, count, sums1, sums4, scales, full)


def on_device(sizes, inputs, cotangent, scales, shifts, hidden_shift, w_inward, w_gating,
              w_outward, w_expand, w_reduce, kernel_local, kernel_dilated, kernel_hidden,
              image_size, band_split, slot_image):
    images, band, columns, channels = inputs.shape
    half = images // 2
    px = columns * half
    core = lax.axis_index("rows")
    counted = jnp.sum(image_size * image_size).astype(f32)
    count = jnp.full((SUB, LANE), counted)
    everyone = jnp.arange(image_size.shape[0], dtype=jnp.int32)
    chosen = (slot_image[:, None] == everyone[None, :]).astype(jnp.int32)
    extent = jnp.sum(chosen * image_size[None, :], axis=1)
    top = band - jnp.sum(chosen * band_split[None, :], axis=1)
    start = jnp.clip(top, 0, 2 * band - columns)
    own_meta = jnp.stack([top - core * band, extent]).astype(f32)
    own_meta = jnp.broadcast_to(own_meta[:, :, None], (2, images, channels))
    meta = jnp.stack([start, top - start, extent]).astype(f32)
    meta = lax.dynamic_slice_in_dim(meta, core * half, half, axis=1)
    meta = jnp.broadcast_to(meta[:, :, None], (3, half, channels))

    x = jnp.transpose(inputs, (1, 2, 0, 3))
    y = jnp.transpose(cotangent, (1, 2, 0, 3))
    stages = stage_list(sizes)
    xa, ca, gl, sl, c1, c2, gp, bn, sums1, sums2 = mixer_forward(
        stages, x, y, own_meta, meta, count, scales, shifts, w_inward, w_gating, w_outward,
        kernel_local, kernel_dilated,
    )
    hidden = w_expand.shape[1]
    plan = wave_plan(sizes, channels, hidden)
    half_tiles = plan[0][1]
    nat, gn, tiles, sums3 = hidden_block(
        stages, plan, band, xa, ca, bn, meta, count, sums2, scales, shifts,
        hidden_shift, w_expand, w_reduce.T, kernel_hidden,
    )
    mixo, mixq, resq, full, sums4 = mixer_back(
        reach_list(sizes), stages, plan, band, gn, bn, xa, ca, gl, sl, c1, c2, gp, tiles, nat, meta, count,
        sums1, sums2, sums3, scales, shifts, w_inward, w_gating, w_outward, kernel_local,
        kernel_dilated,
    )
    square, wide = (channels, channels), (channels, hidden)
    blocks, n = channels // SUB, len(groups_of(channels))
    tap_tile, bias_tile, _ = hidden_tiles(channels, hidden)
    second = 2 * half_tiles
    third = second + plan[2][1]
    near = third + blocks * n
    far = near + pl.cdiv(kernel_local.shape[0], SUB) * n
    targets = [
        (wide, 0),
        (wide, tap_tile // 2),
        (kernel_hidden.shape, tap_tile),
        (hidden_shift.shape, bias_tile),
        (square, second),
        (square, second + blocks * n),
        (square, third),
        (kernel_local.shape, near),
        (kernel_dilated.shape, far),
    ]
    input_grad, result, gwe, gwr, gk, gh, gwo, gwg, gwi, gkl, gkd = finish(
        x, mixo, mixq, nat, resq, own_meta, count, sums1, sums4, scales, full,
        [t[0] for t in targets], [t[1] for t in targets],
    )
    scales_grad = jnp.stack([sums4[1], sums4[2], sums3[1], sums3[3]])
    shifts_grad = jnp.stack(
        [sums4[0], sums4[7], sums4[6], sums4[5], sums4[4], sums4[3], sums3[0], sums3[2]]
    )
    back = lambda v: jnp.transpose(v, (2, 0, 1, 3))
    return (
        back(result), back(input_grad), scales_grad, shifts_grad, gh, gwi, gwg, gwo, gwe, gwr.T,
        gkl, gkd, gk,
    )


def solution(mesh):
    wide = P("imgs", "rows", None, None)
    sizes = dict(mesh.shape)
    return jax.shard_map(
        functools.partial(on_device, sizes),
        mesh=mesh,
        in_specs=(wide, wide) + (P(),) * 13 + (P("imgs"),),
        out_specs=(wide, wide) + (P(),) * 11,
        check_vma=False,
    )
```

```python
import functools
import math

import jax
import jax.numpy as jnp
from jax import lax
from jax.experimental import pallas as pl
from jax.experimental.pallas import tpu as pltpu
from jax.sharding import PartitionSpec as P

MESH = pl.DeviceIdType.MESH
epsilon = 1e-05
bf16 = jnp.bfloat16
f32 = jnp.float32
SUB = 8
LANE = 128
MIB = 1 << 20
ANY = pl.BlockSpec(memory_space=pl.ANY)
VMEM = pl.BlockSpec(memory_space=pltpu.VMEM)


def low(values):
    return values.astype(bf16).astype(f32)


def normal_parts(v):
    bell = jnp.exp2((-0.5 * 1.4426950408889634) * (v * v))
    return 0.5 + 0.5 * lax.erf(v * 0.7071067811865476), bell * 0.3989422804014327


def dot(a, b):
    return jnp.dot(a, b, preferred_element_type=f32)


def dot_nt(a, b):
    return lax.dot_general(a, b, (((1,), (1,)), ((), ())), preferred_element_type=f32)


def dot_tn(a, b):
    return lax.dot_general(a, b, (((0,), (0,)), ((), ())), preferred_element_type=f32)


def groups_of(channels):
    return [(g, min(LANE, channels - g * LANE)) for g in range(pl.cdiv(channels, LANE))]


def spread_taps(k_ref, kb, flip=False):
    count, channels = k_ref.shape
    for tap in range(count):
        from_tap = count - 1 - tap if flip else tap
        row = jnp.broadcast_to(k_ref[from_tap : from_tap + 1, :], (SUB, channels))
        for g, width in groups_of(channels):
            kb[tap, g, :, :width] = row[:, g * LANE : g * LANE + width]


def add_row(acc, load, taps, dilation):
    columns, half = len(acc), len(taps) // 2
    for c in range(columns):
        value = load(c)
        for j, tap in enumerate(taps):
            at = c - (j - half) * dilation
            if 0 <= at < columns:
                acc[at] = acc[at] + tap * value
    return acc


def tap_sums(acc, load_fixed, load_moved, dilation):
    columns, half = load_fixed[1], len(acc) // 2
    fixed = [load_fixed[0](c) for c in range(columns)]
    for c in range(columns):
        value = load_moved(c)
        for j in range(len(acc)):
            at = c - (j - half) * dilation
            if 0 <= at < columns:
                acc[j] = acc[j] + fixed[at] * value
    return acc


def row_range(r, rows, half, dilation):
    low_i = jnp.maximum(half - r // dilation, 0)
    high_i = jnp.minimum(half + (rows - 1 - r) // dilation, 2 * half)
    return low_i, high_i + 1


def zeros_list(count):
    return [jnp.zeros((SUB, LANE), f32) for _ in range(count)]


def b8(ref, i):
    return jnp.broadcast_to(ref[i : i + 1, :], (SUB, ref.shape[1]))


def make_col_mask(meta, cm):
    size = meta[2]
    for c in range(cm.shape[0]):
        cm[c] = (size > c).astype(f32)


def row_mask(meta, cm, r):
    at = (r * 1).astype(f32)
    inside = (at >= meta[1]) & (at < meta[1] + meta[2])
    return cm[...] * inside.astype(f32)[None]


def pixels3(values):
    return values.reshape(values.shape[0] // SUB, SUB, values.shape[1])


def pixels2(values):
    return values.reshape(values.shape[0] * SUB, values.shape[2])


def fold(values):
    return jnp.sum(values, axis=0)


def statistics(sums, count, i):
    mean = b8(sums, i) / count
    return mean, lax.rsqrt(b8(sums, i + 1) / count - mean * mean + epsilon)


def stage_list(sizes):
    stages = [("rows", 1, sizes["rows"])]
    left, stride = sizes["imgs"], 1
    while left > 1:
        size = 4 if left % 4 == 0 else (2 if left % 2 == 0 else left)
        stages.append(("imgs", stride, size))
        left, stride = left // size, stride * size
    return [s for s in stages if s[2] > 1]


def reach_list(sizes):
    return [("rows", 1, sizes["rows"]), ("imgs", 1, sizes["imgs"])]


def stage_peers(stages):
    core = lax.axis_index("rows")
    chip = lax.axis_index("imgs")
    found = []
    for axis, stride, size in stages:
        index = core if axis == "rows" else chip
        place = lax.rem(index // stride, size)
        peers = []
        for step in range(1, size):
            other = lax.rem(place + step, size)
            at = index + (other - place) * stride
            peers.append((step, other, (at, chip) if axis == "rows" else (core, at)))
        found.append((place, peers))
    return found


def say_here(found):
    barrier = pltpu.get_barrier_semaphore()
    for _, peers in found:
        for _, _, device in peers:
            pl.semaphore_signal(barrier, inc=1, device_id=device, device_id_type=MESH)


def wait_all_here(found):
    pl.semaphore_wait(pltpu.get_barrier_semaphore(), sum(len(peers) for _, peers in found))


def greet(found):
    say_here(found)
    wait_all_here(found)


def remote(src, dst, send, recv, device):
    return pltpu.make_async_remote_copy(
        src_ref=src, dst_ref=dst, send_sem=send, recv_sem=recv,
        device_id=device, device_id_type=MESH,
    )


class AllSum:
    def __init__(self, stages, mine, rest):
        self.found, self.mine = stage_peers(stages), mine
        n = len(stages)
        self.slots, self.sems = rest[:n], rest[n : 3 * n]

    def start(self, k):
        slot, (send, recv) = self.slots[k], self.sems[2 * k : 2 * k + 2]
        self.copies = []
        for step, _, device in self.found[k][1]:
            at = step - 1
            self.copies.append(remote(self.mine, slot.at[at], send.at[at], recv.at[at], device))
            self.copies[-1].start()

    def end(self, k):
        for copy in self.copies:
            copy.wait()
        total = self.mine[...]
        for step, _, _ in self.found[k][1]:
            total = total + self.slots[k][step - 1]
        self.mine[...] = total


def all_sum(stages, mine, rest):
    total = AllSum(stages, mine, rest)
    for k in range(len(stages)):
        total.start(k)
        total.end(k)


def sum_scratch(stages, table):
    sems = []
    for _, _, size in stages:
        sems += [pltpu.SemaphoreType.DMA((size - 1,))] * 2
    slots = [pltpu.VMEM((size - 1,) + table, f32) for _, _, size in stages]
    return [pltpu.VMEM(table, f32)] + slots + sems


def mixer_kernel(
    stages, x_i, y_i, sizes, splits, slots, scales, shifts, w_in, w_gate, w_out, kl, kd,
    xa_o, ca_o, gl_o, sl_o, c1_o, c2_o, gp_o, bn_o, sums1_o, sums_o, own_meta, meta, count,
    cm, klb, kdb, xa, ca, gl, sl, c1, c2, gp, bn, gf, c1f, sem,
    own_cm, xs, ys, xw, cw, move_sem, mine, *rest,
):
    found = stage_peers(stages)
    say_here(found)
    rows, px, channels = xa.shape
    columns = px // SUB
    groups = groups_of(channels)
    offsets = xw.shape[0] - rows + 1
    core, chip = lax.axis_index("rows"), lax.axis_index("imgs")
    band = x_i.shape[0]
    upper = core == 0
    place_images(sizes, splits, slots, core, band, columns, own_meta, meta, count)
    size, top = own_meta[1], own_meta[0]
    for c in range(columns):
        own_cm[c] = (size > c).astype(f32)

    def split(value, full, out, r):
        a, b = value[:, :SUB], value[:, SUB:]
        full[core * band + r] = pixels2(jnp.where(upper, a, b)).astype(bf16)
        out[r] = pixels2(jnp.where(upper, b, a)).astype(bf16)

    def split_x(r, sums):
        at = (r * 1).astype(f32)
        inside = ((at >= top) & (at < top + size)).astype(f32)
        value = x_i[r].astype(f32)
        split(value, xw, xs, r)
        value = own_cm[...] * inside[None] * value
        return sums[0] + fold(value), sums[1] + fold(value * value)

    def split_y(r, _):
        split(y_i[r].astype(f32), cw, ys, r)
        return 0

    def to_other(out, full, k):
        at = pl.ds(core * band, band)
        return remote(out, full.at[at], move_sem.at[k], move_sem.at[k + 1], (1 - core, chip))

    zero = jnp.zeros((2 * SUB, channels), f32)
    sums = lax.fori_loop(0, band, split_x, (zero, zero))
    for k in range(2):
        mine[k : k + 1, :] = jnp.sum(sums[k], axis=0, keepdims=True)
    wait_all_here(found)
    moves = [to_other(xs, xw, 0), to_other(ys, cw, 2)]
    first_sum = AllSum(stages, mine, rest)
    first_sum.start(0)
    moves[0].start()
    lax.fori_loop(0, band, split_y, 0)
    moves[1].start()
    first_sum.end(0)
    first_sum.start(1)
    make_col_mask(meta, cm)
    spread_taps(kl, klb)
    spread_taps(kd, kdb)
    for edge in (0, 1, rows + 2, rows + 3):
        gf[:, edge] = jnp.zeros(gf.shape[:1] + gf.shape[2:], f32)
    first_sum.end(1)
    for k in range(2, len(stages)):
        first_sum.start(k)
        first_sum.end(k)
    sums1_o[...] = mine[...]
    for copy in moves:
        copy.wait()
    total = count[0:1, 0:1]
    mean, rstd = statistics(sums1_o, total, 0)
    scale = rstd * b8(scales, 0)
    starts = [meta[0] == float(t) for t in range(offsets)]

    def aligned(ref, r):
        value = pixels3(ref[r].astype(f32))
        for t in range(1, offsets):
            value = jnp.where(starts[t][None], pixels3(ref[r + t].astype(f32)), value)
        return value

    tall_rows = 3

    def first(b, _):
        parts, masks = [], []
        for k in range(tall_rows):
            r = b * tall_rows + k
            mask = row_mask(meta, cm, r)
            x = mask * aligned(xw, r)
            xa[r] = pixels2(x).astype(bf16)
            ca[r] = pixels2(mask * aligned(cw, r)).astype(bf16)
            parts.append(pixels2((x - mean) * scale + b8(shifts, 0)).astype(bf16))
        product = dot(jnp.concatenate(parts, axis=0), w_in[...])
        for k in range(tall_rows):
            r = b * tall_rows + k
            mask = row_mask(meta, cm, r)
            pre = pixels3(product[k * px : (k + 1) * px]) + b8(shifts, 1)
            phi_sum, bell = normal_parts(pre)
            gelu = mask * low(pre * phi_sum)
            sl[r] = pixels2(phi_sum + pre * bell)
            gl[r] = pixels2(gelu).astype(bf16)
            for g, width in groups:
                gf[g, r + 2, :, :, :width] = gelu[:, :, g * LANE : g * LANE + width]
        return 0

    lax.fori_loop(0, rows // tall_rows, first, 0)
    early = [(xa, xa_o), (ca, ca_o), (gl, gl_o), (sl, sl_o)]
    copies = [pltpu.make_async_copy(a, b, sem.at[k]) for k, (a, b) in enumerate(early)]
    for copy in copies:
        copy.start()

    def local(r, _):
        mask = row_mask(meta, cm, r)
        for g, width in groups:
            acc = zeros_list(columns)
            for i in range(5):
                taps = [klb[5 * i + j, g] for j in range(5)]
                acc = add_row(acc, lambda c: gf[g, r + i, c], taps, 1)
            bias = b8(shifts, 2)[:, g * LANE : g * LANE + width]
            value = jnp.stack(acc)[:, :, :width] + bias
            value = mask[:, :, :width] * low(value)
            c1f[g, r, :, :, :width] = value
            c1[r, :, g * LANE : g * LANE + width] = pixels2(value).astype(bf16)
        return 0

    lax.fori_loop(0, rows, local, 0)
    copies.append(pltpu.make_async_copy(c1, c1_o, sem.at[4]))
    copies[-1].start()

    def dilated(r, _):
        low_i, high_i = row_range(r, rows, 3, 3)
        for g, width in groups:

            def tap_row(i, acc):
                taps = [kdb[7 * i + j, g] for j in range(7)]
                at = r + (i - 3) * 3
                return add_row(list(acc), lambda c: c1f[g, at, c], taps, 3)

            acc = lax.fori_loop(low_i, high_i, tap_row, zeros_list(columns))
            bias = b8(shifts, 3)[:, g * LANE : g * LANE + width]
            value = jnp.stack(acc)[:, :, :width] + bias
            c2[r, :, g * LANE : g * LANE + width] = pixels2(value).astype(bf16)
        return 0

    lax.fori_loop(0, rows, dilated, 0)
    copies.append(pltpu.make_async_copy(c2, c2_o, sem.at[5]))
    copies[-1].start()

    def last(b, sums):
        sums = list(sums)
        tall = c2[pl.ds(b * tall_rows, tall_rows)].reshape(tall_rows * px, channels)
        gates = dot(tall, w_gate[...])
        parts = []
        for k in range(tall_rows):
            r = b * tall_rows + k
            gate = pixels3(gates[k * px : (k + 1) * px]) + b8(shifts, 4)
            gate = pixels2(gate)
            gp[r] = gate
            parts.append((gl[r].astype(f32) * gate).astype(bf16))
        branches = dot(jnp.concatenate(parts, axis=0), w_out[...])
        for k in range(tall_rows):
            r = b * tall_rows + k
            mask = row_mask(meta, cm, r)
            x = pixels3(xa[r].astype(f32))
            normed = low((x - mean) * scale + b8(shifts, 0))
            both = pixels3(branches[k * px : (k + 1) * px]) + b8(shifts, 5) + normed
            bn[r] = pixels2(both)
            middle = mask * (x + b8(scales, 1) * both)
            sums[0] = sums[0] + fold(middle)
            sums[1] = sums[1] + fold(middle * middle)
        return tuple(sums)

    zero = jnp.zeros((SUB, channels), f32)
    sums = lax.fori_loop(0, rows // tall_rows, last, (zero, zero))
    copies.append(pltpu.make_async_copy(gp, gp_o, sem.at[6]))
    copies[-1].start()
    copies.append(pltpu.make_async_copy(bn, bn_o, sem.at[7]))
    copies[-1].start()
    for k in range(2):
        mine[k : k + 1, :] = jnp.sum(sums[k], axis=0, keepdims=True)
    all_sum(stages, mine, rest[3 * len(stages) :])
    sums_o[...] = mine[...]
    for copy in copies:
        copy.wait()


def mixer_forward(
    stages, x, y, sizes, splits, slots, scales, shifts, w_in, w_gate, w_out, kl, kd
):
    band, columns, images, channels = x.shape
    px = columns * SUB
    rows = columns
    n = len(groups_of(channels))
    small = (rows, px, channels)
    kinds = (bf16, bf16, bf16, f32, bf16, bf16, f32, f32)
    return pl.pallas_call(
        functools.partial(mixer_kernel, stages),
        name="mixer_forward",
        out_shape=[jax.ShapeDtypeStruct(small, k) for k in kinds]
        + [jax.ShapeDtypeStruct((2, channels), f32)] * 2
        + [
            jax.ShapeDtypeStruct((2, images, channels), f32),
            jax.ShapeDtypeStruct((3, SUB, channels), f32),
            jax.ShapeDtypeStruct((SUB, LANE), f32),
        ],
        in_specs=[VMEM] * 12,
        out_specs=[ANY] * 8 + [VMEM] * 5,
        scratch_shapes=[
            pltpu.VMEM((columns, SUB, channels), f32),
            pltpu.VMEM((25, n, SUB, LANE), f32),
            pltpu.VMEM((49, n, SUB, LANE), f32),
        ]
        + [pltpu.VMEM(small, k) for k in kinds]
        + [
            pltpu.VMEM((n, rows + 4, columns, SUB, LANE), f32),
            pltpu.VMEM((n, rows, columns, SUB, LANE), f32),
            pltpu.SemaphoreType.DMA((8,)),
            pltpu.VMEM((columns, images, channels), f32),
            pltpu.VMEM((band, px, channels), bf16),
            pltpu.VMEM((band, px, channels), bf16),
            pltpu.VMEM((2 * band, px, channels), bf16),
            pltpu.VMEM((2 * band, px, channels), bf16),
            pltpu.SemaphoreType.DMA((4,)),
        ]
        + sum_scratch(stages, (2, channels))
        + sum_scratch(stages, (2, channels))[1:],
        compiler_params=pltpu.CompilerParams(
            collective_id=2, has_side_effects=True, vmem_limit_bytes=62 * MIB
        ),
    )(x, y, sizes, splits, slots, scales, shifts, w_in, w_gate, w_out, kl, kd)


def place_images(sizes, splits, slots, core, band, columns, own_meta, meta, count):
    images, channels = own_meta.shape[1:]
    size = sizes[...].astype(f32)
    total = jnp.sum(size * size, axis=1, keepdims=True)
    count[...] = jnp.broadcast_to(total, count.shape)
    shape = (images, images)
    rows, cols = (lax.broadcasted_iota(jnp.int32, shape, k) for k in range(2))
    spread = jnp.broadcast_to(slots[...].astype(f32), shape)
    column = jnp.sum(jnp.where(rows == cols, spread, 0.0), axis=1, keepdims=True)
    shape = (images, size.shape[1])
    image = lax.broadcasted_iota(jnp.int32, shape, 1).astype(f32)
    chosen = image == jnp.broadcast_to(column, shape)

    def pick(row):
        value = jnp.where(chosen, jnp.broadcast_to(row, shape), 0.0)
        value = jnp.sum(value, axis=1, keepdims=True)
        return jnp.broadcast_to(value, (images, channels))

    extent = pick(size)
    top = float(band) - pick(splits[...].astype(f32))
    own_meta[0] = top - (core * band).astype(f32)
    own_meta[1] = extent
    half = lambda v: jnp.where(core == 0, v[:SUB], v[SUB:])
    top, extent = half(top), half(extent)
    start = jnp.clip(top, 0.0, float(2 * band - columns))
    meta[0] = start
    meta[1] = top - start
    meta[2] = extent


class Wave:
    def __init__(self, order, tiles, refs, buf, base=0, full=None, pair_base=0, done=0):
        self.order, self.found = order, stage_peers(order)
        self.buf, self.base, self.full, self.pair_base = buf, base, full, pair_base
        n = len(order)
        self.slots, self.sems = refs[:n], refs[n:]
        self.start, self.length, self.origin = 0, tiles, 0
        self.shares, self.copies, self.done = [], [], done
        for k in range(done):
            self.take(k)
        self.origin = self.start

    @property
    def steps(self):
        return 2 * len(self.order) + 1

    def take(self, k):
        self.length //= self.order[k][2]
        self.start = self.start + self.found[k][0] * self.length
        self.shares.append((self.start, self.length))

    def wait(self):
        for copy in self.copies:
            copy.wait()
        self.copies = []

    def at(self, tile):
        return self.base + tile - self.origin

    def add(self, k):
        self.wait()
        self.take(k)
        size = math.gcd(self.length, 16)
        start, buf, slot = self.at(self.start), self.buf, self.slots[k]
        count = len(self.found[k][1])

        def some(t, _):
            at = pl.ds(start + t * size, size)
            total = buf[at]
            for i in range(count):
                total = total + slot[i, pl.ds(t * size, size)]
            buf[at] = total
            return 0

        lax.fori_loop(0, self.length // size, some, 0)

    def scatter(self, k):
        share = self.length // self.order[k][2]
        send, recv = self.sems[4 * k : 4 * k + 2]
        for step, other, device in self.found[k][1]:
            src = self.buf.at[pl.ds(self.at(self.start + other * share), share)]
            at = step - 1
            self.copies.append(remote(src, self.slots[k].at[at], send.at[at], recv.at[at], device))
            self.copies[-1].start()

    def round(self):
        start, buf, full = self.at(self.start), self.buf, self.full
        first = self.pair_base + self.start // 2

        def one(p, _):
            both = jnp.concatenate([buf[start + 2 * p], buf[start + 2 * p + 1]], axis=0)
            full[first + p] = both.astype(bf16)
            return 0

        lax.fori_loop(0, self.length // 2, one, 0)

    def part(self, k):
        start, length = self.shares[k]
        return self.full.at[pl.ds(self.pair_base + start // 2, length // 2)]

    def gather(self, k):
        send, recv = self.sems[4 * k + 2 : 4 * k + 4]
        here = self.part(k)
        for step, _, device in self.found[k][1]:
            at = step - 1
            self.copies.append(remote(here, here, send.at[at], recv.at[at], device))
            self.copies[-1].start()

    def guess(self, i):
        n = len(self.order)
        if i >= 2 * n:
            return 0.0
        k = i if i < n else 2 * n - 1 - i
        axis, _, size = self.order[k]
        share = self.length // size if i < n else self.shares[k][1] / 2
        if axis == "rows":
            return 1.5 + share * 0.008
        links = {2: 2, 4: 8}.get(size, 16)
        return LATENCY + links * share * PER_TILE

    def step(self, i):
        n = len(self.order)
        self.wait()
        if self.done < i <= n:
            self.add(i - 1)
        if i < n:
            self.scatter(i)
        elif i < 2 * n:
            if i == n:
                self.round()
            self.gather(2 * n - 1 - i)


def wave_scratch(order, tiles, first=0, last=None):
    last = len(order) if last is None else last
    slots, sems, length = [], [], tiles
    for k, (_, _, size) in enumerate(order):
        length //= size
        used = first <= k < last
        slots.append(pltpu.VMEM((size - 1, length if used else 1, SUB, LANE), f32))
        sems += [pltpu.SemaphoreType.DMA((size - 1,))] * 4
    return slots + sems


def wave_refs(order):
    return 5 * len(order)


LATENCY, PER_TILE = 3.0, 0.065
EARLY = 2


def early_tiles(order, tiles):
    return tiles // math.prod(size for _, _, size in order[:EARLY])


def hidden_kernel(
    stages, plan, xa, ca, bn, meta, count, sums2, scales, shifts, hshift, w_e, w_rt, kh,
    nat_o, gn_o, tiles_o, sums_o,
    cm, khb, kfb, n2, gr, ha, ge, em, gc, kacc, wet, wr, res, nat, gn_s, tiles, sem, mine, *rest,
):
    found = stage_peers(stages)
    say_here(found)
    tail, waves = list(rest[3 * len(stages) :]), []
    for k, (order, count_tiles) in enumerate(plan[:2]):
        refs, tail = tail[: wave_refs(order)], tail[wave_refs(order) :]
        waves.append(Wave(order, count_tiles, refs, tiles, base=k * count_tiles))
    rows, px, channels = xa.shape
    columns = px // SUB
    hidden = w_e.shape[1]
    wide = em.shape[0] * LANE
    parts = em.shape[0]
    wide_step = 6
    groups = hidden // LANE
    tap_tile, bias_tile, last_tile = hidden_tiles(channels, hidden)
    for t in range(tap_tile, last_tile):
        tiles[t] = jnp.zeros((SUB, LANE), f32)
    make_col_mask(meta, cm)
    spread_taps(kh, khb)
    spread_taps(kh, kfb, flip=True)
    for edge in (0, rows + 1):
        em[:, edge] = jnp.zeros(em.shape[:1] + em.shape[2:], f32)
        gc[:, edge] = jnp.zeros(gc.shape[:1] + gc.shape[2:], f32)
    wet[...] = w_e[...].astype(f32).T.astype(bf16)
    wr[...] = w_rt[...].astype(f32).T.astype(bf16)
    total = count[0:1, 0:1]
    mean, rstd = statistics(sums2, total, 0)
    scale = rstd * b8(scales, 2)

    def middle_of(r):
        return pixels3(xa[r].astype(f32)) + b8(scales, 1) * pixels3(bn[r])

    def prepare(r, acc):
        normed = (middle_of(r) - mean) * scale + b8(shifts, 6)
        n2[r] = pixels2(normed).astype(bf16)
        grad = (b8(scales, 3) * pixels3(ca[r].astype(f32))).astype(bf16)
        gr[r] = pixels2(grad)
        return acc + fold(grad.astype(f32))

    zero = jnp.zeros((SUB, channels), f32)
    grad_sum = lax.fori_loop(0, rows, prepare, zero)

    def chunk(f, _):
        base = pl.multiple_of(f * wide, wide)
        lanes = pl.ds(base, wide)
        group = f * parts

        def expand(b, _):
            tall = n2[pl.ds(b * wide_step, wide_step)].reshape(wide_step * px, channels)
            product = dot(tall, w_e[:, lanes])
            grads = gr[pl.ds(b * wide_step, wide_step)].reshape(wide_step * px, channels)
            grads = dot(grads, w_rt[:, lanes])
            for k in range(wide_step):
                r = b * wide_step + k
                for g in range(parts):
                    at = slice(g * LANE, (g + 1) * LANE)
                    gc[g, r + 1] = pixels3(grads[k * px : (k + 1) * px, at])
                mask = row_mask(meta, cm, r)[:, :, :LANE]
                value = product[k * px : (k + 1) * px]
                value = low(value + jnp.broadcast_to(hshift[0:1, lanes], value.shape))
                for g in range(parts):
                    em[g, r + 1] = mask * pixels3(value[:, g * LANE : (g + 1) * LANE])
            return 0

        lax.fori_loop(0, rows // wide_step, expand, 0)

        def forward(r, acc):
            out = []
            for g in range(parts):
                conv = zeros_list(columns)
                for i in range(3):
                    taps = [khb[3 * i + j, group + g] for j in range(3)]
                    conv = add_row(conv, lambda c: em[g, r + i, c], taps, 1)
                here = pl.ds(pl.multiple_of(base + g * LANE, LANE), LANE)
                v = jnp.stack(conv) + jnp.broadcast_to(hshift[1:2, here], (SUB, LANE))
                phi_sum, bell = normal_parts(v)
                ha[r, :, here] = pixels2(v * phi_sum).astype(bf16)
                back = low(gc[g, r + 1] * (phi_sum + v * bell))
                gc[g, r + 1] = back
                out.append(acc[g] + fold(back))
            return tuple(out)

        bias = lax.fori_loop(0, rows, forward, tuple(zeros_list(parts)))
        for g in range(parts):
            tiles[bias_tile + group + g, 1:2, :] = jnp.sum(bias[g], axis=0, keepdims=True)
            for tap in range(9):
                kacc[g, tap] = jnp.zeros((SUB, LANE), f32)

        def backward(r, acc):
            mask = row_mask(meta, cm, r)[:, :, :LANE]
            out = []
            for g in range(parts):
                conv = zeros_list(columns)
                for i in range(3):
                    taps = [kfb[3 * i + j, group + g] for j in range(3)]
                    sums = [kacc[g, 3 * i + j] for j in range(3)]
                    fixed = [em[g, r + 1, c] for c in range(columns)]
                    for c in range(columns):
                        value = gc[g, r + i, c]
                        for j in range(3):
                            at = c - (j - 1)
                            if 0 <= at < columns:
                                conv[at] = conv[at] + taps[j] * value
                                sums[j] = sums[j] + fixed[at] * value
                    for j in range(3):
                        kacc[g, 3 * i + j] = sums[j]
                here = pl.ds(pl.multiple_of(base + g * LANE, LANE), LANE)
                value = low(mask * jnp.stack(conv))
                ge[r, :, here] = pixels2(value).astype(bf16)
                out.append(acc[g] + fold(value))
            return tuple(out)

        bias = lax.fori_loop(0, rows, backward, tuple(zeros_list(parts)))
        for g in range(parts):
            tiles[bias_tile + group + g, 0:1, :] = jnp.sum(bias[g], axis=0, keepdims=True)
            for tap in range(9):
                at = tap_tile + (8 - tap) // SUB * groups + group + g
                row = (8 - tap) % SUB
                tiles[at, row : row + 1, :] = jnp.sum(kacc[g, tap], axis=0, keepdims=True)
        return 0

    lax.fori_loop(0, hidden // wide, chunk, 0)

    whole = rows * px
    blocks = channels // SUB
    for k, (left, right) in enumerate(((n2, ge), (gr, ha))):
        grad = dot_tn(left[...].reshape(whole, channels), right[...].reshape(whole, hidden))
        for g in range(groups):
            part = grad[:, g * LANE : (g + 1) * LANE].reshape(blocks, SUB, LANE)
            tiles[pl.ds(k * blocks * groups + g, blocks, stride=groups)] = part
    wait_all_here(found)
    for wave in waves:
        wave.step(0)

    step = 3

    def finish(b, sums):
        sums = list(sums)
        at = pl.ds(b * step, step)
        tall = step * px
        reduced_all = dot(ha[at].reshape(tall, hidden), wr[...])
        gn_all = dot(ge[at].reshape(tall, hidden), wet[...])
        for k in range(step):
            r = b * step + k
            mask = row_mask(meta, cm, r)
            reduced = pixels3(reduced_all[k * px : (k + 1) * px]) + b8(shifts, 7)
            middle = middle_of(r)
            res[r] = pixels2(mask * (middle + b8(scales, 3) * reduced))
            gn = pixels3(gn_all[k * px : (k + 1) * px])
            gn_s[r] = pixels2(gn)
            hat = (middle - mean) * rstd
            out = pixels3(ca[r].astype(f32))
            sums[0] = sums[0] + fold(gn)
            sums[1] = sums[1] + fold(gn * hat)
            sums[2] = sums[2] + fold(out * reduced)
        return tuple(sums)

    sums = lax.fori_loop(0, 2, finish, (zero, zero, zero))
    for wave in waves:
        wave.step(1)
    sums = lax.fori_loop(2, rows // step, finish, sums)
    copies = [pltpu.make_async_copy(gn_s, gn_o, sem.at[1])]
    copies[-1].start()
    for k, value in enumerate((sums[0], sums[1], grad_sum, sums[2])):
        mine[k : k + 1, :] = jnp.sum(value, axis=0, keepdims=True)
    unalign(res, meta, nat)
    copies.append(pltpu.make_async_copy(nat, nat_o, sem.at[2]))
    copies[-1].start()
    all_sum(stages, mine, rest)
    sums_o[...] = mine[...]
    for k, wave in enumerate(waves):
        wave.add(EARLY - 1)
        at = pl.ds(wave.at(wave.start), wave.length)
        here = pl.ds(k * wave.length, wave.length)
        copies.append(pltpu.make_async_copy(tiles.at[at], tiles_o.at[here], sem.at[k and 3]))
        copies[-1].start()
    for copy in copies:
        copy.wait()


def hidden_tiles(channels, hidden):
    groups = hidden // LANE
    tap_tile = 2 * (channels // SUB) * groups
    return tap_tile, tap_tile + 2 * groups, tap_tile + 3 * groups


def hidden_block(stages, plan, band, xa, ca, bn, meta, count, sums2, scales, shifts, hshift, w_e, w_rt, kh):
    rows, px, channels = xa.shape
    columns = px // SUB
    hidden = w_e.shape[1]
    groups = hidden // LANE
    parts = 2
    shape = jax.ShapeDtypeStruct
    tiles = sum(count_tiles for _, count_tiles in plan[:2])
    early = sum(early_tiles(*wave) for wave in plan[:2])
    waves = []
    for wave in plan[:2]:
        waves += wave_scratch(*wave, 0, EARLY)
    return pl.pallas_call(
        functools.partial(hidden_kernel, stages, plan),
        name="hidden_block",
        out_shape=[
            shape((2 * band, columns, SUB, channels), f32),
            shape((rows, px, channels), f32),
            shape((early, SUB, LANE), f32),
            shape((4, channels), f32),
        ],
        in_specs=[VMEM] * 12,
        out_specs=[ANY] * 3 + [VMEM],
        scratch_shapes=[
            pltpu.VMEM((columns, SUB, channels), f32),
            pltpu.VMEM((9, groups, SUB, LANE), f32),
            pltpu.VMEM((9, groups, SUB, LANE), f32),
            pltpu.VMEM((rows, px, channels), bf16),
            pltpu.VMEM((rows, px, channels), bf16),
            pltpu.VMEM((rows, px, hidden), bf16),
            pltpu.VMEM((rows, px, hidden), bf16),
            pltpu.VMEM((parts, rows + 2, columns, SUB, LANE), f32),
            pltpu.VMEM((parts, rows + 2, columns, SUB, LANE), f32),
            pltpu.VMEM((parts, 9, SUB, LANE), f32),
            pltpu.VMEM((hidden, channels), bf16),
            pltpu.VMEM((hidden, channels), bf16),
            pltpu.VMEM((rows, px, channels), f32),
            pltpu.VMEM((2 * band, columns, SUB, channels), f32),
            pltpu.VMEM((rows, px, channels), f32),
            pltpu.VMEM((tiles, SUB, LANE), f32),
            pltpu.SemaphoreType.DMA((4,)),
        ]
        + sum_scratch(stages, (4, channels))
        + waves,
        compiler_params=pltpu.CompilerParams(
            collective_id=3, has_side_effects=True, vmem_limit_bytes=63 * MIB
        ),
    )(xa, ca, bn, meta, count, sums2, scales, shifts, hshift, w_e, w_rt, kh)


def wave_plan(sizes, channels, hidden):
    chips = sizes["imgs"]
    side = 2 if chips == 16 else 4
    one, two = ("imgs", 1, side), ("imgs", side, side)
    rest = ("imgs", side * side, chips // (side * side))
    first = ("rows", 1, sizes["rows"])
    first_order, second_order = [first, one, two, rest], [first, two, one, rest]
    short_order = [first, ("imgs", 1, chips)]
    step = 2 * sizes["rows"] * chips
    square = channels // SUB * pl.cdiv(channels, LANE)
    small = pl.cdiv(25, SUB) + pl.cdiv(49, SUB)
    half = pl.cdiv(hidden_tiles(channels, hidden)[2], 2 * step) * step
    return [
        (first_order, half),
        (second_order, half),
        (first_order, pl.cdiv(2 * square, step) * step),
        (short_order, pl.cdiv(square, step) * step),
        (short_order, pl.cdiv(small * pl.cdiv(channels, LANE), step) * step),
    ]


def back_kernel(
    reach, stages, plan, gn, bn_i, xa_i, ca_i, gl_i, sl_i, c1_i, c2_i, gp, tiles_i, nat_i,
    meta, count, sums1, sums2, sums3, scales, shifts, w_in, w_gate, w_out, kl, kd,
    mixo_o, mixq_o, resq_o, full_o, sums_o,
    cm, klb, kdb, gm, tt, sl, xa, ca, gl, c2, gb, gg, gt, g2, g1, src, gw, full,
    in_sem, move_sem, mine, *rest,
):
    found = stage_peers(stages)
    say_here(stage_peers(reach))
    rows, px, channels = xa.shape
    columns = px // SUB
    groups = groups_of(channels)
    core, chip = lax.axis_index("rows"), lax.axis_index("imgs")
    band = mixq_o.shape[0]
    parts = 3
    step = rows // parts
    pairs = [
        (gn, gm), (bn_i, gw), (xa_i, xa), (ca_i, ca), (gl_i, gl), (gp, tt), (c1_i, gg),
    ]
    loads = []
    for p in range(parts):
        at = pl.ds(p * step, step)
        loads.append([])
        for k, (a, b) in enumerate(pairs):
            loads[p].append(pltpu.make_async_copy(a.at[at], b.at[at], in_sem.at[p, k]))
            loads[p][-1].start()
    tail, waves, pair_base = list(rest[len(stages) * 3 :]), [], 0
    for k, (order, tiles) in enumerate(plan):
        (buf, *refs), tail = tail[: 1 + wave_refs(order)], tail[1 + wave_refs(order) :]
        early = EARLY if k < 2 else 0
        waves.append(Wave(order, tiles, refs, buf, 0, full, pair_base, early))
        pair_base += tiles // 2
    late = [
        pltpu.make_async_copy(c2_i, c2, in_sem.at[0, 7]),
        pltpu.make_async_copy(sl_i, sl, in_sem.at[1, 7]),
    ]
    half = early_tiles(*plan[0])
    tile_loads = [
        pltpu.make_async_copy(tiles_i.at[pl.ds(k * half, half)], waves[k].buf, in_sem.at[k, 8])
        for k in range(2)
    ]
    for copy in tile_loads + late:
        copy.start()
    make_col_mask(meta, cm)
    spread_taps(kl, klb, flip=True)
    spread_taps(kd, kdb, flip=True)
    for edge in (0, 1, rows + 2, rows + 3):
        g1[:, edge] = jnp.zeros(g1.shape[:1] + g1.shape[2:], f32)
    total = count[0:1, 0:1]
    mean1, rstd1 = statistics(sums1, total, 0)
    scale1 = rstd1 * b8(scales, 0)
    mean2, rstd2 = statistics(sums2, total, 0)
    scale2 = rstd2 * b8(scales, 2)
    back0 = b8(sums3, 0) / total
    back1 = b8(sums3, 1) / total
    zero = jnp.zeros((SUB, channels), f32)

    def to_other(v, out, first_sem):
        return remote(
            v.at[pl.ds((1 - core) * band, band)], out,
            move_sem.at[first_sem], move_sem.at[first_sem + 1], (1 - core, chip),
        )

    all_found = stage_peers(reach)
    wait_all_here(all_found)
    for copy in tile_loads:
        copy.wait()
    done, ready, clock = [EARLY, EARLY, 0, 0, 0], [0.0, 0.0, None, None, None], [0.0]

    def take(w):
        wave = waves[w]
        wave.step(done[w])
        ready[w] = clock[0] + wave.guess(done[w])
        done[w] += 1

    def stop(spent):
        clock[0] += spent
        for w, wave in enumerate(waves):
            if ready[w] is not None and done[w] < wave.steps and ready[w] <= clock[0]:
                take(w)

    stop(0.0)
    moves = [to_other(nat_i, resq_o, 0)]
    moves[0].start()

    def first(b, sums):
        sums = list(sums)
        gated_parts = []
        for k in range(step // 2):
            r = b * (step // 2) + k
            for g, width in groups:
                conv = gg[r, :, g * LANE : g * LANE + width].astype(f32)
                src[g, r, :, :, :width] = pixels3(conv)
            mask = row_mask(meta, cm, r)
            both = gw[r]
            middle = pixels3(xa[r].astype(f32)) + b8(scales, 1) * both
            hat = (middle - mean2) * rstd2
            grad = pixels3(ca[r].astype(f32)) + scale2 * (
                pixels3(gm[r]) - mask * (back0 + hat * back1)
            )
            gm[r] = pixels2(grad)
            branch = (b8(scales, 1) * grad).astype(bf16)
            gb[r] = pixels2(branch)
            sums[0] = sums[0] + fold(grad * both)
            sums[1] = sums[1] + fold(branch.astype(f32))
            gated_parts.append(pixels2(branch))
        gated_grad = dot_nt(jnp.concatenate(gated_parts, axis=0), w_out[...])
        gate_parts = []
        for k in range(step // 2):
            r = b * (step // 2) + k
            mine_grad = gated_grad[k * px : (k + 1) * px]
            gelu = gl[r].astype(f32)
            gate_grad = (mine_grad * gelu).astype(bf16)
            gg[r] = gate_grad
            gate = tt[r]
            gt[r] = (gelu * gate).astype(bf16)
            tt[r] = mine_grad * gate
            sums[2] = sums[2] + fold(pixels3(gate_grad.astype(f32)))
            gate_parts.append(gate_grad)
        conv_all = low(dot_nt(jnp.concatenate(gate_parts, axis=0), w_gate[...]))
        for k in range(step // 2):
            r = b * (step // 2) + k
            conv = conv_all[k * px : (k + 1) * px]
            for g, width in groups:
                at = slice(g * LANE, g * LANE + width)
                g2[g, r, :, :, :width] = pixels3(conv[:, at])
            sums[3] = sums[3] + fold(pixels3(conv))
        return tuple(sums)

    sums = (zero,) * 4
    for p in range(parts):
        for copy in loads[p]:
            copy.wait()
        sums = lax.fori_loop(2 * p, 2 * p + 2, first, sums)
        stop(3.0)
    for k in range(4):
        mine[2 + k : 3 + k, :] = jnp.sum(sums[k], axis=0, keepdims=True)
    whole = rows * px
    flat = lambda ref: ref[...].reshape(whole, channels)
    blocks, n = channels // SUB, len(groups)

    def square(left, right, wave, base):
        grad = dot_tn(flat(left), flat(right))
        for g, width in groups:
            part = grad[:, g * LANE : g * LANE + width].reshape(blocks, SUB, width)
            wave.buf[pl.ds(base + g, blocks, stride=n), :, :width] = part

    def clear(buf):
        def one(t, _):
            buf[t] = jnp.zeros((SUB, LANE), f32)
            return 0

        lax.fori_loop(0, buf.shape[0], one, 0)

    for wave in waves[2:]:
        clear(wave.buf)
    square(gt, gb, waves[2], 0)
    for copy in late:
        copy.wait()
    square(c2, gg, waves[2], blocks * n)
    ready[2] = 0.0
    stop(1.7)

    def put_tap(tap, g, acc, base):
        row = jnp.sum(acc, axis=0, keepdims=True)
        at = base + tap // SUB * n + g
        waves[4].buf[at, tap % SUB : tap % SUB + 1, :] = row

    near_base, far_base = 0, pl.cdiv(kl.shape[0], SUB) * n
    for g, width in groups:
        for i in range(7):
            first_row = max(0, 3 * (3 - i))
            last_row = min(rows, rows - 3 * (i - 3))

            def taps_row(r, acc, g=g, i=i):
                at = r + (i - 3) * 3
                return tap_sums(
                    list(acc), (lambda c: g2[g, r, c], columns), lambda c: src[g, at, c], 3
                )

            acc = lax.fori_loop(first_row, last_row, taps_row, zeros_list(7))
            for j in range(7):
                put_tap(7 * i + j, g, acc[j], far_base)
            stop(0.39)


    def dilated(r, sums):
        mask = row_mask(meta, cm, r)
        low_i, high_i = row_range(r, rows, 3, 3)
        out = []
        for g, width in groups:

            def tap_row(i, acc):
                taps = [kdb[7 * i + j, g] for j in range(7)]
                at = r + (i - 3) * 3
                return add_row(list(acc), lambda c: g2[g, at, c], taps, 3)

            acc = lax.fori_loop(low_i, high_i, tap_row, zeros_list(columns))
            value = low(mask[:, :, :width] * jnp.stack(acc)[:, :, :width])
            g1[g, r + 2, :, :, :width] = value
            out.append(sums[g] + fold(value))
        return tuple(out)

    start = tuple(jnp.zeros((SUB, width), f32) for g, width in groups)
    sums = start
    for p in range(parts * 2):
        sums = lax.fori_loop(p * (step // 2), (p + 1) * (step // 2), dilated, sums)
        stop(1.5)
    for g, width in groups:
        at = slice(g * LANE, g * LANE + width)
        mine[6:7, at] = jnp.sum(sums[g], axis=0, keepdims=True)

    def refill(r, _):
        for g, width in groups:
            src[g, r, :, :, :width] = pixels3(gl[r, :, g * LANE : g * LANE + width].astype(f32))
        return 0

    lax.fori_loop(0, rows, refill, 0)

    for g, width in groups:
        for i in range(5):

            def taps_row(r, acc, g=g, i=i):
                return tap_sums(
                    list(acc), (lambda c: src[g, r, c], columns), lambda c: g1[g, r + i, c], 1
                )

            acc = lax.fori_loop(0, rows, taps_row, zeros_list(5))
            for j in range(5):
                put_tap(24 - (5 * i + j), g, acc[j], near_base)
            stop(0.48)

    ready[4] = 0.0
    stop(0.0)

    def local(r, sums):
        mask = row_mask(meta, cm, r)
        out = []
        for g, width in groups:
            acc = zeros_list(columns)
            for i in range(5):
                taps = [klb[5 * i + j, g] for j in range(5)]
                acc = add_row(acc, lambda c: g1[g, r + i, c], taps, 1)
            value = mask[:, :, :width] * jnp.stack(acc)[:, :, :width]
            at = slice(g * LANE, g * LANE + width)
            grad = (tt[r, :, at] + pixels2(value)) * sl[r, :, at]
            gg[r, :, at] = grad.astype(bf16)
            out.append(sums[g] + fold(pixels3(low(grad))))
        x = pixels3(xa[r].astype(f32))
        gb[r] = pixels2((x - mean1) * scale1 + b8(shifts, 0)).astype(bf16)
        return tuple(out)

    sums = start
    for p in range(parts * 2):
        sums = lax.fori_loop(p * (step // 2), (p + 1) * (step // 2), local, sums)
        stop(1.25)
    for g, width in groups:
        at = slice(g * LANE, g * LANE + width)
        mine[7:8, at] = jnp.sum(sums[g], axis=0, keepdims=True)
    square(gb, gg, waves[3], 0)
    ready[3] = 0.0
    stop(1.0)

    def last(b, sums):
        sums = list(sums)
        tall = gg[pl.ds(b * (step // 2), step // 2)].reshape(step // 2 * px, channels)
        product = dot_nt(tall, w_in[...])
        for k in range(step // 2):
            r = b * (step // 2) + k
            x = pixels3(xa[r].astype(f32))
            grad = pixels3(gm[r])
            gn1 = pixels3(product[k * px : (k + 1) * px]) + b8(scales, 1) * grad
            gm[r] = pixels2(grad + scale1 * gn1)
            hat = (x - mean1) * rstd1
            sums[0] = sums[0] + fold(gn1)
            sums[1] = sums[1] + fold(gn1 * hat)
        return tuple(sums)

    sums = (zero, zero)
    for p in range(parts * 2):
        sums = lax.fori_loop(p, p + 1, last, sums)
        stop(0.8)
    for k in range(2):
        mine[k : k + 1, :] = jnp.sum(sums[k], axis=0, keepdims=True)
    total_sum = AllSum(stages, mine, rest)
    total_sum.start(0)
    total_sum.end(0)
    stop(1.3)
    for k in range(1, len(stages)):
        total_sum.start(k)
        if k == 1:
            unalign(gm, meta, gw)
            moves.append(to_other(gw, mixq_o, 2))
            own_rows = gw.at[pl.ds(core * band, band)]
            moves.append(pltpu.make_async_copy(own_rows, mixo_o, move_sem.at[4]))
            for copy in moves[1:]:
                copy.start()
        total_sum.end(k)
        stop(3.0)
    sums_o[...] = mine[...]
    pair_base = 0
    for w, (_, tiles) in enumerate(plan):
        while done[w] < waves[w].steps:
            take(w)
        at = pl.ds(pair_base, tiles // 2)
        moves.append(pltpu.make_async_copy(full.at[at], full_o.at[at], move_sem.at[5 + w]))
        moves[-1].start()
        pair_base += tiles // 2
    for copy in moves:
        copy.wait()


def mixer_back(reach, stages, plan, band, gn, bn, xa, ca, gl, sl, c1, c2, gp, tiles, nat, meta, count,
               sums1, sums2, sums3, scales, shifts, w_in, w_gate, w_out, kl, kd):
    rows, px, channels = xa.shape
    columns = px // SUB
    n = len(groups_of(channels))
    small = (rows, px, channels)
    shape = jax.ShapeDtypeStruct
    pairs = sum(tiles // 2 for _, tiles in plan)
    waves = []
    for k, (order, count_tiles) in enumerate(plan):
        early = early_tiles(order, count_tiles) if k < 2 else count_tiles
        waves.append(pltpu.VMEM((early, SUB, LANE), f32))
        waves += wave_scratch(order, count_tiles, EARLY if k < 2 else 0)
    half = shape((band, columns, SUB, channels), f32)
    return pl.pallas_call(
        functools.partial(back_kernel, reach, stages, plan),
        name="mixer_back",
        out_shape=[
            half,
            half,
            half,
            shape((pairs, 2 * SUB, LANE), bf16),
            shape((8, channels), f32),
        ],
        in_specs=[ANY] * 11 + [VMEM] * 12,
        out_specs=[ANY] * 4 + [VMEM],
        scratch_shapes=[
            pltpu.VMEM((columns, SUB, channels), f32),
            pltpu.VMEM((25, n, SUB, LANE), f32),
            pltpu.VMEM((49, n, SUB, LANE), f32),
        ]
        + [pltpu.VMEM(small, k) for k in (f32,) * 3 + (bf16,) * 7]
        + [
            pltpu.VMEM((n, rows, columns, SUB, LANE), f32),
            pltpu.VMEM((n, rows + 4, columns, SUB, LANE), f32),
            pltpu.VMEM((n, rows, columns, SUB, LANE), f32),
            pltpu.VMEM((2 * band, columns, SUB, channels), f32),
            pltpu.VMEM((pairs, 2 * SUB, LANE), bf16),
            pltpu.SemaphoreType.DMA((3, 9)),
            pltpu.SemaphoreType.DMA((5 + len(plan),)),
        ]
        + sum_scratch(stages, (8, channels))
        + waves,
        compiler_params=pltpu.CompilerParams(
            collective_id=4, has_side_effects=True, vmem_limit_bytes=63 * MIB
        ),
    )(gn, bn.reshape(rows, columns, SUB, channels), xa, ca, gl, sl, c1, c2, gp, tiles, nat, meta,
      count, sums1, sums2, sums3, scales,
      shifts, w_in, w_gate, w_out, kl, kd)


def unalign(al, meta, out):
    rows, px, channels = al.shape
    offsets = out.shape[0] - rows + 1
    for at in range(out.shape[0]):
        value = jnp.zeros((px // SUB, SUB, channels), f32)
        for t in range(offsets):
            if 0 <= at - t < rows:
                chosen = (meta[0] == float(t))[None]
                value = jnp.where(chosen, pixels3(al[at - t]), value)
        out[at] = value


def tiles_out(full, base, ref):
    rows, width = ref.shape
    groups = groups_of(width)
    n, blocks = len(groups), rows // SUB
    period = 1 if n % 2 == 0 else 2

    def block(b, _):
        for k in range(period):
            for g, wide in groups:
                tile = k * n + g
                pair = base // 2 + b * (period * n // 2) + tile // 2
                value = full[pair].astype(f32)[tile % 2 * SUB : (tile % 2 + 1) * SUB]
                at = pl.ds(pl.multiple_of((b * period + k) * SUB, SUB), SUB)
                ref[at, g * LANE : g * LANE + wide] = value[:, :wide]
        return 0

    lax.fori_loop(0, blocks // period, block, 0)
    for b in range(blocks // period * period, pl.cdiv(rows, SUB)):
        count = min(SUB, rows - b * SUB)
        for g, wide in groups:
            tile = base + b * n + g
            value = full[tile // 2].astype(f32)[tile % 2 * SUB : tile % 2 * SUB + count]
            ref[b * SUB : b * SUB + count, g * LANE : g * LANE + wide] = value[:, :wide]


def finish_kernel(
    bases, x_i, mixo, mixq, nat, resq, meta, count, sums1, sums3, sums4, scales, full,
    in_o, res_o, sg_o, bg_o, *rest,
):
    for ref, order in (
        (sg_o, ((sums4, 1), (sums4, 2), (sums3, 1), (sums3, 3))),
        (bg_o, tuple((sums4, k) for k in (0, 7, 6, 5, 4, 3)) + ((sums3, 0), (sums3, 2))),
    ):
        for k, (table, row) in enumerate(order):
            ref[k : k + 1, :] = table[row : row + 1, :]
    n = len(bases)
    grads, (x, mix, res, cm), grad_s = rest[:n], rest[n : n + 4], rest[n + 4 : -3]
    in_sem, out_sem, grad_sem = rest[-3:]
    band, columns = x.shape[:2]
    core = lax.axis_index("rows")
    mine = pl.ds(pl.multiple_of(core * SUB, SUB), SUB)
    other = pl.ds(pl.multiple_of((1 - core) * SUB, SUB), SUB)

    def loads(r):
        pairs = [
            (x_i.at[r], x.at[r]),
            (mixo.at[r], mix.at[r, :, mine]),
            (mixq.at[r], mix.at[r, :, other]),
            (nat.at[core * band + r], res.at[r, :, mine]),
            (resq.at[r], res.at[r, :, other]),
        ]
        return [pltpu.make_async_copy(a, b, in_sem.at[r, k]) for k, (a, b) in enumerate(pairs)]

    def stores(r):
        pairs = [(mix.at[r], in_o.at[r]), (res.at[r], res_o.at[r])]
        return [pltpu.make_async_copy(a, b, out_sem.at[r, k]) for k, (a, b) in enumerate(pairs)]

    def begin(r, _):
        for copy in loads(r):
            copy.start()
        return 0

    lax.fori_loop(0, band, begin, 0)
    size, top = meta[1], meta[0]
    for c in range(columns):
        cm[c] = (size > c).astype(f32)
    copies = []
    for k, (ref, base) in enumerate(zip(grad_s, bases)):
        tiles_out(full, base, ref)
        copies.append(pltpu.make_async_copy(ref, grads[k], grad_sem.at[k]))
        copies[-1].start()
    total = count[0:1, 0:1]
    mean = sums1[0:1, :] / total
    rstd = lax.rsqrt(sums1[1:2, :] / total - mean * mean + epsilon)
    scale = rstd * scales[0:1, :]
    back0, back1 = sums4[0:1, :] / total, sums4[1:2, :] / total
    spread = lambda v: jnp.broadcast_to(v, size.shape)
    mean, rstd, scale, back0, back1 = (spread(v) for v in (mean, rstd, scale, back0, back1))

    def row(r, _):
        for copy in loads(r):
            copy.wait()
        at = (r * 1).astype(f32)
        inside = ((at >= top) & (at < top + size)).astype(f32)
        mask = cm[...] * inside[None]
        hat = (mask * x[r].astype(f32) - mean) * rstd
        mix[r] = mask * (mix[r] - scale * (back0 + hat * back1))
        for copy in stores(r):
            copy.start()
        return 0

    lax.fori_loop(0, band, row, 0)

    def end(r, _):
        for copy in stores(r):
            copy.wait()
        return 0

    lax.fori_loop(0, band, end, 0)
    for copy in copies:
        copy.wait()


def finish(
    x, mixo, mixq, nat, resq, meta, count, sums1, sums3, sums4, scales, full, shapes, bases
):
    band, columns, images, channels = x.shape
    shape = jax.ShapeDtypeStruct
    return pl.pallas_call(
        functools.partial(finish_kernel, bases),
        name="finish",
        in_specs=[ANY] * 5 + [VMEM] * 7,
        out_specs=[ANY] * 2 + [VMEM] * 2 + [ANY] * len(shapes),
        scratch_shapes=[
            pltpu.VMEM(x.shape, bf16),
            pltpu.VMEM(x.shape, f32),
            pltpu.VMEM(x.shape, f32),
            pltpu.VMEM((columns, images, channels), f32),
        ]
        + [pltpu.VMEM(s, f32) for s in shapes]
        + [
            pltpu.SemaphoreType.DMA((band, 5)),
            pltpu.SemaphoreType.DMA((band, 2)),
            pltpu.SemaphoreType.DMA((len(shapes),)),
        ],
        out_shape=[shape(x.shape, f32)] * 2
        + [shape((k, channels), f32) for k in (4, 8)]
        + [shape(s, f32) for s in shapes],
        compiler_params=pltpu.CompilerParams(vmem_limit_bytes=62 * MIB),
    )(x, mixo, mixq, nat, resq, meta, count, sums1, sums3, sums4, scales, full)


def on_device(sizes, inputs, cotangent, scales, shifts, hidden_shift, w_inward, w_gating,
              w_outward, w_expand, w_reduce, kernel_local, kernel_dilated, kernel_hidden,
              image_size, band_split, slot_image):
    images, band, columns, channels = inputs.shape
    x = jnp.transpose(inputs, (1, 2, 0, 3))
    y = jnp.transpose(cotangent, (1, 2, 0, 3))
    stages = stage_list(sizes)
    xa, ca, gl, sl, c1, c2, gp, bn, sums1, sums2, own_meta, meta, count = mixer_forward(
        stages, x, y, image_size[None], band_split[None], slot_image[None], scales, shifts,
        w_inward, w_gating, w_outward, kernel_local, kernel_dilated,
    )
    hidden = w_expand.shape[1]
    plan = wave_plan(sizes, channels, hidden)
    half_tiles = plan[0][1]
    nat, gn, tiles, sums3 = hidden_block(
        stages, plan, band, xa, ca, bn, meta, count, sums2, scales, shifts,
        hidden_shift, w_expand, w_reduce.T, kernel_hidden,
    )
    mixo, mixq, resq, full, sums4 = mixer_back(
        reach_list(sizes), stages, plan, band, gn, bn, xa, ca, gl, sl, c1, c2, gp, tiles, nat, meta, count,
        sums1, sums2, sums3, scales, shifts, w_inward, w_gating, w_outward, kernel_local,
        kernel_dilated,
    )
    square, wide = (channels, channels), (channels, hidden)
    blocks, n = channels // SUB, len(groups_of(channels))
    tap_tile, bias_tile, _ = hidden_tiles(channels, hidden)
    second = 2 * half_tiles
    third = second + plan[2][1]
    near = third + plan[3][1]
    far = near + pl.cdiv(kernel_local.shape[0], SUB) * n
    targets = [
        (wide, 0),
        (wide, tap_tile // 2),
        (kernel_hidden.shape, tap_tile),
        (hidden_shift.shape, bias_tile),
        (square, second),
        (square, second + blocks * n),
        (square, third),
        (kernel_local.shape, near),
        (kernel_dilated.shape, far),
    ]
    (input_grad, result, scales_grad, shifts_grad, gwe, gwr, gk, gh, gwo, gwg, gwi, gkl,
     gkd) = finish(
        x, mixo, mixq, nat, resq, own_meta, count, sums1, sums3, sums4, scales, full,
        [t[0] for t in targets], [t[1] for t in targets],
    )
    back = lambda v: jnp.transpose(v, (2, 0, 1, 3))
    return (
        back(result), back(input_grad), scales_grad, shifts_grad, gh, gwi, gwg, gwo, gwe, gwr.T,
        gkl, gkd, gk,
    )


def solution(mesh):
    wide = P("imgs", "rows", None, None)
    sizes = dict(mesh.shape)
    return jax.shard_map(
        functools.partial(on_device, sizes),
        mesh=mesh,
        in_specs=(wide, wide) + (P(),) * 13 + (P("imgs"),),
        out_specs=(wide, wide) + (P(),) * 11,
        check_vma=False,
    )
```

```python
import functools
import math

import jax
import jax.numpy as jnp
from jax import lax
from jax.experimental import pallas as pl
from jax.experimental.pallas import tpu as pltpu
from jax.sharding import PartitionSpec as P

MESH = pl.DeviceIdType.MESH
epsilon = 1e-05
bf16 = jnp.bfloat16
f32 = jnp.float32
SUB = 8
LANE = 128
MIB = 1 << 20
ANY = pl.BlockSpec(memory_space=pl.ANY)
VMEM = pl.BlockSpec(memory_space=pltpu.VMEM)


def low(values):
    return values.astype(bf16).astype(f32)


def normal_parts(v):
    bell = jnp.exp2((-0.5 * 1.4426950408889634) * (v * v))
    return 0.5 + 0.5 * lax.erf(v * 0.7071067811865476), bell * 0.3989422804014327


def dot(a, b):
    return jnp.dot(a, b, preferred_element_type=f32)


def dot_nt(a, b):
    return lax.dot_general(a, b, (((1,), (1,)), ((), ())), preferred_element_type=f32)


def dot_tn(a, b):
    return lax.dot_general(a, b, (((0,), (0,)), ((), ())), preferred_element_type=f32)


def groups_of(channels):
    return [(g, min(LANE, channels - g * LANE)) for g in range(pl.cdiv(channels, LANE))]


def spread_taps(k_ref, kb, flip=False):
    count, channels = k_ref.shape
    for tap in range(count):
        from_tap = count - 1 - tap if flip else tap
        row = jnp.broadcast_to(k_ref[from_tap : from_tap + 1, :], (SUB, channels))
        for g, width in groups_of(channels):
            kb[tap, g, :, :width] = row[:, g * LANE : g * LANE + width]


def add_row(acc, load, taps, dilation):
    columns, half = len(acc), len(taps) // 2
    for c in range(columns):
        value = load(c)
        for j, tap in enumerate(taps):
            at = c - (j - half) * dilation
            if 0 <= at < columns:
                acc[at] = acc[at] + tap * value
    return acc


def tap_sums(acc, load_fixed, load_moved, dilation):
    columns, half = load_fixed[1], len(acc) // 2
    fixed = [load_fixed[0](c) for c in range(columns)]
    for c in range(columns):
        value = load_moved(c)
        for j in range(len(acc)):
            at = c - (j - half) * dilation
            if 0 <= at < columns:
                acc[j] = acc[j] + fixed[at] * value
    return acc


def row_range(r, rows, half, dilation):
    low_i = jnp.maximum(half - r // dilation, 0)
    high_i = jnp.minimum(half + (rows - 1 - r) // dilation, 2 * half)
    return low_i, high_i + 1


def zeros_list(count):
    return [jnp.zeros((SUB, LANE), f32) for _ in range(count)]


def b8(ref, i):
    return jnp.broadcast_to(ref[i : i + 1, :], (SUB, ref.shape[1]))


def make_col_mask(meta, cm):
    size = meta[2]
    for c in range(cm.shape[0]):
        cm[c] = (size > c).astype(f32)


def row_mask(meta, cm, r):
    at = (r * 1).astype(f32)
    inside = (at >= meta[1]) & (at < meta[1] + meta[2])
    return cm[...] * inside.astype(f32)[None]


def pixels3(values):
    return values.reshape(values.shape[0] // SUB, SUB, values.shape[1])


def pixels2(values):
    return values.reshape(values.shape[0] * SUB, values.shape[2])


def fold(values):
    return jnp.sum(values, axis=0)


def statistics(sums, count, i):
    mean = b8(sums, i) / count
    return mean, lax.rsqrt(b8(sums, i + 1) / count - mean * mean + epsilon)


def stage_list(sizes):
    stages = [("rows", 1, sizes["rows"])]
    left, stride = sizes["imgs"], 1
    while left > 1:
        size = 4 if left % 4 == 0 else (2 if left % 2 == 0 else left)
        stages.append(("imgs", stride, size))
        left, stride = left // size, stride * size
    return [s for s in stages if s[2] > 1]


def reach_list(sizes):
    return [("rows", 1, sizes["rows"]), ("imgs", 1, sizes["imgs"])]


def stage_peers(stages):
    core = lax.axis_index("rows")
    chip = lax.axis_index("imgs")
    found = []
    for axis, stride, size in stages:
        index = core if axis == "rows" else chip
        place = lax.rem(index // stride, size)
        peers = []
        for step in range(1, size):
            other = lax.rem(place + step, size)
            at = index + (other - place) * stride
            peers.append((step, other, (at, chip) if axis == "rows" else (core, at)))
        found.append((place, peers))
    return found


def say_here(found):
    barrier = pltpu.get_barrier_semaphore()
    for _, peers in found:
        for _, _, device in peers:
            pl.semaphore_signal(barrier, inc=1, device_id=device, device_id_type=MESH)


def wait_all_here(found):
    pl.semaphore_wait(pltpu.get_barrier_semaphore(), sum(len(peers) for _, peers in found))


def greet(found):
    say_here(found)
    wait_all_here(found)


def remote(src, dst, send, recv, device):
    return pltpu.make_async_remote_copy(
        src_ref=src, dst_ref=dst, send_sem=send, recv_sem=recv,
        device_id=device, device_id_type=MESH,
    )


class AllSum:
    def __init__(self, stages, mine, rest):
        self.found, self.mine = stage_peers(stages), mine
        n = len(stages)
        self.slots, self.sems = rest[:n], rest[n : 3 * n]

    def start(self, k):
        slot, (send, recv) = self.slots[k], self.sems[2 * k : 2 * k + 2]
        self.copies = []
        for step, _, device in self.found[k][1]:
            at = step - 1
            self.copies.append(remote(self.mine, slot.at[at], send.at[at], recv.at[at], device))
            self.copies[-1].start()

    def end(self, k):
        for copy in self.copies:
            copy.wait()
        total = self.mine[...]
        for step, _, _ in self.found[k][1]:
            total = total + self.slots[k][step - 1]
        self.mine[...] = total


def all_sum(stages, mine, rest):
    total = AllSum(stages, mine, rest)
    for k in range(len(stages)):
        total.start(k)
        total.end(k)


def sum_scratch(stages, table):
    sems = []
    for _, _, size in stages:
        sems += [pltpu.SemaphoreType.DMA((size - 1,))] * 2
    slots = [pltpu.VMEM((size - 1,) + table, f32) for _, _, size in stages]
    return [pltpu.VMEM(table, f32)] + slots + sems


def mixer_kernel(
    stages, x_i, y_i, sizes, splits, slots, scales, shifts, w_in, w_gate, w_out, kl, kd,
    xa_o, ca_o, gl_o, sl_o, c1_o, c2_o, gp_o, bn_o, sums1_o, sums_o, own_meta, meta, count,
    cm, klb, kdb, xa, ca, gl, sl, c1, c2, gp, bn, gf, c1f, sem,
    own_cm, xs, ys, xw, cw, move_sem, mine, *rest,
):
    found = stage_peers(stages)
    say_here(found)
    rows, px, channels = xa.shape
    columns = px // SUB
    groups = groups_of(channels)
    offsets = xw.shape[0] - rows + 1
    core, chip = lax.axis_index("rows"), lax.axis_index("imgs")
    band = x_i.shape[0]
    upper = core == 0
    place_images(sizes, splits, slots, core, band, columns, own_meta, meta, count)
    size, top = own_meta[1], own_meta[0]
    for c in range(columns):
        own_cm[c] = (size > c).astype(f32)

    def split(value, full, out, r):
        a, b = value[:, :SUB], value[:, SUB:]
        full[core * band + r] = pixels2(jnp.where(upper, a, b)).astype(bf16)
        out[r] = pixels2(jnp.where(upper, b, a)).astype(bf16)

    def split_x(r, sums):
        at = (r * 1).astype(f32)
        inside = ((at >= top) & (at < top + size)).astype(f32)
        value = x_i[r].astype(f32)
        split(value, xw, xs, r)
        value = own_cm[...] * inside[None] * value
        return sums[0] + fold(value), sums[1] + fold(value * value)

    def split_y(r, _):
        split(y_i[r].astype(f32), cw, ys, r)
        return 0

    def to_other(out, full, k):
        at = pl.ds(core * band, band)
        return remote(out, full.at[at], move_sem.at[k], move_sem.at[k + 1], (1 - core, chip))

    zero = jnp.zeros((2 * SUB, channels), f32)
    sums = lax.fori_loop(0, band, split_x, (zero, zero))
    for k in range(2):
        mine[k : k + 1, :] = jnp.sum(sums[k], axis=0, keepdims=True)
    wait_all_here(found)
    moves = [to_other(xs, xw, 0), to_other(ys, cw, 2)]
    first_sum = AllSum(stages, mine, rest)
    first_sum.start(0)
    moves[0].start()
    lax.fori_loop(0, band, split_y, 0)
    moves[1].start()
    first_sum.end(0)
    first_sum.start(1)
    make_col_mask(meta, cm)
    spread_taps(kl, klb)
    spread_taps(kd, kdb)
    for edge in (0, 1, rows + 2, rows + 3):
        gf[:, edge] = jnp.zeros(gf.shape[:1] + gf.shape[2:], f32)
    first_sum.end(1)
    for k in range(2, len(stages)):
        first_sum.start(k)
        first_sum.end(k)
    sums1_o[...] = mine[...]
    for copy in moves:
        copy.wait()
    total = count[0:1, 0:1]
    mean, rstd = statistics(sums1_o, total, 0)
    scale = rstd * b8(scales, 0)
    starts = [meta[0] == float(t) for t in range(offsets)]

    def aligned(ref, r):
        value = pixels3(ref[r].astype(f32))
        for t in range(1, offsets):
            value = jnp.where(starts[t][None], pixels3(ref[r + t].astype(f32)), value)
        return value

    tall_rows = 6

    def first(b, _):
        parts, masks = [], []
        for k in range(tall_rows):
            r = b * tall_rows + k
            mask = row_mask(meta, cm, r)
            x = mask * aligned(xw, r)
            xa[r] = pixels2(x).astype(bf16)
            ca[r] = pixels2(mask * aligned(cw, r)).astype(bf16)
            parts.append(pixels2((x - mean) * scale + b8(shifts, 0)).astype(bf16))
        product = dot(jnp.concatenate(parts, axis=0), w_in[...])
        for k in range(tall_rows):
            r = b * tall_rows + k
            mask = row_mask(meta, cm, r)
            pre = pixels3(product[k * px : (k + 1) * px]) + b8(shifts, 1)
            phi_sum, bell = normal_parts(pre)
            gelu = mask * low(pre * phi_sum)
            sl[r] = pixels2(phi_sum + pre * bell)
            gl[r] = pixels2(gelu).astype(bf16)
            for g, width in groups:
                gf[g, r + 2, :, :, :width] = gelu[:, :, g * LANE : g * LANE + width]
        return 0

    lax.fori_loop(0, rows // tall_rows, first, 0)
    early = [(xa, xa_o), (ca, ca_o), (gl, gl_o), (sl, sl_o)]
    copies = [pltpu.make_async_copy(a, b, sem.at[k]) for k, (a, b) in enumerate(early)]
    for copy in copies:
        copy.start()

    def local(r, _):
        mask = row_mask(meta, cm, r)
        for g, width in groups:
            acc = zeros_list(columns)
            for i in range(5):
                taps = [klb[5 * i + j, g] for j in range(5)]
                acc = add_row(acc, lambda c: gf[g, r + i, c], taps, 1)
            bias = b8(shifts, 2)[:, g * LANE : g * LANE + width]
            value = jnp.stack(acc)[:, :, :width] + bias
            value = mask[:, :, :width] * low(value)
            c1f[g, r, :, :, :width] = value
            c1[r, :, g * LANE : g * LANE + width] = pixels2(value).astype(bf16)
        return 0

    lax.fori_loop(0, rows, local, 0)
    copies.append(pltpu.make_async_copy(c1, c1_o, sem.at[4]))
    copies[-1].start()

    def dilated(r, _):
        low_i, high_i = row_range(r, rows, 3, 3)
        for g, width in groups:

            def tap_row(i, acc):
                taps = [kdb[7 * i + j, g] for j in range(7)]
                at = r + (i - 3) * 3
                return add_row(list(acc), lambda c: c1f[g, at, c], taps, 3)

            acc = lax.fori_loop(low_i, high_i, tap_row, zeros_list(columns))
            bias = b8(shifts, 3)[:, g * LANE : g * LANE + width]
            value = jnp.stack(acc)[:, :, :width] + bias
            c2[r, :, g * LANE : g * LANE + width] = pixels2(value).astype(bf16)
        return 0

    lax.fori_loop(0, rows, dilated, 0)
    copies.append(pltpu.make_async_copy(c2, c2_o, sem.at[5]))
    copies[-1].start()

    def last(b, sums):
        sums = list(sums)
        tall = c2[pl.ds(b * tall_rows, tall_rows)].reshape(tall_rows * px, channels)
        gates = dot(tall, w_gate[...])
        parts = []
        for k in range(tall_rows):
            r = b * tall_rows + k
            gate = pixels3(gates[k * px : (k + 1) * px]) + b8(shifts, 4)
            gate = pixels2(gate)
            gp[r] = gate
            parts.append((gl[r].astype(f32) * gate).astype(bf16))
        branches = dot(jnp.concatenate(parts, axis=0), w_out[...])
        for k in range(tall_rows):
            r = b * tall_rows + k
            mask = row_mask(meta, cm, r)
            x = pixels3(xa[r].astype(f32))
            normed = low((x - mean) * scale + b8(shifts, 0))
            both = pixels3(branches[k * px : (k + 1) * px]) + b8(shifts, 5) + normed
            bn[r] = pixels2(both)
            middle = mask * (x + b8(scales, 1) * both)
            sums[0] = sums[0] + fold(middle)
            sums[1] = sums[1] + fold(middle * middle)
        return tuple(sums)

    zero = jnp.zeros((SUB, channels), f32)
    sums = lax.fori_loop(0, rows // tall_rows, last, (zero, zero))
    copies.append(pltpu.make_async_copy(gp, gp_o, sem.at[6]))
    copies[-1].start()
    copies.append(pltpu.make_async_copy(bn, bn_o, sem.at[7]))
    copies[-1].start()
    for k in range(2):
        mine[k : k + 1, :] = jnp.sum(sums[k], axis=0, keepdims=True)
    all_sum(stages, mine, rest[3 * len(stages) :])
    sums_o[...] = mine[...]
    for copy in copies:
        copy.wait()


def mixer_forward(
    stages, x, y, sizes, splits, slots, scales, shifts, w_in, w_gate, w_out, kl, kd
):
    band, columns, images, channels = x.shape
    px = columns * SUB
    rows = columns
    n = len(groups_of(channels))
    small = (rows, px, channels)
    kinds = (bf16, bf16, bf16, f32, bf16, bf16, f32, f32)
    return pl.pallas_call(
        functools.partial(mixer_kernel, stages),
        name="mixer_forward",
        out_shape=[jax.ShapeDtypeStruct(small, k) for k in kinds]
        + [jax.ShapeDtypeStruct((2, channels), f32)] * 2
        + [
            jax.ShapeDtypeStruct((2, images, channels), f32),
            jax.ShapeDtypeStruct((3, SUB, channels), f32),
            jax.ShapeDtypeStruct((SUB, LANE), f32),
        ],
        in_specs=[VMEM] * 12,
        out_specs=[ANY] * 8 + [VMEM] * 5,
        scratch_shapes=[
            pltpu.VMEM((columns, SUB, channels), f32),
            pltpu.VMEM((25, n, SUB, LANE), f32),
            pltpu.VMEM((49, n, SUB, LANE), f32),
        ]
        + [pltpu.VMEM(small, k) for k in kinds]
        + [
            pltpu.VMEM((n, rows + 4, columns, SUB, LANE), f32),
            pltpu.VMEM((n, rows, columns, SUB, LANE), f32),
            pltpu.SemaphoreType.DMA((8,)),
            pltpu.VMEM((columns, images, channels), f32),
            pltpu.VMEM((band, px, channels), bf16),
            pltpu.VMEM((band, px, channels), bf16),
            pltpu.VMEM((2 * band, px, channels), bf16),
            pltpu.VMEM((2 * band, px, channels), bf16),
            pltpu.SemaphoreType.DMA((4,)),
        ]
        + sum_scratch(stages, (2, channels))
        + sum_scratch(stages, (2, channels))[1:],
        compiler_params=pltpu.CompilerParams(
            collective_id=2, has_side_effects=True, vmem_limit_bytes=62 * MIB
        ),
    )(x, y, sizes, splits, slots, scales, shifts, w_in, w_gate, w_out, kl, kd)


def place_images(sizes, splits, slots, core, band, columns, own_meta, meta, count):
    images, channels = own_meta.shape[1:]
    size = sizes[...].astype(f32)
    total = jnp.sum(size * size, axis=1, keepdims=True)
    count[...] = jnp.broadcast_to(total, count.shape)
    shape = (images, images)
    rows, cols = (lax.broadcasted_iota(jnp.int32, shape, k) for k in range(2))
    spread = jnp.broadcast_to(slots[...].astype(f32), shape)
    column = jnp.sum(jnp.where(rows == cols, spread, 0.0), axis=1, keepdims=True)
    shape = (images, size.shape[1])
    image = lax.broadcasted_iota(jnp.int32, shape, 1).astype(f32)
    chosen = image == jnp.broadcast_to(column, shape)

    def pick(row):
        value = jnp.where(chosen, jnp.broadcast_to(row, shape), 0.0)
        value = jnp.sum(value, axis=1, keepdims=True)
        return jnp.broadcast_to(value, (images, channels))

    extent = pick(size)
    top = float(band) - pick(splits[...].astype(f32))
    own_meta[0] = top - (core * band).astype(f32)
    own_meta[1] = extent
    half = lambda v: jnp.where(core == 0, v[:SUB], v[SUB:])
    top, extent = half(top), half(extent)
    start = jnp.clip(top, 0.0, float(2 * band - columns))
    meta[0] = start
    meta[1] = top - start
    meta[2] = extent


class Wave:
    def __init__(self, order, tiles, refs, buf, base=0, full=None, pair_base=0, done=0):
        self.order, self.found = order, stage_peers(order)
        self.buf, self.base, self.full, self.pair_base = buf, base, full, pair_base
        n = len(order)
        self.slots, self.sems = refs[:n], refs[n:]
        self.start, self.length, self.origin = 0, tiles, 0
        self.shares, self.copies, self.done = [], [], done
        for k in range(done):
            self.take(k)
        self.origin = self.start

    @property
    def steps(self):
        return 2 * len(self.order) + 1

    def take(self, k):
        self.length //= self.order[k][2]
        self.start = self.start + self.found[k][0] * self.length
        self.shares.append((self.start, self.length))

    def wait(self):
        for copy in self.copies:
            copy.wait()
        self.copies = []

    def at(self, tile):
        return self.base + tile - self.origin

    def add(self, k):
        self.wait()
        self.take(k)
        size = math.gcd(self.length, 16)
        start, buf, slot = self.at(self.start), self.buf, self.slots[k]
        count = len(self.found[k][1])

        def some(t, _):
            at = pl.ds(start + t * size, size)
            total = buf[at]
            for i in range(count):
                total = total + slot[i, pl.ds(t * size, size)]
            buf[at] = total
            return 0

        lax.fori_loop(0, self.length // size, some, 0)

    def scatter(self, k):
        share = self.length // self.order[k][2]
        send, recv = self.sems[4 * k : 4 * k + 2]
        for step, other, device in self.found[k][1]:
            src = self.buf.at[pl.ds(self.at(self.start + other * share), share)]
            at = step - 1
            self.copies.append(remote(src, self.slots[k].at[at], send.at[at], recv.at[at], device))
            self.copies[-1].start()

    def round(self):
        start, buf, full = self.at(self.start), self.buf, self.full
        first = self.pair_base + self.start // 2

        def one(p, _):
            both = jnp.concatenate([buf[start + 2 * p], buf[start + 2 * p + 1]], axis=0)
            full[first + p] = both.astype(bf16)
            return 0

        lax.fori_loop(0, self.length // 2, one, 0)

    def part(self, k):
        start, length = self.shares[k]
        return self.full.at[pl.ds(self.pair_base + start // 2, length // 2)]

    def gather(self, k):
        send, recv = self.sems[4 * k + 2 : 4 * k + 4]
        here = self.part(k)
        for step, _, device in self.found[k][1]:
            at = step - 1
            self.copies.append(remote(here, here, send.at[at], recv.at[at], device))
            self.copies[-1].start()

    def guess(self, i):
        n = len(self.order)
        if i >= 2 * n:
            return 0.0
        k = i if i < n else 2 * n - 1 - i
        axis, _, size = self.order[k]
        share = self.length // size if i < n else self.shares[k][1] / 2
        if axis == "rows":
            return 1.5 + share * 0.008
        links = {2: 2, 4: 8}.get(size, 16)
        return LATENCY + links * share * PER_TILE

    def step(self, i):
        n = len(self.order)
        self.wait()
        if self.done < i <= n:
            self.add(i - 1)
        if i < n:
            self.scatter(i)
        elif i < 2 * n:
            if i == n:
                self.round()
            self.gather(2 * n - 1 - i)


def wave_scratch(order, tiles, first=0, last=None):
    last = len(order) if last is None else last
    slots, sems, length = [], [], tiles
    for k, (_, _, size) in enumerate(order):
        length //= size
        used = first <= k < last
        slots.append(pltpu.VMEM((size - 1, length if used else 1, SUB, LANE), f32))
        sems += [pltpu.SemaphoreType.DMA((size - 1,))] * 4
    return slots + sems


def wave_refs(order):
    return 5 * len(order)


LATENCY, PER_TILE = 2.5, 0.055
EARLY = 2


def early_tiles(order, tiles):
    return tiles // math.prod(size for _, _, size in order[:EARLY])


def hidden_kernel(
    stages, plan, xa, ca, bn, meta, count, sums2, scales, shifts, hshift, w_e, w_rt, kh,
    nat_o, gn_o, tiles_o, sums_o,
    cm, khb, kfb, n2, gr, ha, ge, em, gc, kacc, wet, wr, res, nat, gn_s, tiles, sem, mine, *rest,
):
    found = stage_peers(stages)
    say_here(found)
    tail, waves = list(rest[3 * len(stages) :]), []
    for k, (order, count_tiles) in enumerate(plan[:2]):
        refs, tail = tail[: wave_refs(order)], tail[wave_refs(order) :]
        waves.append(Wave(order, count_tiles, refs, tiles, base=k * count_tiles))
    rows, px, channels = xa.shape
    columns = px // SUB
    hidden = w_e.shape[1]
    wide = em.shape[0] * LANE
    parts = em.shape[0]
    wide_step = 9
    groups = hidden // LANE
    tap_tile, bias_tile, last_tile = hidden_tiles(channels, hidden)
    for t in range(tap_tile, last_tile):
        tiles[t] = jnp.zeros((SUB, LANE), f32)
    make_col_mask(meta, cm)
    spread_taps(kh, khb)
    spread_taps(kh, kfb, flip=True)
    for edge in (0, rows + 1):
        em[:, edge] = jnp.zeros(em.shape[:1] + em.shape[2:], f32)
        gc[:, edge] = jnp.zeros(gc.shape[:1] + gc.shape[2:], f32)
    wet[...] = w_e[...].astype(f32).T.astype(bf16)
    wr[...] = w_rt[...].astype(f32).T.astype(bf16)
    total = count[0:1, 0:1]
    mean, rstd = statistics(sums2, total, 0)
    scale = rstd * b8(scales, 2)

    def middle_of(r):
        return pixels3(xa[r].astype(f32)) + b8(scales, 1) * pixels3(bn[r])

    def prepare(r, acc):
        normed = (middle_of(r) - mean) * scale + b8(shifts, 6)
        n2[r] = pixels2(normed).astype(bf16)
        grad = (b8(scales, 3) * pixels3(ca[r].astype(f32))).astype(bf16)
        gr[r] = pixels2(grad)
        return acc + fold(grad.astype(f32))

    zero = jnp.zeros((SUB, channels), f32)
    grad_sum = lax.fori_loop(0, rows, prepare, zero)

    def chunk(f, _):
        base = pl.multiple_of(f * wide, wide)
        lanes = pl.ds(base, wide)
        group = f * parts

        def expand(b, _):
            tall = n2[pl.ds(b * wide_step, wide_step)].reshape(wide_step * px, channels)
            product = dot(tall, w_e[:, lanes])
            grads = gr[pl.ds(b * wide_step, wide_step)].reshape(wide_step * px, channels)
            grads = dot(grads, w_rt[:, lanes])
            for k in range(wide_step):
                r = b * wide_step + k
                for g in range(parts):
                    at = slice(g * LANE, (g + 1) * LANE)
                    gc[g, r + 1] = pixels3(grads[k * px : (k + 1) * px, at])
                mask = row_mask(meta, cm, r)[:, :, :LANE]
                value = product[k * px : (k + 1) * px]
                value = low(value + jnp.broadcast_to(hshift[0:1, lanes], value.shape))
                for g in range(parts):
                    em[g, r + 1] = mask * pixels3(value[:, g * LANE : (g + 1) * LANE])
            return 0

        lax.fori_loop(0, rows // wide_step, expand, 0)

        def forward(r, acc):
            out = []
            for g in range(parts):
                conv = zeros_list(columns)
                for i in range(3):
                    taps = [khb[3 * i + j, group + g] for j in range(3)]
                    conv = add_row(conv, lambda c: em[g, r + i, c], taps, 1)
                here = pl.ds(pl.multiple_of(base + g * LANE, LANE), LANE)
                v = jnp.stack(conv) + jnp.broadcast_to(hshift[1:2, here], (SUB, LANE))
                phi_sum, bell = normal_parts(v)
                ha[r, :, here] = pixels2(v * phi_sum).astype(bf16)
                back = low(gc[g, r + 1] * (phi_sum + v * bell))
                gc[g, r + 1] = back
                out.append(acc[g] + fold(back))
            return tuple(out)

        bias = lax.fori_loop(0, rows, forward, tuple(zeros_list(parts)))
        for g in range(parts):
            tiles[bias_tile + group + g, 1:2, :] = jnp.sum(bias[g], axis=0, keepdims=True)
            for tap in range(9):
                kacc[g, tap] = jnp.zeros((SUB, LANE), f32)

        def backward(r, acc):
            mask = row_mask(meta, cm, r)[:, :, :LANE]
            out = []
            for g in range(parts):
                conv = zeros_list(columns)
                for i in range(3):
                    taps = [kfb[3 * i + j, group + g] for j in range(3)]
                    sums = [kacc[g, 3 * i + j] for j in range(3)]
                    fixed = [em[g, r + 1, c] for c in range(columns)]
                    for c in range(columns):
                        value = gc[g, r + i, c]
                        for j in range(3):
                            at = c - (j - 1)
                            if 0 <= at < columns:
                                conv[at] = conv[at] + taps[j] * value
                                sums[j] = sums[j] + fixed[at] * value
                    for j in range(3):
                        kacc[g, 3 * i + j] = sums[j]
                here = pl.ds(pl.multiple_of(base + g * LANE, LANE), LANE)
                value = low(mask * jnp.stack(conv))
                ge[r, :, here] = pixels2(value).astype(bf16)
                out.append(acc[g] + fold(value))
            return tuple(out)

        bias = lax.fori_loop(0, rows, backward, tuple(zeros_list(parts)))
        for g in range(parts):
            tiles[bias_tile + group + g, 0:1, :] = jnp.sum(bias[g], axis=0, keepdims=True)
            for tap in range(9):
                at = tap_tile + (8 - tap) // SUB * groups + group + g
                row = (8 - tap) % SUB
                tiles[at, row : row + 1, :] = jnp.sum(kacc[g, tap], axis=0, keepdims=True)
        return 0

    lax.fori_loop(0, hidden // wide, chunk, 0)

    whole = rows * px
    blocks = channels // SUB
    for k, (left, right) in enumerate(((n2, ge), (gr, ha))):
        grad = dot_tn(left[...].reshape(whole, channels), right[...].reshape(whole, hidden))
        for g in range(groups):
            part = grad[:, g * LANE : (g + 1) * LANE].reshape(blocks, SUB, LANE)
            tiles[pl.ds(k * blocks * groups + g, blocks, stride=groups)] = part
    wait_all_here(found)
    for wave in waves:
        wave.step(0)

    step = 3

    def finish(b, sums):
        sums = list(sums)
        at = pl.ds(b * step, step)
        tall = step * px
        reduced_all = dot(ha[at].reshape(tall, hidden), wr[...])
        gn_all = dot(ge[at].reshape(tall, hidden), wet[...])
        for k in range(step):
            r = b * step + k
            mask = row_mask(meta, cm, r)
            reduced = pixels3(reduced_all[k * px : (k + 1) * px]) + b8(shifts, 7)
            middle = middle_of(r)
            res[r] = pixels2(mask * (middle + b8(scales, 3) * reduced))
            gn = pixels3(gn_all[k * px : (k + 1) * px])
            gn_s[r] = pixels2(gn)
            hat = (middle - mean) * rstd
            out = pixels3(ca[r].astype(f32))
            sums[0] = sums[0] + fold(gn)
            sums[1] = sums[1] + fold(gn * hat)
            sums[2] = sums[2] + fold(out * reduced)
        return tuple(sums)

    sums = lax.fori_loop(0, 2, finish, (zero, zero, zero))
    for wave in waves:
        wave.step(1)
    sums = lax.fori_loop(2, rows // step, finish, sums)
    copies = [pltpu.make_async_copy(gn_s, gn_o, sem.at[1])]
    copies[-1].start()
    for k, value in enumerate((sums[0], sums[1], grad_sum, sums[2])):
        mine[k : k + 1, :] = jnp.sum(value, axis=0, keepdims=True)
    unalign(res, meta, nat)
    copies.append(pltpu.make_async_copy(nat, nat_o, sem.at[2]))
    copies[-1].start()
    all_sum(stages, mine, rest)
    sums_o[...] = mine[...]
    for k, wave in enumerate(waves):
        wave.add(EARLY - 1)
        at = pl.ds(wave.at(wave.start), wave.length)
        here = pl.ds(k * wave.length, wave.length)
        copies.append(pltpu.make_async_copy(tiles.at[at], tiles_o.at[here], sem.at[k and 3]))
        copies[-1].start()
    for copy in copies:
        copy.wait()


def hidden_tiles(channels, hidden):
    groups = hidden // LANE
    tap_tile = 2 * (channels // SUB) * groups
    return tap_tile, tap_tile + 2 * groups, tap_tile + 3 * groups


def hidden_block(stages, plan, band, xa, ca, bn, meta, count, sums2, scales, shifts, hshift, w_e, w_rt, kh):
    rows, px, channels = xa.shape
    columns = px // SUB
    hidden = w_e.shape[1]
    groups = hidden // LANE
    parts = 2
    shape = jax.ShapeDtypeStruct
    tiles = sum(count_tiles for _, count_tiles in plan[:2])
    early = sum(early_tiles(*wave) for wave in plan[:2])
    waves = []
    for wave in plan[:2]:
        waves += wave_scratch(*wave, 0, EARLY)
    return pl.pallas_call(
        functools.partial(hidden_kernel, stages, plan),
        name="hidden_block",
        out_shape=[
            shape((2 * band, columns, SUB, channels), f32),
            shape((rows, px, channels), f32),
            shape((early, SUB, LANE), f32),
            shape((4, channels), f32),
        ],
        in_specs=[VMEM] * 12,
        out_specs=[ANY] * 3 + [VMEM],
        scratch_shapes=[
            pltpu.VMEM((columns, SUB, channels), f32),
            pltpu.VMEM((9, groups, SUB, LANE), f32),
            pltpu.VMEM((9, groups, SUB, LANE), f32),
            pltpu.VMEM((rows, px, channels), bf16),
            pltpu.VMEM((rows, px, channels), bf16),
            pltpu.VMEM((rows, px, hidden), bf16),
            pltpu.VMEM((rows, px, hidden), bf16),
            pltpu.VMEM((parts, rows + 2, columns, SUB, LANE), f32),
            pltpu.VMEM((parts, rows + 2, columns, SUB, LANE), f32),
            pltpu.VMEM((parts, 9, SUB, LANE), f32),
            pltpu.VMEM((hidden, channels), bf16),
            pltpu.VMEM((hidden, channels), bf16),
            pltpu.VMEM((rows, px, channels), f32),
            pltpu.VMEM((2 * band, columns, SUB, channels), f32),
            pltpu.VMEM((rows, px, channels), f32),
            pltpu.VMEM((tiles, SUB, LANE), f32),
            pltpu.SemaphoreType.DMA((4,)),
        ]
        + sum_scratch(stages, (4, channels))
        + waves,
        compiler_params=pltpu.CompilerParams(
            collective_id=3, has_side_effects=True, vmem_limit_bytes=63 * MIB
        ),
    )(xa, ca, bn, meta, count, sums2, scales, shifts, hshift, w_e, w_rt, kh)


def wave_plan(sizes, channels, hidden):
    chips = sizes["imgs"]
    side = 2 if chips == 16 else 4
    one, two = ("imgs", 1, side), ("imgs", side, side)
    rest = ("imgs", side * side, chips // (side * side))
    first = ("rows", 1, sizes["rows"])
    first_order, second_order = [first, one, two, rest], [first, two, one, rest]
    short_order = [first, ("imgs", 1, chips)]
    step = 2 * sizes["rows"] * chips
    square = channels // SUB * pl.cdiv(channels, LANE)
    small = pl.cdiv(25, SUB) + pl.cdiv(49, SUB)
    half = pl.cdiv(hidden_tiles(channels, hidden)[2], 2 * step) * step
    return [
        (first_order, half),
        (second_order, half),
        (first_order, pl.cdiv(2 * square, step) * step),
        (short_order, pl.cdiv(square, step) * step),
        (short_order, pl.cdiv(small * pl.cdiv(channels, LANE), step) * step),
    ]


def back_kernel(
    reach, stages, plan, gn, bn_i, xa_i, ca_i, gl_i, sl_i, c1_i, c2_i, gp, tiles_i, nat_i,
    meta, count, sums1, sums2, sums3, scales, shifts, w_in, w_gate, w_out, kl, kd,
    mixo_o, mixq_o, resq_o, full_o, sums_o,
    cm, klb, kdb, gm, tt, sl, xa, ca, gl, c2, gb, gg, gt, g2, g1, src, gw, full,
    in_sem, move_sem, mine, *rest,
):
    found = stage_peers(stages)
    say_here(stage_peers(reach))
    rows, px, channels = xa.shape
    columns = px // SUB
    groups = groups_of(channels)
    core, chip = lax.axis_index("rows"), lax.axis_index("imgs")
    band = mixq_o.shape[0]
    parts = 3
    step = rows // parts
    pairs = [
        (gn, gm), (bn_i, gw), (xa_i, xa), (ca_i, ca), (gl_i, gl), (gp, tt), (c1_i, gg),
    ]
    loads = []
    for p in range(parts):
        at = pl.ds(p * step, step)
        loads.append([])
        for k, (a, b) in enumerate(pairs):
            loads[p].append(pltpu.make_async_copy(a.at[at], b.at[at], in_sem.at[p, k]))
            loads[p][-1].start()
    tail, waves, pair_base = list(rest[len(stages) * 3 :]), [], 0
    for k, (order, tiles) in enumerate(plan):
        (buf, *refs), tail = tail[: 1 + wave_refs(order)], tail[1 + wave_refs(order) :]
        early = EARLY if k < 2 else 0
        waves.append(Wave(order, tiles, refs, buf, 0, full, pair_base, early))
        pair_base += tiles // 2
    late = [
        pltpu.make_async_copy(c2_i, c2, in_sem.at[0, 7]),
        pltpu.make_async_copy(sl_i, sl, in_sem.at[1, 7]),
    ]
    half = early_tiles(*plan[0])
    tile_loads = [
        pltpu.make_async_copy(tiles_i.at[pl.ds(k * half, half)], waves[k].buf, in_sem.at[k, 8])
        for k in range(2)
    ]
    for copy in tile_loads + late:
        copy.start()
    make_col_mask(meta, cm)
    spread_taps(kl, klb, flip=True)
    spread_taps(kd, kdb, flip=True)
    for edge in (0, 1, rows + 2, rows + 3):
        g1[:, edge] = jnp.zeros(g1.shape[:1] + g1.shape[2:], f32)
    total = count[0:1, 0:1]
    mean1, rstd1 = statistics(sums1, total, 0)
    scale1 = rstd1 * b8(scales, 0)
    mean2, rstd2 = statistics(sums2, total, 0)
    scale2 = rstd2 * b8(scales, 2)
    back0 = b8(sums3, 0) / total
    back1 = b8(sums3, 1) / total
    zero = jnp.zeros((SUB, channels), f32)

    def to_other(v, out, first_sem):
        return remote(
            v.at[pl.ds((1 - core) * band, band)], out,
            move_sem.at[first_sem], move_sem.at[first_sem + 1], (1 - core, chip),
        )

    all_found = stage_peers(reach)
    wait_all_here(all_found)
    for copy in tile_loads:
        copy.wait()
    done, ready, clock = [EARLY, EARLY, 0, 0, 0], [0.0, 0.0, None, None, None], [0.0]

    def take(w):
        wave = waves[w]
        wave.step(done[w])
        ready[w] = clock[0] + wave.guess(done[w])
        done[w] += 1

    def stop(spent):
        clock[0] += spent
        for w, wave in enumerate(waves):
            if ready[w] is not None and done[w] < wave.steps and ready[w] <= clock[0]:
                take(w)

    stop(0.0)
    moves = [to_other(nat_i, resq_o, 0)]
    moves[0].start()

    def first(b, sums):
        sums = list(sums)
        gated_parts = []
        for k in range(step // 2):
            r = b * (step // 2) + k
            for g, width in groups:
                conv = gg[r, :, g * LANE : g * LANE + width].astype(f32)
                src[g, r, :, :, :width] = pixels3(conv)
            mask = row_mask(meta, cm, r)
            both = gw[r]
            middle = pixels3(xa[r].astype(f32)) + b8(scales, 1) * both
            hat = (middle - mean2) * rstd2
            grad = pixels3(ca[r].astype(f32)) + scale2 * (
                pixels3(gm[r]) - mask * (back0 + hat * back1)
            )
            gm[r] = pixels2(grad)
            branch = (b8(scales, 1) * grad).astype(bf16)
            gb[r] = pixels2(branch)
            sums[0] = sums[0] + fold(grad * both)
            sums[1] = sums[1] + fold(branch.astype(f32))
            gated_parts.append(pixels2(branch))
        gated_grad = dot_nt(jnp.concatenate(gated_parts, axis=0), w_out[...])
        gate_parts = []
        for k in range(step // 2):
            r = b * (step // 2) + k
            mine_grad = gated_grad[k * px : (k + 1) * px]
            gelu = gl[r].astype(f32)
            gate_grad = (mine_grad * gelu).astype(bf16)
            gg[r] = gate_grad
            gate = tt[r]
            gt[r] = (gelu * gate).astype(bf16)
            tt[r] = mine_grad * gate
            sums[2] = sums[2] + fold(pixels3(gate_grad.astype(f32)))
            gate_parts.append(gate_grad)
        conv_all = low(dot_nt(jnp.concatenate(gate_parts, axis=0), w_gate[...]))
        for k in range(step // 2):
            r = b * (step // 2) + k
            conv = conv_all[k * px : (k + 1) * px]
            for g, width in groups:
                at = slice(g * LANE, g * LANE + width)
                g2[g, r, :, :, :width] = pixels3(conv[:, at])
            sums[3] = sums[3] + fold(pixels3(conv))
        return tuple(sums)

    sums = (zero,) * 4
    for p in range(parts):
        for copy in loads[p]:
            copy.wait()
        sums = lax.fori_loop(2 * p, 2 * p + 2, first, sums)
        stop(3.0)
    for k in range(4):
        mine[2 + k : 3 + k, :] = jnp.sum(sums[k], axis=0, keepdims=True)
    whole = rows * px
    flat = lambda ref: ref[...].reshape(whole, channels)
    blocks, n = channels // SUB, len(groups)

    def square(left, right, wave, base):
        grad = dot_tn(flat(left), flat(right))
        for g, width in groups:
            part = grad[:, g * LANE : g * LANE + width].reshape(blocks, SUB, width)
            wave.buf[pl.ds(base + g, blocks, stride=n), :, :width] = part

    def clear(buf):
        def one(t, _):
            buf[t] = jnp.zeros((SUB, LANE), f32)
            return 0

        lax.fori_loop(0, buf.shape[0], one, 0)

    for wave in waves[2:]:
        clear(wave.buf)
    square(gt, gb, waves[2], 0)
    for copy in late:
        copy.wait()
    square(c2, gg, waves[2], blocks * n)
    ready[2] = 0.0
    stop(1.7)

    def put_tap(tap, g, acc, base):
        row = jnp.sum(acc, axis=0, keepdims=True)
        at = base + tap // SUB * n + g
        waves[4].buf[at, tap % SUB : tap % SUB + 1, :] = row

    near_base, far_base = 0, pl.cdiv(kl.shape[0], SUB) * n
    for g, width in groups:
        for i in range(7):
            first_row = max(0, 3 * (3 - i))
            last_row = min(rows, rows - 3 * (i - 3))

            def taps_row(r, acc, g=g, i=i):
                at = r + (i - 3) * 3
                return tap_sums(
                    list(acc), (lambda c: g2[g, r, c], columns), lambda c: src[g, at, c], 3
                )

            acc = lax.fori_loop(first_row, last_row, taps_row, zeros_list(7))
            for j in range(7):
                put_tap(7 * i + j, g, acc[j], far_base)
            stop(0.39)


    def dilated(r, sums):
        mask = row_mask(meta, cm, r)
        low_i, high_i = row_range(r, rows, 3, 3)
        out = []
        for g, width in groups:

            def tap_row(i, acc):
                taps = [kdb[7 * i + j, g] for j in range(7)]
                at = r + (i - 3) * 3
                return add_row(list(acc), lambda c: g2[g, at, c], taps, 3)

            acc = lax.fori_loop(low_i, high_i, tap_row, zeros_list(columns))
            value = low(mask[:, :, :width] * jnp.stack(acc)[:, :, :width])
            g1[g, r + 2, :, :, :width] = value
            out.append(sums[g] + fold(value))
        return tuple(out)

    start = tuple(jnp.zeros((SUB, width), f32) for g, width in groups)
    sums = start
    for p in range(parts * 2):
        sums = lax.fori_loop(p * (step // 2), (p + 1) * (step // 2), dilated, sums)
        stop(1.5)
    for g, width in groups:
        at = slice(g * LANE, g * LANE + width)
        mine[6:7, at] = jnp.sum(sums[g], axis=0, keepdims=True)

    def refill(r, _):
        for g, width in groups:
            src[g, r, :, :, :width] = pixels3(gl[r, :, g * LANE : g * LANE + width].astype(f32))
        return 0

    lax.fori_loop(0, rows, refill, 0)

    for g, width in groups:
        for i in range(5):

            def taps_row(r, acc, g=g, i=i):
                return tap_sums(
                    list(acc), (lambda c: src[g, r, c], columns), lambda c: g1[g, r + i, c], 1
                )

            acc = lax.fori_loop(0, rows, taps_row, zeros_list(5))
            for j in range(5):
                put_tap(24 - (5 * i + j), g, acc[j], near_base)
            stop(0.48)

    ready[4] = 0.0
    stop(0.0)

    def local(r, sums):
        mask = row_mask(meta, cm, r)
        out = []
        for g, width in groups:
            acc = zeros_list(columns)
            for i in range(5):
                taps = [klb[5 * i + j, g] for j in range(5)]
                acc = add_row(acc, lambda c: g1[g, r + i, c], taps, 1)
            value = mask[:, :, :width] * jnp.stack(acc)[:, :, :width]
            at = slice(g * LANE, g * LANE + width)
            grad = (tt[r, :, at] + pixels2(value)) * sl[r, :, at]
            gg[r, :, at] = grad.astype(bf16)
            out.append(sums[g] + fold(pixels3(low(grad))))
        x = pixels3(xa[r].astype(f32))
        gb[r] = pixels2((x - mean1) * scale1 + b8(shifts, 0)).astype(bf16)
        return tuple(out)

    sums = start
    for p in range(parts * 2):
        sums = lax.fori_loop(p * (step // 2), (p + 1) * (step // 2), local, sums)
        stop(1.25)
    for g, width in groups:
        at = slice(g * LANE, g * LANE + width)
        mine[7:8, at] = jnp.sum(sums[g], axis=0, keepdims=True)
    square(gb, gg, waves[3], 0)
    ready[3] = 0.0
    stop(1.0)

    def last(b, sums):
        sums = list(sums)
        tall = gg[pl.ds(b * (step // 2), step // 2)].reshape(step // 2 * px, channels)
        product = dot_nt(tall, w_in[...])
        for k in range(step // 2):
            r = b * (step // 2) + k
            x = pixels3(xa[r].astype(f32))
            grad = pixels3(gm[r])
            gn1 = pixels3(product[k * px : (k + 1) * px]) + b8(scales, 1) * grad
            gm[r] = pixels2(grad + scale1 * gn1)
            hat = (x - mean1) * rstd1
            sums[0] = sums[0] + fold(gn1)
            sums[1] = sums[1] + fold(gn1 * hat)
        return tuple(sums)

    sums = (zero, zero)
    for p in range(parts * 2):
        sums = lax.fori_loop(p, p + 1, last, sums)
        stop(0.8)
    for k in range(2):
        mine[k : k + 1, :] = jnp.sum(sums[k], axis=0, keepdims=True)
    total_sum = AllSum(stages, mine, rest)
    total_sum.start(0)
    total_sum.end(0)
    stop(1.3)
    for k in range(1, len(stages)):
        total_sum.start(k)
        if k == 1:
            unalign(gm, meta, gw)
            moves.append(to_other(gw, mixq_o, 2))
            own_rows = gw.at[pl.ds(core * band, band)]
            moves.append(pltpu.make_async_copy(own_rows, mixo_o, move_sem.at[4]))
            for copy in moves[1:]:
                copy.start()
        total_sum.end(k)
        stop(3.0)
    sums_o[...] = mine[...]
    pair_base = 0
    for w, (_, tiles) in enumerate(plan):
        while done[w] < waves[w].steps:
            take(w)
        at = pl.ds(pair_base, tiles // 2)
        moves.append(pltpu.make_async_copy(full.at[at], full_o.at[at], move_sem.at[5 + w]))
        moves[-1].start()
        pair_base += tiles // 2
    for copy in moves:
        copy.wait()


def mixer_back(reach, stages, plan, band, gn, bn, xa, ca, gl, sl, c1, c2, gp, tiles, nat, meta, count,
               sums1, sums2, sums3, scales, shifts, w_in, w_gate, w_out, kl, kd):
    rows, px, channels = xa.shape
    columns = px // SUB
    n = len(groups_of(channels))
    small = (rows, px, channels)
    shape = jax.ShapeDtypeStruct
    pairs = sum(tiles // 2 for _, tiles in plan)
    waves = []
    for k, (order, count_tiles) in enumerate(plan):
        early = early_tiles(order, count_tiles) if k < 2 else count_tiles
        waves.append(pltpu.VMEM((early, SUB, LANE), f32))
        waves += wave_scratch(order, count_tiles, EARLY if k < 2 else 0)
    half = shape((band, columns, SUB, channels), f32)
    return pl.pallas_call(
        functools.partial(back_kernel, reach, stages, plan),
        name="mixer_back",
        out_shape=[
            half,
            half,
            half,
            shape((pairs, 2 * SUB, LANE), bf16),
            shape((8, channels), f32),
        ],
        in_specs=[ANY] * 11 + [VMEM] * 12,
        out_specs=[ANY] * 4 + [VMEM],
        scratch_shapes=[
            pltpu.VMEM((columns, SUB, channels), f32),
            pltpu.VMEM((25, n, SUB, LANE), f32),
            pltpu.VMEM((49, n, SUB, LANE), f32),
        ]
        + [pltpu.VMEM(small, k) for k in (f32,) * 3 + (bf16,) * 7]
        + [
            pltpu.VMEM((n, rows, columns, SUB, LANE), f32),
            pltpu.VMEM((n, rows + 4, columns, SUB, LANE), f32),
            pltpu.VMEM((n, rows, columns, SUB, LANE), f32),
            pltpu.VMEM((2 * band, columns, SUB, channels), f32),
            pltpu.VMEM((pairs, 2 * SUB, LANE), bf16),
            pltpu.SemaphoreType.DMA((3, 9)),
            pltpu.SemaphoreType.DMA((5 + len(plan),)),
        ]
        + sum_scratch(stages, (8, channels))
        + waves,
        compiler_params=pltpu.CompilerParams(
            collective_id=4, has_side_effects=True, vmem_limit_bytes=63 * MIB
        ),
    )(gn, bn.reshape(rows, columns, SUB, channels), xa, ca, gl, sl, c1, c2, gp, tiles, nat, meta,
      count, sums1, sums2, sums3, scales,
      shifts, w_in, w_gate, w_out, kl, kd)


def unalign(al, meta, out):
    rows, px, channels = al.shape
    offsets = out.shape[0] - rows + 1
    for at in range(out.shape[0]):
        value = jnp.zeros((px // SUB, SUB, channels), f32)
        for t in range(offsets):
            if 0 <= at - t < rows:
                chosen = (meta[0] == float(t))[None]
                value = jnp.where(chosen, pixels3(al[at - t]), value)
        out[at] = value


def tiles_out(full, base, ref):
    rows, width = ref.shape
    groups = groups_of(width)
    n, blocks = len(groups), rows // SUB
    period = 1 if n % 2 == 0 else 2

    def block(b, _):
        for k in range(period):
            for g, wide in groups:
                tile = k * n + g
                pair = base // 2 + b * (period * n // 2) + tile // 2
                value = full[pair].astype(f32)[tile % 2 * SUB : (tile % 2 + 1) * SUB]
                at = pl.ds(pl.multiple_of((b * period + k) * SUB, SUB), SUB)
                ref[at, g * LANE : g * LANE + wide] = value[:, :wide]
        return 0

    lax.fori_loop(0, blocks // period, block, 0)
    for b in range(blocks // period * period, pl.cdiv(rows, SUB)):
        count = min(SUB, rows - b * SUB)
        for g, wide in groups:
            tile = base + b * n + g
            value = full[tile // 2].astype(f32)[tile % 2 * SUB : tile % 2 * SUB + count]
            ref[b * SUB : b * SUB + count, g * LANE : g * LANE + wide] = value[:, :wide]


def finish_kernel(
    bases, x_i, mixo, mixq, nat, resq, meta, count, sums1, sums3, sums4, scales, full,
    in_o, res_o, sg_o, bg_o, *rest,
):
    for ref, order in (
        (sg_o, ((sums4, 1), (sums4, 2), (sums3, 1), (sums3, 3))),
        (bg_o, tuple((sums4, k) for k in (0, 7, 6, 5, 4, 3)) + ((sums3, 0), (sums3, 2))),
    ):
        for k, (table, row) in enumerate(order):
            ref[k : k + 1, :] = table[row : row + 1, :]
    n = len(bases)
    grads, (x, mix, res, cm), grad_s = rest[:n], rest[n : n + 4], rest[n + 4 : -3]
    in_sem, out_sem, grad_sem = rest[-3:]
    band, columns = x.shape[:2]
    core = lax.axis_index("rows")
    mine = pl.ds(pl.multiple_of(core * SUB, SUB), SUB)
    other = pl.ds(pl.multiple_of((1 - core) * SUB, SUB), SUB)

    def loads(r):
        pairs = [
            (x_i.at[r], x.at[r]),
            (mixo.at[r], mix.at[r, :, mine]),
            (mixq.at[r], mix.at[r, :, other]),
            (nat.at[core * band + r], res.at[r, :, mine]),
            (resq.at[r], res.at[r, :, other]),
        ]
        return [pltpu.make_async_copy(a, b, in_sem.at[r, k]) for k, (a, b) in enumerate(pairs)]

    def stores(r):
        pairs = [(mix.at[r], in_o.at[r]), (res.at[r], res_o.at[r])]
        return [pltpu.make_async_copy(a, b, out_sem.at[r, k]) for k, (a, b) in enumerate(pairs)]

    def begin(r, _):
        for copy in loads(r):
            copy.start()
        return 0

    lax.fori_loop(0, band, begin, 0)
    size, top = meta[1], meta[0]
    for c in range(columns):
        cm[c] = (size > c).astype(f32)
    copies = []
    for k, (ref, base) in enumerate(zip(grad_s, bases)):
        tiles_out(full, base, ref)
        copies.append(pltpu.make_async_copy(ref, grads[k], grad_sem.at[k]))
        copies[-1].start()
    total = count[0:1, 0:1]
    mean = sums1[0:1, :] / total
    rstd = lax.rsqrt(sums1[1:2, :] / total - mean * mean + epsilon)
    scale = rstd * scales[0:1, :]
    back0, back1 = sums4[0:1, :] / total, sums4[1:2, :] / total
    spread = lambda v: jnp.broadcast_to(v, size.shape)
    mean, rstd, scale, back0, back1 = (spread(v) for v in (mean, rstd, scale, back0, back1))

    def row(r, _):
        for copy in loads(r):
            copy.wait()
        at = (r * 1).astype(f32)
        inside = ((at >= top) & (at < top + size)).astype(f32)
        mask = cm[...] * inside[None]
        hat = (mask * x[r].astype(f32) - mean) * rstd
        mix[r] = mask * (mix[r] - scale * (back0 + hat * back1))
        for copy in stores(r):
            copy.start()
        return 0

    lax.fori_loop(0, band, row, 0)

    def end(r, _):
        for copy in stores(r):
            copy.wait()
        return 0

    lax.fori_loop(0, band, end, 0)
    for copy in copies:
        copy.wait()


def finish(
    x, mixo, mixq, nat, resq, meta, count, sums1, sums3, sums4, scales, full, shapes, bases
):
    band, columns, images, channels = x.shape
    shape = jax.ShapeDtypeStruct
    return pl.pallas_call(
        functools.partial(finish_kernel, bases),
        name="finish",
        in_specs=[ANY] * 5 + [VMEM] * 7,
        out_specs=[ANY] * 2 + [VMEM] * 2 + [ANY] * len(shapes),
        scratch_shapes=[
            pltpu.VMEM(x.shape, bf16),
            pltpu.VMEM(x.shape, f32),
            pltpu.VMEM(x.shape, f32),
            pltpu.VMEM((columns, images, channels), f32),
        ]
        + [pltpu.VMEM(s, f32) for s in shapes]
        + [
            pltpu.SemaphoreType.DMA((band, 5)),
            pltpu.SemaphoreType.DMA((band, 2)),
            pltpu.SemaphoreType.DMA((len(shapes),)),
        ],
        out_shape=[shape(x.shape, f32)] * 2
        + [shape((k, channels), f32) for k in (4, 8)]
        + [shape(s, f32) for s in shapes],
        compiler_params=pltpu.CompilerParams(vmem_limit_bytes=62 * MIB),
    )(x, mixo, mixq, nat, resq, meta, count, sums1, sums3, sums4, scales, full)


def on_device(sizes, inputs, cotangent, scales, shifts, hidden_shift, w_inward, w_gating,
              w_outward, w_expand, w_reduce, kernel_local, kernel_dilated, kernel_hidden,
              image_size, band_split, slot_image):
    images, band, columns, channels = inputs.shape
    x = jnp.transpose(inputs, (1, 2, 0, 3))
    y = jnp.transpose(cotangent, (1, 2, 0, 3))
    stages = stage_list(sizes)
    xa, ca, gl, sl, c1, c2, gp, bn, sums1, sums2, own_meta, meta, count = mixer_forward(
        stages, x, y, image_size[None], band_split[None], slot_image[None], scales, shifts,
        w_inward, w_gating, w_outward, kernel_local, kernel_dilated,
    )
    hidden = w_expand.shape[1]
    plan = wave_plan(sizes, channels, hidden)
    half_tiles = plan[0][1]
    nat, gn, tiles, sums3 = hidden_block(
        stages, plan, band, xa, ca, bn, meta, count, sums2, scales, shifts,
        hidden_shift, w_expand, w_reduce.T, kernel_hidden,
    )
    mixo, mixq, resq, full, sums4 = mixer_back(
        reach_list(sizes), stages, plan, band, gn, bn, xa, ca, gl, sl, c1, c2, gp, tiles, nat, meta, count,
        sums1, sums2, sums3, scales, shifts, w_inward, w_gating, w_outward, kernel_local,
        kernel_dilated,
    )
    square, wide = (channels, channels), (channels, hidden)
    blocks, n = channels // SUB, len(groups_of(channels))
    tap_tile, bias_tile, _ = hidden_tiles(channels, hidden)
    second = 2 * half_tiles
    third = second + plan[2][1]
    near = third + plan[3][1]
    far = near + pl.cdiv(kernel_local.shape[0], SUB) * n
    targets = [
        (wide, 0),
        (wide, tap_tile // 2),
        (kernel_hidden.shape, tap_tile),
        (hidden_shift.shape, bias_tile),
        (square, second),
        (square, second + blocks * n),
        (square, third),
        (kernel_local.shape, near),
        (kernel_dilated.shape, far),
    ]
    (input_grad, result, scales_grad, shifts_grad, gwe, gwr, gk, gh, gwo, gwg, gwi, gkl,
     gkd) = finish(
        x, mixo, mixq, nat, resq, own_meta, count, sums1, sums3, sums4, scales, full,
        [t[0] for t in targets], [t[1] for t in targets],
    )
    back = lambda v: jnp.transpose(v, (2, 0, 1, 3))
    return (
        back(result), back(input_grad), scales_grad, shifts_grad, gh, gwi, gwg, gwo, gwe, gwr.T,
        gkl, gkd, gk,
    )


def solution(mesh):
    wide = P("imgs", "rows", None, None)
    sizes = dict(mesh.shape)
    return jax.shard_map(
        functools.partial(on_device, sizes),
        mesh=mesh,
        in_specs=(wide, wide) + (P(),) * 13 + (P("imgs"),),
        out_specs=(wide, wide) + (P(),) * 11,
        check_vma=False,
    )
```
